32 devices in a mesh: grp: 2 (over y), ex: 8 (over z, x), dim: 2 (over core).
Axes of the slice: x: 2, y: 2, z: 4, core: 2. Of those that a mesh axis runs over, the one named last changes fastest.
Arguments:
- queries: bfloat16 [96, 16384], P(None, 'ex'), may hold values from -6 to 6
- inverse_fisher: bfloat16 [16384, 16384], P('ex', 'dim'), as said below
- stored_grads: bfloat16 [2048, 16384], P(('grp', 'ex'), 'dim'), parts along dimension 0, may hold values from -0.046875 to 0.046875
Outputs:
- scores: float32 [96, 2048], P('dim', ('grp', 'ex')), parts along dimension 1
The draws below stay inside these ranges and needn't reach their ends.
There are 2 independent parts, one for each index of `grp`. The reference program is written for one: setup_inputs(seed, part) draws one part's arguments, and reference() takes and returns one part's arrays. A program takes and returns all parts, laid end to end along the dimension named above; an argument that names none is the same for every part. Nothing has to cross between parts.
Inputs may be any that keep to these rules, and one draw needn't show every extreme that they name: inverse_fisher is symmetric up to rounding.
All inputs are finite; a program needn't handle non-finite values.
Results may differ from the reference program's by a relative error of at most 0.0029.
Values may be sent and summed in bfloat16 or wider, within the bound.
No kernel may reach another device: no remote copies, remote signals or barrier semaphores. Data moves between devices by JAX's collectives and lax.ppermute only.
A program may use at most 128 MiB of HBM per device.

```python
import math
import jax
import jax.numpy as jnp
from jax import lax

K = 16384
NQ = 96
NEX = 1024


def draw_inverse_fisher(key, part):
    key = jax.random.fold_in(key, 7)
    first, second = jax.random.split(key, 2)
    noise = jax.random.normal(first, (K, K), jnp.float32)
    matrix = (noise + noise.T) * (0.3 / math.sqrt(2.0 * K))
    diag_values = jnp.exp(jax.random.uniform(second, (K,), jnp.float32, 0.0, math.log(3.0)))
    matrix = matrix + jnp.eye(K, dtype=jnp.float32) * diag_values[:, None]
    return matrix.astype(jnp.bfloat16)


def block_scale(rng, dims, pieces, least, high):
    loudness = 1.0
    for dim, parts in pieces:
        draws = jax.random.uniform(jax.random.fold_in(jax.random.fold_in(rng, 6), dim), (parts,), jnp.float32, least / len(pieces), high / len(pieces))
        loudness = loudness * jnp.repeat(jnp.exp(draws), dims[dim] // parts).reshape((-1,) + (1,) * (len(dims) - 1 - dim))
    return loudness


def bell_draw(rng, shape, width, most, shards=(), kind=jnp.bfloat16):
    level = block_scale(rng, shape, shards, -0.22, 0.18) if shards else 1.0
    array = jax.random.normal(rng, shape, jnp.float32) * width * level
    return jnp.minimum(jnp.maximum(array, -most), most).astype(kind)


def setup_inputs(seed: int = 0, part: int = 0) -> dict:
    keys = jax.random.split(jax.random.key(seed), 4)
    own_keys = jax.random.split(jax.random.fold_in(keys[3], part), 4)
    queries = bell_draw(keys[0], (NQ, K), 1.0, 6.0, ((1, 8),))
    inverse_fisher = draw_inverse_fisher(jax.random.fold_in(keys[3], 71), part)
    stored_grads = bell_draw(own_keys[2], (NEX, K), K ** -0.5, 0.046875, ((0, 8), (1, 2)))
    return {"queries": queries, "inverse_fisher": inverse_fisher, "stored_grads": stored_grads}


def reference(queries, inverse_fisher, stored_grads):
    preconditioned = jnp.dot(queries, inverse_fisher, preferred_element_type=jnp.float32).astype(jnp.bfloat16)
    scores = lax.dot_general(preconditioned, stored_grads, (((1,), (1,)), ((), ())), preferred_element_type=jnp.float32)
    return scores
```

```python
import functools

import jax
import jax.numpy as jnp
from jax import lax
from jax.experimental import pallas as pl
from jax.experimental.pallas import tpu as pltpu
from jax.sharding import PartitionSpec as P

AXES = ("grp", "ex", "dim")
NT = (((1,), (1,)), ((), ()))


def per_device_any(queries, inverse_fisher, stored_grads):
    term_block = jnp.dot(queries, inverse_fisher, preferred_element_type=jnp.float32)
    own_panel = lax.psum_scatter(term_block, "ex", scatter_dimension=1, tiled=True).astype(
        jnp.bfloat16
    )
    partial_scores = lax.dot_general(
        lax.all_gather(own_panel, "ex", axis=1, tiled=True),
        stored_grads,
        NT,
        preferred_element_type=jnp.float32,
    )
    return lax.psum_scatter(partial_scores, "dim", scatter_dimension=0, tiled=True)


def fisher_kernel(n, has_base, cols_ref, *refs):
    del cols_ref
    out_ref = refs[-1]
    acc = refs[2 * n][...] if has_base else None
    for i in range(n):
        term = lax.dot_general(refs[i][...], refs[n + i][...], NT, preferred_element_type=jnp.float32)
        acc = term if acc is None else acc + term
    out_ref[...] = acc


def fisher_dot(chunks, cols, fisher, base=None, rows=512):
    n = len(chunks)
    nq, width = chunks[0].shape
    total = fisher.shape[0]
    in_specs = [pl.BlockSpec((nq, width), lambda i, c: (0, 0)) for _ in range(n)]
    in_specs += [
        pl.BlockSpec((rows, width), functools.partial(lambda k, i, c: (i, c[k]), k)) for k in range(n)
    ]
    operands = list(chunks) + [fisher] * n
    if base is not None:
        in_specs.append(pl.BlockSpec((nq, rows), lambda i, c: (0, i)))
        operands.append(base)
    return pl.pallas_call(
        functools.partial(fisher_kernel, n, base is not None),
        out_shape=jax.ShapeDtypeStruct((nq, total), jnp.float32),
        grid_spec=pltpu.PrefetchScalarGridSpec(
            num_scalar_prefetch=1,
            grid=(total // rows,),
            in_specs=in_specs,
            out_specs=pl.BlockSpec((nq, rows), lambda i, c: (0, i)),
        ),
        compiler_params=pltpu.CompilerParams(vmem_limit_bytes=32 * 1024 * 1024),
        cost_estimate=pl.CostEstimate(
            flops=2 * n * nq * width * total,
            bytes_accessed=n * width * total * 2,
            transcendentals=0,
        ),
    )(jnp.stack(cols).astype(jnp.int32), *operands)


def per_device_quad(nz, nx, ny, queries, inverse_fisher, stored_grads):
    nex = nz * nx
    near = nz // 2
    nq, block = queries.shape
    half = block // ny
    y, e, d = (lax.axis_index(a) for a in AXES)
    z = e // nx
    x = e % nx
    u = jnp.where(d == 0, z, nz - 1 - z)
    owner = u < near

    def move(value, target):
        pairs = []
        for sy in range(ny):
            for sz in range(nz):
                for sx in range(nx):
                    for sd in range(2):
                        to = target(sy, sz, sx, sd)
                        if to is not None:
                            ty, tz, tx, td = to
                            pairs.append(((sy * nex + sz * nx + sx) * 2 + sd, (ty * nex + tz * nx + tx) * 2 + td))
        return lax.ppermute(value, AXES, pairs)

    def along_z(value, hops):
        def target(sy, sz, sx, sd):
            su = sz if sd == 0 else nz - 1 - sz
            if su not in hops:
                return None
            tu = hops[su]
            return sy, tu if sd == 0 else nz - 1 - tu, sx, sd

        return move(value, target)

    def gather_z(own):
        swap = along_z(own, {0: 1, 1: 0})
        same = along_z(own, {0: 2, 1: 3})
        other = along_z(own, {0: 3, 1: 2})
        return jnp.where(owner, own, same), jnp.where(owner, swap, other)

    def real_plane(k):
        return jnp.where(d == 0, k, nz - 1 - k)

    planes = [real_plane(u % 2), real_plane(1 - u % 2)]
    first = d * (nex // 2)

    def column(plane, x_):
        return (plane * nx + x_ - first) * ny

    def slab(x_, y_):
        return jnp.concatenate(
            [
                lax.dynamic_slice_in_dim(stored_grads, (column(p, x_) + y_) * half, half, axis=1)
                for p in planes
            ],
            axis=1,
        )

    grads = [slab(x, y)]
    grads.append(move(slab(x, 1 - y), lambda sy, sz, sx, sd: (1 - sy, sz, sx, sd)))

    own = lax.dynamic_slice_in_dim(queries, y * half, half, axis=1)
    near_q = gather_z(own)
    far_q = [move(q, lambda sy, sz, sx, sd: (sy, sz, 1 - sx, sd)) for q in near_q]
    partial = fisher_dot(near_q, [column(p, x) + y for p in planes], inverse_fisher)
    partial = fisher_dot(far_q, [column(p, 1 - x) + y for p in planes], inverse_fisher, partial)

    grads.append(move(slab(1 - x, y), lambda sy, sz, sx, sd: (sy, sz, 1 - sx, sd)))
    grads.append(move(slab(1 - x, 1 - y), lambda sy, sz, sx, sd: (1 - sy, sz, 1 - sx, sd)))

    def to_owner(sy, sz, sx, sd):
        su = sz if sd == 0 else nz - 1 - sz
        return None if su < near else (sy, sz, sx, 1 - sd)

    def across_y(sy, sz, sx, sd):
        su = sz if sd == 0 else nz - 1 - sz
        return (1 - sy, sz, sx, sd) if su < near else None

    partial = partial + move(partial, to_owner)
    theirs = lax.dynamic_slice_in_dim(partial, (1 - y) * half, half, axis=1)
    ours = lax.dynamic_slice_in_dim(partial, y * half, half, axis=1)
    panel = (ours + move(theirs, across_y)).astype(jnp.bfloat16)

    panels = gather_z(panel)
    panels = jnp.concatenate(panels, axis=1)
    scores = [lax.dot_general(panels, g, NT, preferred_element_type=jnp.float32) for g in grads]

    rows = nq // 2
    stacked = jnp.stack(scores)
    keep = lax.dynamic_slice_in_dim(stacked, d * rows, rows, axis=1)
    give = lax.dynamic_slice_in_dim(stacked, (1 - d) * rows, rows, axis=1)
    mine = keep + move(give, lambda sy, sz, sx, sd: (sy, sz, sx, 1 - sd))
    return (
        mine[0]
        + move(mine[1], lambda sy, sz, sx, sd: (1 - sy, sz, sx, sd))
        + move(mine[2], lambda sy, sz, sx, sd: (sy, sz, 1 - sx, sd))
        + move(mine[3], lambda sy, sz, sx, sd: (1 - sy, sz, 1 - sx, sd))
    )


def solution(mesh):
    coords = [getattr(device, "coords", None) for device in mesh.devices.flat]
    nx = 2 if None in coords else len({c[0] for c in coords})
    nz = mesh.shape["ex"] // nx
    ny = mesh.shape["grp"]
    if (nz, nx, ny) == (4, 2, 2):
        body = functools.partial(per_device_quad, nz, nx, ny)
    else:
        body = per_device_any
    return jax.shard_map(
        body,
        mesh=mesh,
        in_specs=(P(None, "ex"), P("ex", "dim"), P(("grp", "ex"), "dim")),
        out_specs=P("dim", ("grp", "ex")),
        check_vma=False,
    )
```

```python
import functools

import jax
import jax.numpy as jnp
from jax import lax
from jax.experimental import pallas as pl
from jax.experimental.pallas import tpu as pltpu
from jax.sharding import PartitionSpec as P

AXES = ("grp", "ex", "dim")
NT = (((1,), (1,)), ((), ()))
VMEM = pl.BlockSpec(memory_space=pltpu.VMEM)


def per_device_any(queries, inverse_fisher, stored_grads):
    term_block = jnp.dot(queries, inverse_fisher, preferred_element_type=jnp.float32)
    own_panel = lax.psum_scatter(term_block, "ex", scatter_dimension=1, tiled=True).astype(
        jnp.bfloat16
    )
    partial_scores = lax.dot_general(
        lax.all_gather(own_panel, "ex", axis=1, tiled=True),
        stored_grads,
        NT,
        preferred_element_type=jnp.float32,
    )
    return lax.psum_scatter(partial_scores, "dim", scatter_dimension=0, tiled=True)


def fisher_kernel(n, has_base, index_ref, *refs):
    del index_ref
    out_ref = refs[-1]
    acc = None
    for i in range(n):
        term = lax.dot_general(refs[n + i][...], refs[i][...], NT, preferred_element_type=jnp.float32)
        acc = term if acc is None else acc + term
    acc = acc.T
    if has_base:
        acc = acc + refs[2 * n][0]
    out_ref[...] = acc.reshape(out_ref.shape)


def cut_kernel(at, at_ref, src_ref, *refs):
    outs, sem = refs[:-1], refs[-1]
    copies = []
    for out_ref, pieces in zip(outs, at):
        width = out_ref.shape[1] // len(pieces)
        for p, i in enumerate(pieces):
            start = pl.multiple_of(at_ref[i] * width, width)
            copies.append(
                pltpu.make_async_copy(
                    src_ref.at[:, pl.ds(start, width)],
                    out_ref.at[:, p * width : (p + 1) * width],
                    sem.at[len(copies)],
                )
            )
            copies[-1].start()
    for copy in copies:
        copy.wait()


def cut(src, width, starts):
    flat = [s for pieces in starts for s in pieces]
    at, i = [], 0
    for pieces in starts:
        at.append(list(range(i, i + len(pieces))))
        i += len(pieces)
    return pl.pallas_call(
        functools.partial(cut_kernel, at),
        out_shape=[jax.ShapeDtypeStruct((src.shape[0], width * len(p)), src.dtype) for p in starts],
        in_specs=[pl.BlockSpec(memory_space=pltpu.SMEM), pl.BlockSpec(memory_space=pltpu.HBM)],
        out_specs=[VMEM] * len(starts),
        scratch_shapes=[pltpu.SemaphoreType.DMA((len(flat),))],
        cost_estimate=pl.CostEstimate(
            flops=0, bytes_accessed=4 * src.shape[0] * width * len(flat), transcendentals=0
        ),
    )(jnp.stack(flat).astype(jnp.int32), src)


def panel_kernel(ours_ref, core_ref, y_ref, after_ref, out_ref):
    del after_ref
    out_ref[...] = ((ours_ref[...] + core_ref[...]) + y_ref[...]).astype(out_ref.dtype)


def panel_sum(ours, from_core, from_y, after):
    return pl.pallas_call(
        panel_kernel,
        out_shape=jax.ShapeDtypeStruct(ours.shape, jnp.bfloat16),
        in_specs=[VMEM] * 3 + [pl.BlockSpec(memory_space=pl.ANY)],
        out_specs=VMEM,
    )(ours, from_core, from_y, after)


def fisher_dot(chunks, cols, row_halves, fisher, base=None, base_at=0, after=(), rows=256):
    n, parts = len(chunks), len(row_halves)
    nq, width = chunks[0].shape
    half = fisher.shape[0] // 2
    steps = half // rows
    in_specs = [pl.BlockSpec((nq, width), lambda h, i, s: (0, 0)) for _ in range(n)]
    in_specs += [
        pl.BlockSpec(
            (rows, width), functools.partial(lambda k, h, i, s: (s[n + h] * steps + i, s[k]), k)
        )
        for k in range(n)
    ]
    operands = list(chunks) + [fisher] * n
    if base is not None:
        in_specs.append(pl.BlockSpec((1, nq, rows), lambda h, i, s: (base_at + h, 0, i)))
        operands.append(base)
    in_specs += [pl.BlockSpec(memory_space=pl.ANY)] * len(after)
    operands += after
    if parts == 1:
        out_shape = jax.ShapeDtypeStruct((nq, half), jnp.float32)
        out_spec = pl.BlockSpec((nq, rows), lambda h, i, s: (0, i))
    else:
        out_shape = jax.ShapeDtypeStruct((parts, nq, half), jnp.float32)
        out_spec = pl.BlockSpec((1, nq, rows), lambda h, i, s: (h, 0, i))
    return pl.pallas_call(
        functools.partial(fisher_kernel, n, base is not None),
        out_shape=out_shape,
        grid_spec=pltpu.PrefetchScalarGridSpec(
            num_scalar_prefetch=1,
            grid=(parts, steps),
            in_specs=in_specs,
            out_specs=out_spec,
        ),
        compiler_params=pltpu.CompilerParams(vmem_limit_bytes=24 * 1024 * 1024),
        cost_estimate=pl.CostEstimate(
            flops=2 * n * nq * width * half * parts,
            bytes_accessed=n * width * half * parts * 2,
            transcendentals=0,
        ),
    )(jnp.stack(list(cols) + list(row_halves)).astype(jnp.int32), *operands)


def score_kernel(n, at, panel_ref, *refs):
    out_ref = refs[n]
    width = panel_ref.shape[1]
    panel = panel_ref[...]
    for k in range(n):
        piece = refs[k][:, at * width : (at + 1) * width]
        term = lax.dot_general(piece, panel, NT, preferred_element_type=jnp.float32)
        out_ref[k] = term.T


def score_end_kernel(n, at, d_ref, panel_ref, *refs):
    base_ref, keep_ref, give_ref, total_ref = refs[n : n + 4]
    width = panel_ref.shape[1]
    rows = keep_ref.shape[1]
    panel = panel_ref[...]
    for k in range(n):
        piece = refs[k][:, at * width : (at + 1) * width]
        term = lax.dot_general(piece, panel, NT, preferred_element_type=jnp.float32)
        total_ref[k] = base_ref[k] + term.T
    d = d_ref[0]
    keep_ref[...] = total_ref[:, pl.ds(pl.multiple_of(d * rows, 8), rows), :]
    give_ref[...] = total_ref[:, pl.ds(pl.multiple_of((1 - d) * rows, 8), rows), :]


def score_dot(panel, slabs):
    n = len(slabs)
    return pl.pallas_call(
        functools.partial(score_kernel, n, 0),
        out_shape=jax.ShapeDtypeStruct((n, panel.shape[0], slabs[0].shape[0]), jnp.float32),
        in_specs=[VMEM] * (n + 1),
        out_specs=VMEM,
        compiler_params=pltpu.CompilerParams(vmem_limit_bytes=24 * 1024 * 1024),
    )(panel, *slabs)


def score_dot_end(panel, slabs, base, d):
    n = len(slabs)
    nq, ne = panel.shape[0], slabs[0].shape[0]
    half = jax.ShapeDtypeStruct((n, nq // 2, ne), jnp.float32)
    return pl.pallas_call(
        functools.partial(score_end_kernel, n, 1),
        out_shape=(half, half),
        in_specs=[pl.BlockSpec(memory_space=pltpu.SMEM)] + [VMEM] * (n + 2),
        out_specs=(VMEM, VMEM),
        scratch_shapes=[pltpu.VMEM((n, nq, ne), jnp.float32)],
        compiler_params=pltpu.CompilerParams(vmem_limit_bytes=24 * 1024 * 1024),
    )(d.reshape(1).astype(jnp.int32), panel, *slabs, base)


def per_device_quad(nz, nx, ny, queries, inverse_fisher, stored_grads):
    nex = nz * nx
    near = nz // 2
    nq, block = queries.shape
    half = block // ny
    y, e, d = (lax.axis_index(a) for a in AXES)
    z = e // nx
    x = e % nx
    u = jnp.where(d == 0, z, nz - 1 - z)
    owner = u < near

    def move(value, target):
        pairs = []
        for sy in range(ny):
            for sz in range(nz):
                for sx in range(nx):
                    for sd in range(2):
                        to = target(sy, sz, sx, sd)
                        if to is not None:
                            ty, tz, tx, td = to
                            pairs.append(((sy * nex + sz * nx + sx) * 2 + sd, (ty * nex + tz * nx + tx) * 2 + td))
        return lax.ppermute(value, AXES, pairs)

    def along_z(value, hops):
        def target(sy, sz, sx, sd):
            su = sz if sd == 0 else nz - 1 - sz
            if su not in hops:
                return None
            tu = hops[su]
            return sy, tu if sd == 0 else nz - 1 - tu, sx, sd

        return move(value, target)

    def swap_x(value):
        return move(value, lambda sy, sz, sx, sd: (sy, sz, 1 - sx, sd))

    def swap_y(value):
        return move(value, lambda sy, sz, sx, sd: (1 - sy, sz, sx, sd))

    def swap_core(value):
        return move(value, lambda sy, sz, sx, sd: (sy, sz, sx, 1 - sd))

    def gather_z(own):
        first = jnp.where(owner, own, along_z(own, {0: 2, 1: 3}))
        return first, along_z(first, {0: 1, 1: 0, 2: 3, 3: 2})

    def real_plane(k):
        return jnp.where(d == 0, k, nz - 1 - k)

    planes = [real_plane(u % 2), real_plane(1 - u % 2)]

    def column(plane, x_, y_):
        return (plane * nx + x_ - d * (nex // 2)) * ny + y_

    def slab(x_, y_):
        return [column(p, x_, y_) for p in planes]

    (own,) = cut(queries, half, [[y]])
    own_slab, to_x, to_y, to_xy = cut(
        stored_grads, half, [slab(x, y), slab(1 - x, y), slab(x, 1 - y), slab(1 - x, 1 - y)]
    )
    pass_on = swap_y(to_xy)
    from_y = swap_y(to_y)
    from_x = swap_x(to_x)
    from_xy = swap_x(pass_on)
    slabs = [own_slab, from_x, from_y, from_xy]

    q0, q1 = gather_z(own)
    q2, q3 = swap_x(q0), swap_x(q1)
    halves = [1 - y, y]
    base = fisher_dot(
        [q0, q1, q2],
        [column(planes[0], x, y), column(planes[1], x, y), column(planes[0], 1 - x, y)],
        halves,
        inverse_fisher,
        after=[pass_on],
    )
    last = [column(planes[1], 1 - x, y)]
    theirs = fisher_dot([q3], last, halves[:1], inverse_fisher, base, 0)
    ours = fisher_dot([q3], last, halves[1:], inverse_fisher, base, 1, [from_y])

    def to_owner(sy, sz, sx, sd):
        su = sz if sd == 0 else nz - 1 - sz
        return None if su < near else (sy, sz, sx, 1 - sd)

    def across_y(sy, sz, sx, sd):
        su = sz if sd == 0 else nz - 1 - sz
        return (1 - sy, sz, sx, sd) if su < near else None

    theirs = move(theirs + move(theirs, to_owner), across_y)
    panel = panel_sum(ours, move(ours, to_owner), theirs, from_x)

    p0, p1 = gather_z(panel)
    keep, give = score_dot_end(p1, slabs, score_dot(p0, slabs), d)

    mine = keep + swap_core(give)
    mine = mine[:2] + swap_y(mine[2:])
    return mine[0] + swap_x(mine[1])


def solution(mesh):
    coords = [getattr(device, "coords", None) for device in mesh.devices.flat]
    nx = 2 if None in coords else len({c[0] for c in coords})
    nz = mesh.shape["ex"] // nx
    ny = mesh.shape["grp"]
    if (nz, nx, ny) == (4, 2, 2):
        body = functools.partial(per_device_quad, nz, nx, ny)
    else:
        body = per_device_any
    return jax.shard_map(
        body,
        mesh=mesh,
        in_specs=(P(None, "ex"), P("ex", "dim"), P(("grp", "ex"), "dim")),
        out_specs=P("dim", ("grp", "ex")),
        check_vma=False,
    )
```

```python
import functools

import jax
import jax.numpy as jnp
from jax import lax
from jax.experimental import pallas as pl
from jax.experimental.pallas import tpu as pltpu
from jax.sharding import PartitionSpec as P

AXES = ("grp", "ex", "dim")
NT = (((1,), (1,)), ((), ()))
VMEM = pl.BlockSpec(memory_space=pltpu.VMEM)
SMEM = pl.BlockSpec(memory_space=pltpu.SMEM)
HBM = pl.BlockSpec(memory_space=pltpu.HBM)
ANY = pl.BlockSpec(memory_space=pl.ANY)


def limit(mib):
    return pltpu.CompilerParams(vmem_limit_bytes=mib * 1024 * 1024)


def per_device_any(queries, inverse_fisher, stored_grads):
    term_block = jnp.dot(queries, inverse_fisher, preferred_element_type=jnp.float32)
    own_panel = lax.psum_scatter(term_block, "ex", scatter_dimension=1, tiled=True).astype(
        jnp.bfloat16
    )
    partial_scores = lax.dot_general(
        lax.all_gather(own_panel, "ex", axis=1, tiled=True),
        stored_grads,
        NT,
        preferred_element_type=jnp.float32,
    )
    return lax.psum_scatter(partial_scores, "dim", scatter_dimension=0, tiled=True)


def scalars(*values):
    return jnp.stack([jnp.asarray(v, jnp.int32) for v in values])


def cut_rows_kernel(at_ref, src_ref, out_ref, sem):
    rows = out_ref.shape[0]
    start = pl.multiple_of(at_ref[0] * rows, rows)
    copy = pltpu.make_async_copy(src_ref.at[pl.ds(start, rows), :], out_ref, sem)
    copy.start()
    copy.wait()


def cut_rows(src, rows, at):
    return pl.pallas_call(
        cut_rows_kernel,
        out_shape=jax.ShapeDtypeStruct((rows, src.shape[1]), src.dtype),
        in_specs=[SMEM, HBM],
        out_specs=VMEM,
        scratch_shapes=[pltpu.SemaphoreType.DMA],
        compiler_params=limit(2),
    )(scalars(at), src)


def cut_kernel(at, at_ref, src_ref, *refs):
    outs, sem = refs[:-1], refs[-1]
    copies = []
    for out_ref, pieces in zip(outs, at):
        width = out_ref.shape[1] // len(pieces)
        for p, i in enumerate(pieces):
            start = pl.multiple_of(at_ref[i] * width, width)
            copies.append(
                pltpu.make_async_copy(
                    src_ref.at[:, pl.ds(start, width)],
                    out_ref.at[:, p * width : (p + 1) * width],
                    sem.at[len(copies)],
                )
            )
            copies[-1].start()
    for copy in copies:
        copy.wait()


def cut(src, width, starts):
    flat = [s for pieces in starts for s in pieces]
    at, i = [], 0
    for pieces in starts:
        at.append(list(range(i, i + len(pieces))))
        i += len(pieces)
    return pl.pallas_call(
        functools.partial(cut_kernel, at),
        out_shape=[jax.ShapeDtypeStruct((src.shape[0], width * len(p)), src.dtype) for p in starts],
        in_specs=[SMEM, HBM],
        out_specs=[VMEM] * len(starts),
        scratch_shapes=[pltpu.SemaphoreType.DMA((len(flat),))],
        compiler_params=limit(4),
        cost_estimate=pl.CostEstimate(
            flops=0, bytes_accessed=2 * src.shape[0] * width * len(flat) * src.dtype.itemsize, transcendentals=0
        ),
    )(scalars(*flat), src)


def fisher_kernel(part, steps, rows, has_base, n_after, at_ref, chunk_ref, fisher_ref, *refs):
    refs = list(refs)
    base_ref = refs.pop(0) if has_base else None
    out_ref, held, sem = refs[n_after:]
    width = chunk_ref.shape[1]
    first = pl.multiple_of(at_ref[1] * (steps * rows), steps * rows) if part else 0
    columns = pl.ds(pl.multiple_of(at_ref[0] * width, width), width)
    copies = []
    for i in range(steps):
        copies.append(
            pltpu.make_async_copy(
                fisher_ref.at[pl.ds(first + i * rows, rows), columns], held.at[i], sem.at[i]
            )
        )
        copies[-1].start()
    chunk = chunk_ref[...].T
    for i in range(steps):
        copies[i].wait()
        term = jnp.dot(held[i], chunk, preferred_element_type=jnp.float32)
        if has_base:
            term = term + base_ref[pl.ds(first + i * rows, rows), :]
        if part:
            out_ref[:, i * rows : (i + 1) * rows] = term.T
        else:
            out_ref[i * rows : (i + 1) * rows, :] = term


def fisher_dot(chunk, column, fisher, base=None, half=None, after=(), rows=256):
    nq, width = chunk.shape
    part = half is not None
    total = fisher.shape[0] // 2 if part else fisher.shape[0]
    steps = total // rows
    operands = [scalars(column, half if part else 0), chunk, fisher]
    operands += [] if base is None else [base]
    return pl.pallas_call(
        functools.partial(fisher_kernel, part, steps, rows, base is not None, len(after)),
        out_shape=jax.ShapeDtypeStruct((nq, total) if part else (total, nq), jnp.float32),
        in_specs=[SMEM, VMEM, HBM] + [VMEM] * (base is not None) + [ANY] * len(after),
        out_specs=VMEM,
        scratch_shapes=[
            pltpu.VMEM((steps, rows, width), fisher.dtype),
            pltpu.SemaphoreType.DMA((steps,)),
        ],
        compiler_params=limit(40),
        cost_estimate=pl.CostEstimate(
            flops=2 * nq * width * total, bytes_accessed=2 * width * total, transcendentals=0
        ),
    )(*operands, *after)


def panel_kernel(mine_ref, core_ref, *refs):
    refs[-1][...] = (mine_ref[...] + core_ref[...]).astype(refs[-1].dtype)


def panel_sum(mine, from_core, after=()):
    return pl.pallas_call(
        panel_kernel,
        out_shape=jax.ShapeDtypeStruct(mine.shape, jnp.bfloat16),
        in_specs=[VMEM] * 2 + [ANY] * len(after),
        out_specs=VMEM,
        compiler_params=limit(2),
    )(mine, from_core, *after)


def score_kernel(n, at_ref, *refs):
    pieces, slabs = refs[:8], refs[8 : 8 + n]
    keep_ref, give_ref, panel, total = refs[8 + n :]
    rows, width = pieces[0].shape
    owner = at_ref[0] == 1
    for q in range(2):
        for p in range(2):
            mine, other = pieces[q * 4 + p * 2], pieces[q * 4 + p * 2 + 1]
            panel[q * rows : (q + 1) * rows, p * width : (p + 1) * width] = jnp.where(
                owner, mine[...], other[...]
            )
    columns = panel[...].T
    for k in range(n):
        total[k] = jnp.dot(slabs[k][...], columns, preferred_element_type=jnp.float32).T
    here = at_ref[1]
    keep_ref[...] = total[:, pl.ds(pl.multiple_of(here * rows, 8), rows), :]
    give_ref[...] = total[:, pl.ds(pl.multiple_of((1 - here) * rows, 8), rows), :]


def score_dot(pieces, slabs, owner, here):
    n = len(slabs)
    rows, width = pieces[0].shape
    ne = slabs[0].shape[0]
    half = jax.ShapeDtypeStruct((n, rows, ne), jnp.float32)
    return pl.pallas_call(
        functools.partial(score_kernel, n),
        out_shape=(half, half),
        in_specs=[SMEM] + [VMEM] * (8 + n),
        out_specs=(VMEM, VMEM),
        scratch_shapes=[
            pltpu.VMEM((2 * rows, 2 * width), jnp.bfloat16),
            pltpu.VMEM((n, 2 * rows, ne), jnp.float32),
        ],
        compiler_params=limit(8),
    )(scalars(owner, here), *pieces, *slabs)


def spread_kernel(a_ref, b_ref, *outs):
    for k, out_ref in enumerate(outs):
        out_ref[...] = a_ref[k] + b_ref[k]


def spread_sum(a, b):
    return pl.pallas_call(
        spread_kernel,
        out_shape=[jax.ShapeDtypeStruct(a.shape[1:], a.dtype)] * a.shape[0],
        in_specs=[VMEM] * 2,
        out_specs=[VMEM] * a.shape[0],
        compiler_params=limit(2),
    )(a, b)


def per_device_quad(nz, nx, ny, queries, inverse_fisher, stored_grads):
    nex = nz * nx
    near = nz // 2
    nq, block = queries.shape
    half = block // ny
    rows = nq // ny
    y, e, d = (lax.axis_index(a) for a in AXES)
    z = e // nx
    x = e % nx
    u = jnp.where(d == 0, z, nz - 1 - z)
    owner = u < near

    def move(value, target):
        pairs = []
        for sy in range(ny):
            for sz in range(nz):
                for sx in range(nx):
                    for sd in range(2):
                        to = target(sy, sz, sx, sd)
                        if to is not None:
                            ty, tz, tx, td = to
                            pairs.append(((sy * nex + sz * nx + sx) * 2 + sd, (ty * nex + tz * nx + tx) * 2 + td))
        return lax.ppermute(value, AXES, pairs)

    def along_z(value, hops, flip=False):
        def target(sy, sz, sx, sd):
            su = sz if sd == 0 else nz - 1 - sz
            if su not in hops:
                return None
            tu = hops[su]
            return 1 - sy if flip else sy, tu if sd == 0 else nz - 1 - tu, sx, sd

        return move(value, target)

    def swap_x(value):
        return move(value, lambda sy, sz, sx, sd: (sy, sz, 1 - sx, sd))

    def swap_y(value):
        return move(value, lambda sy, sz, sx, sd: (1 - sy, sz, sx, sd))

    def swap_xy(value):
        return move(value, lambda sy, sz, sx, sd: (1 - sy, sz, 1 - sx, sd))

    def swap_core(value):
        return move(value, lambda sy, sz, sx, sd: (sy, sz, sx, 1 - sd))

    def to_owner(value):
        def target(sy, sz, sx, sd):
            su = sz if sd == 0 else nz - 1 - sz
            return None if su < near else (sy, sz, sx, 1 - sd)

        return move(value, target)

    same, far, cross, swap = {0: 0, 1: 1}, {0: 2, 1: 3}, {0: 3, 1: 2}, {0: 1, 1: 0}

    def real_plane(k):
        return jnp.where(d == 0, k, nz - 1 - k)

    planes = [real_plane(u % 2), real_plane(1 - u % 2)]

    def column(plane, x_):
        return plane * nx + x_ - d * (nex // 2)

    def slab(x_, y_):
        return [column(p, x_) * ny + y_ for p in planes]

    own = cut_rows(queries, rows, y)
    q0 = jnp.where(owner, own, along_z(own, far))
    q1 = jnp.where(owner, along_z(own, swap), along_z(own, cross))
    q2, q3 = swap_x(q0), swap_x(q1)

    own_slab, to_x, to_y, to_xy = cut(
        stored_grads, half, [slab(x, y), slab(1 - x, y), slab(x, 1 - y), slab(1 - x, 1 - y)]
    )
    pass_on = swap_y(to_xy)
    from_y = swap_y(to_y)
    from_x = swap_x(to_x)
    from_xy = swap_x(pass_on)

    total = fisher_dot(q0, column(planes[0], x), inverse_fisher)
    total = fisher_dot(q1, column(planes[1], x), inverse_fisher, total)
    total = fisher_dot(q2, column(planes[0], 1 - x), inverse_fisher, total, after=[pass_on])
    last = column(planes[1], 1 - x)
    flip = fisher_dot(q3, last, inverse_fisher, total, 1 - y)
    keep = fisher_dot(q3, last, inverse_fisher, total, y, after=[from_y])

    flip = panel_sum(flip, to_owner(flip))
    keep = panel_sum(keep, to_owner(keep), [from_x])

    pieces = [
        keep,
        along_z(keep, far),
        along_z(keep, swap),
        along_z(keep, cross),
        along_z(flip, same, True),
        along_z(flip, far, True),
        along_z(flip, swap, True),
        along_z(flip, cross, True),
    ]
    slabs = [own_slab, from_x, from_y, from_xy]
    keep, give = score_dot(pieces, slabs, owner, y ^ d)

    mine = spread_sum(keep, swap_core(give))
    return ((mine[0] + swap_x(mine[1])) + swap_y(mine[2])) + swap_xy(mine[3])


def solution(mesh):
    coords = [getattr(device, "coords", None) for device in mesh.devices.flat]
    nx = 2 if None in coords else len({c[0] for c in coords})
    nz = mesh.shape["ex"] // nx
    ny = mesh.shape["grp"]
    if (nz, nx, ny) == (4, 2, 2):
        body = functools.partial(per_device_quad, nz, nx, ny)
    else:
        body = per_device_any
    return jax.shard_map(
        body,
        mesh=mesh,
        in_specs=(P(None, "ex"), P("ex", "dim"), P(("grp", "ex"), "dim")),
        out_specs=P("dim", ("grp", "ex")),
        check_vma=False,
    )
```

```python
import functools

import jax
import jax.numpy as jnp
from jax import lax
from jax.experimental import pallas as pl
from jax.experimental.pallas import tpu as pltpu
from jax.sharding import PartitionSpec as P

AXES = ("grp", "ex", "dim")
NT = (((1,), (1,)), ((), ()))
VMEM = pl.BlockSpec(memory_space=pltpu.VMEM)
SMEM = pl.BlockSpec(memory_space=pltpu.SMEM)
HBM = pl.BlockSpec(memory_space=pltpu.HBM)
ANY = pl.BlockSpec(memory_space=pl.ANY)


def limit(mib):
    return pltpu.CompilerParams(vmem_limit_bytes=mib * 1024 * 1024)


def per_device_any(queries, inverse_fisher, stored_grads):
    term_block = jnp.dot(queries, inverse_fisher, preferred_element_type=jnp.float32)
    own_panel = lax.psum_scatter(term_block, "ex", scatter_dimension=1, tiled=True).astype(
        jnp.bfloat16
    )
    partial_scores = lax.dot_general(
        lax.all_gather(own_panel, "ex", axis=1, tiled=True),
        stored_grads,
        NT,
        preferred_element_type=jnp.float32,
    )
    return lax.psum_scatter(partial_scores, "dim", scatter_dimension=0, tiled=True)


def scalars(*values):
    return jnp.stack([jnp.asarray(v, jnp.int32) for v in values])


def cut_rows_kernel(at_ref, src_ref, out_ref, sem):
    rows = out_ref.shape[0]
    start = pl.multiple_of(at_ref[0] * rows, rows)
    copy = pltpu.make_async_copy(src_ref.at[pl.ds(start, rows), :], out_ref, sem)
    copy.start()
    copy.wait()


def cut_rows(src, rows, at):
    return pl.pallas_call(
        cut_rows_kernel,
        out_shape=jax.ShapeDtypeStruct((rows, src.shape[1]), src.dtype),
        in_specs=[SMEM, HBM],
        out_specs=VMEM,
        scratch_shapes=[pltpu.SemaphoreType.DMA],
        compiler_params=limit(2),
    )(scalars(at), src)


def cut_kernel(at, at_ref, src_ref, *refs):
    outs, sem = refs[:-1], refs[-1]
    copies = []
    for out_ref, pieces in zip(outs, at):
        width = out_ref.shape[1] // len(pieces)
        for p, i in enumerate(pieces):
            start = pl.multiple_of(at_ref[i] * width, width)
            copies.append(
                pltpu.make_async_copy(
                    src_ref.at[:, pl.ds(start, width)],
                    out_ref.at[:, p * width : (p + 1) * width],
                    sem.at[len(copies)],
                )
            )
            copies[-1].start()
    for copy in copies:
        copy.wait()


def cut(src, width, starts):
    flat = [s for pieces in starts for s in pieces]
    at, i = [], 0
    for pieces in starts:
        at.append(list(range(i, i + len(pieces))))
        i += len(pieces)
    return pl.pallas_call(
        functools.partial(cut_kernel, at),
        out_shape=[jax.ShapeDtypeStruct((src.shape[0], width * len(p)), src.dtype) for p in starts],
        in_specs=[SMEM, HBM],
        out_specs=[VMEM] * len(starts),
        scratch_shapes=[pltpu.SemaphoreType.DMA((len(flat),))],
        compiler_params=limit(4),
        cost_estimate=pl.CostEstimate(
            flops=0, bytes_accessed=2 * src.shape[0] * width * len(flat) * src.dtype.itemsize, transcendentals=0
        ),
    )(scalars(*flat), src)


def fisher_kernel(part, steps, n_after, has_base, at_ref, chunk_ref, fisher_ref, *refs):
    refs = list(refs)
    base_ref = refs.pop(0) if has_base else None
    out_ref, held, acc, sem = refs[n_after:]
    width = chunk_ref.shape[1]
    rows, step = held.shape[1:]
    first = pl.multiple_of(at_ref[1] * rows, rows) if part else 0
    start = pl.multiple_of(at_ref[0] * width, width)
    copies = []
    for i in range(steps):
        copies.append(
            pltpu.make_async_copy(
                fisher_ref.at[pl.ds(first, rows), pl.ds(start + i * step, step)], held.at[i], sem.at[i]
            )
        )
        copies[-1].start()
    chunk = chunk_ref[...].T
    total = acc if part else out_ref
    for i in range(steps):
        copies[i].wait()
        term = jnp.dot(
            held[i], chunk[i * step : (i + 1) * step], preferred_element_type=jnp.float32
        )
        if i:
            term = term + total[...]
        elif has_base:
            term = term + base_ref[pl.ds(first, rows), :]
        if part and i == steps - 1:
            out_ref[...] = term.T
        else:
            total[...] = term


def fisher_dot(chunk, column, fisher, base=None, half=None, after=(), step=512):
    nq, width = chunk.shape
    part = half is not None
    rows = fisher.shape[0] // 2 if part else fisher.shape[0]
    steps = width // step
    operands = [scalars(column, half if part else 0), chunk, fisher]
    operands += [] if base is None else [base]
    return pl.pallas_call(
        functools.partial(fisher_kernel, part, steps, len(after), base is not None),
        out_shape=jax.ShapeDtypeStruct((nq, rows) if part else (rows, nq), jnp.float32),
        in_specs=[SMEM, VMEM, HBM] + [VMEM] * (base is not None) + [ANY] * len(after),
        out_specs=VMEM,
        scratch_shapes=[
            pltpu.VMEM((steps, rows, step), fisher.dtype),
            pltpu.VMEM((rows if part else 8, nq), jnp.float32),
            pltpu.SemaphoreType.DMA((steps,)),
        ],
        compiler_params=limit(40),
        cost_estimate=pl.CostEstimate(
            flops=2 * nq * width * rows, bytes_accessed=2 * width * rows, transcendentals=0
        ),
    )(*operands, *after)


def panel_kernel(mine_ref, core_ref, *refs):
    refs[-1][...] = (mine_ref[...] + core_ref[...]).astype(refs[-1].dtype)


def panel_sum(mine, from_core, after=()):
    return pl.pallas_call(
        panel_kernel,
        out_shape=jax.ShapeDtypeStruct(mine.shape, jnp.bfloat16),
        in_specs=[VMEM] * 2 + [ANY] * len(after),
        out_specs=VMEM,
        compiler_params=limit(2),
    )(mine, from_core, *after)


def score_kernel(n, at_ref, *refs):
    pieces, slabs = refs[:8], refs[8 : 8 + n]
    out_ref, panel = refs[8 + n :]
    rows, width = pieces[0].shape
    owner = at_ref[0] == 1
    y, x = at_ref[1], at_ref[2]
    for q in range(2):
        for p in range(2):
            mine, other = pieces[q * 4 + p * 2], pieces[q * 4 + p * 2 + 1]
            panel[q * rows : (q + 1) * rows, p * width : (p + 1) * width] = jnp.where(
                owner, mine[...], other[...]
            )
    columns = panel[...].T
    for k in range(n):
        term = jnp.dot(slabs[k][...], columns, preferred_element_type=jnp.float32).T
        chip = (y ^ (k // 2)) * 2 + (x ^ (k % 2))
        for q in range(2):
            out_ref[chip * 2 + (y ^ q)] = term[q * rows : (q + 1) * rows]


def score_dot(pieces, slabs, owner, y, x):
    n = len(slabs)
    rows, width = pieces[0].shape
    return pl.pallas_call(
        functools.partial(score_kernel, n),
        out_shape=jax.ShapeDtypeStruct((2 * n, rows, slabs[0].shape[0]), jnp.float32),
        in_specs=[SMEM] + [VMEM] * (8 + n),
        out_specs=VMEM,
        scratch_shapes=[pltpu.VMEM((2 * rows, 2 * width), jnp.bfloat16)],
        compiler_params=limit(8),
    )(scalars(owner, y, x), *pieces, *slabs)


def per_device_quad(nz, nx, ny, queries, inverse_fisher, stored_grads):
    nex = nz * nx
    near = nz // 2
    nq, block = queries.shape
    half = block // ny
    rows = nq // ny
    y, e, d = (lax.axis_index(a) for a in AXES)
    z = e // nx
    x = e % nx
    u = jnp.where(d == 0, z, nz - 1 - z)
    owner = u < near

    def move(value, target):
        pairs = []
        for sy in range(ny):
            for sz in range(nz):
                for sx in range(nx):
                    for sd in range(2):
                        to = target(sy, sz, sx, sd)
                        if to is not None:
                            ty, tz, tx, td = to
                            pairs.append(((sy * nex + sz * nx + sx) * 2 + sd, (ty * nex + tz * nx + tx) * 2 + td))
        return lax.ppermute(value, AXES, pairs)

    def along_z(value, hops, flip=False):
        def target(sy, sz, sx, sd):
            su = sz if sd == 0 else nz - 1 - sz
            if su not in hops:
                return None
            tu = hops[su]
            return 1 - sy if flip else sy, tu if sd == 0 else nz - 1 - tu, sx, sd

        return move(value, target)

    def swap_x(value):
        return move(value, lambda sy, sz, sx, sd: (sy, sz, 1 - sx, sd))

    def swap_y(value):
        return move(value, lambda sy, sz, sx, sd: (1 - sy, sz, sx, sd))

    def to_owner(value):
        def target(sy, sz, sx, sd):
            su = sz if sd == 0 else nz - 1 - sz
            return None if su < near else (sy, sz, sx, 1 - sd)

        return move(value, target)

    same, far, cross, swap = {0: 0, 1: 1}, {0: 2, 1: 3}, {0: 3, 1: 2}, {0: 1, 1: 0}

    def real_plane(k):
        return jnp.where(d == 0, k, nz - 1 - k)

    planes = [real_plane(u % 2), real_plane(1 - u % 2)]

    def column(plane, x_):
        return plane * nx + x_ - d * (nex // 2)

    def slab(x_, y_):
        return [column(p, x_) * ny + y_ for p in planes]

    own = cut_rows(queries, rows, y)
    q0 = jnp.where(owner, own, along_z(own, far))
    q1 = jnp.where(owner, along_z(own, swap), along_z(own, cross))
    q2, q3 = swap_x(q0), swap_x(q1)

    own_slab, to_x, to_y, to_xy = cut(
        stored_grads, half, [slab(x, y), slab(1 - x, y), slab(x, 1 - y), slab(1 - x, 1 - y)]
    )
    pass_on = swap_y(to_xy)
    from_y = swap_y(to_y)
    from_x = swap_x(to_x)
    from_xy = swap_x(pass_on)

    total = fisher_dot(q0, column(planes[0], x), inverse_fisher)
    total = fisher_dot(q1, column(planes[1], x), inverse_fisher, total)
    total = fisher_dot(q2, column(planes[0], 1 - x), inverse_fisher, total, after=[pass_on])
    last = column(planes[1], 1 - x)
    flip = fisher_dot(q3, last, inverse_fisher, total, 1 - y)
    keep = fisher_dot(q3, last, inverse_fisher, total, y, after=[from_y])

    flip = panel_sum(flip, to_owner(flip))
    keep = panel_sum(keep, to_owner(keep), [from_x])

    pieces = [
        keep,
        along_z(keep, far),
        along_z(keep, swap),
        along_z(keep, cross),
        along_z(flip, same, True),
        along_z(flip, far, True),
        along_z(flip, swap, True),
        along_z(flip, cross, True),
    ]
    slabs = [own_slab, from_x, from_y, from_xy]
    scores = score_dot(pieces, slabs, owner, y, x)

    planes_devices = [
        [(sy * nex + sz * nx + sx) * 2 + sd for sy in range(ny) for sx in range(nx) for sd in range(2)]
        for sz in range(nz)
    ]
    return jnp.sum(lax.all_to_all(scores, AXES, 0, 0, axis_index_groups=planes_devices), axis=0)


def solution(mesh):
    coords = [getattr(device, "coords", None) for device in mesh.devices.flat]
    nx = 2 if None in coords else len({c[0] for c in coords})
    nz = mesh.shape["ex"] // nx
    ny = mesh.shape["grp"]
    if (nz, nx, ny) == (4, 2, 2):
        body = functools.partial(per_device_quad, nz, nx, ny)
    else:
        body = per_device_any
    return jax.shard_map(
        body,
        mesh=mesh,
        in_specs=(P(None, "ex"), P("ex", "dim"), P(("grp", "ex"), "dim")),
        out_specs=P("dim", ("grp", "ex")),
        check_vma=False,
    )
```

```python
import functools

import jax
import jax.numpy as jnp
from jax import lax
from jax.experimental import pallas as pl
from jax.experimental.pallas import tpu as pltpu
from jax.sharding import PartitionSpec as P

AXES = ("grp", "ex", "dim")
NT = (((1,), (1,)), ((), ()))
VMEM = pl.BlockSpec(memory_space=pltpu.VMEM)
SMEM = pl.BlockSpec(memory_space=pltpu.SMEM)
HBM = pl.BlockSpec(memory_space=pltpu.HBM)
ANY = pl.BlockSpec(memory_space=pl.ANY)


def limit(mib):
    return pltpu.CompilerParams(vmem_limit_bytes=mib * 1024 * 1024)


def per_device_any(queries, inverse_fisher, stored_grads):
    term_block = jnp.dot(queries, inverse_fisher, preferred_element_type=jnp.float32)
    own_panel = lax.psum_scatter(term_block, "ex", scatter_dimension=1, tiled=True).astype(
        jnp.bfloat16
    )
    partial_scores = lax.dot_general(
        lax.all_gather(own_panel, "ex", axis=1, tiled=True),
        stored_grads,
        NT,
        preferred_element_type=jnp.float32,
    )
    return lax.psum_scatter(partial_scores, "dim", scatter_dimension=0, tiled=True)


def scalars(*values):
    return jnp.stack([jnp.asarray(v, jnp.int32) for v in values])


def cut_rows_kernel(at_ref, src_ref, out_ref, sem):
    rows = out_ref.shape[0]
    start = pl.multiple_of(at_ref[0] * rows, rows)
    copy = pltpu.make_async_copy(src_ref.at[pl.ds(start, rows), :], out_ref, sem)
    copy.start()
    copy.wait()


def cut_rows(src, rows, at):
    return pl.pallas_call(
        cut_rows_kernel,
        out_shape=jax.ShapeDtypeStruct((rows, src.shape[1]), src.dtype),
        in_specs=[SMEM, HBM],
        out_specs=VMEM,
        scratch_shapes=[pltpu.SemaphoreType.DMA],
        compiler_params=limit(2),
    )(scalars(at), src)


def fisher_kernel(part, steps, has_base, at_ref, chunk_ref, fisher_ref, *refs):
    refs = list(refs)
    base_ref = refs.pop(0) if has_base else None
    out_ref, held, sem = refs
    width = chunk_ref.shape[1]
    rows, step = held.shape[1:]
    first = pl.multiple_of(at_ref[1] * rows, rows) if part else 0
    start = pl.multiple_of(at_ref[0] * width, width)
    copies = []
    for i in range(steps):
        copies.append(
            pltpu.make_async_copy(
                fisher_ref.at[pl.ds(first, rows), pl.ds(start + i * step, step)], held.at[i], sem.at[i]
            )
        )
        copies[-1].start()
    for i in range(steps):
        copies[i].wait()
        term = lax.dot_general(
            chunk_ref[:, i * step : (i + 1) * step], held[i], NT, preferred_element_type=jnp.float32
        )
        if i:
            term = term + out_ref[...]
        elif has_base:
            term = term + base_ref[:, pl.ds(first, rows)]
        out_ref[...] = term


def fisher_dot(chunk, column, fisher, base=None, half=None, step=512):
    nq, width = chunk.shape
    part = half is not None
    rows = fisher.shape[0] // 2 if part else fisher.shape[0]
    steps = width // step
    operands = [scalars(column, half if part else 0), chunk, fisher]
    operands += [] if base is None else [base]
    return pl.pallas_call(
        functools.partial(fisher_kernel, part, steps, base is not None),
        out_shape=jax.ShapeDtypeStruct((nq, rows), jnp.float32),
        in_specs=[SMEM, VMEM, HBM] + [VMEM] * (base is not None),
        out_specs=VMEM,
        scratch_shapes=[
            pltpu.VMEM((steps, rows, step), fisher.dtype),
            pltpu.SemaphoreType.DMA((steps,)),
        ],
        compiler_params=limit(34),
        cost_estimate=pl.CostEstimate(
            flops=2 * nq * width * rows, bytes_accessed=2 * width * rows, transcendentals=0
        ),
    )(*operands)


def panel_kernel(*refs):
    out_ref = refs[-1]
    width = refs[0].shape[1]
    for k in range(len(refs) // 2):
        out_ref[:, k * width : (k + 1) * width] = (refs[2 * k][...] + refs[2 * k + 1][...]).astype(out_ref.dtype)


def panel_sum(*terms):
    rows, width = terms[0].shape
    return pl.pallas_call(
        panel_kernel,
        out_shape=jax.ShapeDtypeStruct((rows, width * len(terms) // 2), jnp.bfloat16),
        in_specs=[VMEM] * len(terms),
        out_specs=VMEM,
        compiler_params=limit(2),
    )(*terms)


def score_kernel(n, at_ref, *refs):
    grads_ref, out_ref = refs[n:]
    width = refs[0].shape[1]
    total = None
    for k in range(n):
        grads = grads_ref[:, pl.ds(pl.multiple_of(at_ref[k] * width, width), width)]
        term = lax.dot_general(refs[k][...], grads, NT, preferred_element_type=jnp.float32)
        total = term if total is None else total + term
    out_ref[...] = total


def score_dot(pieces, columns, grads):
    n = len(pieces)
    rows, width = pieces[0].shape
    return pl.pallas_call(
        functools.partial(score_kernel, n),
        out_shape=jax.ShapeDtypeStruct((rows, grads.shape[0]), jnp.float32),
        in_specs=[SMEM] + [VMEM] * (n + 1),
        out_specs=VMEM,
        compiler_params=limit(8),
        cost_estimate=pl.CostEstimate(
            flops=2 * n * rows * width * grads.shape[0],
            bytes_accessed=2 * n * width * grads.shape[0],
            transcendentals=0,
        ),
    )(scalars(*columns), *pieces, grads)


def per_device_quad(nz, nx, ny, queries, inverse_fisher, stored_grads):
    nex = nz * nx
    near = nz // 2
    nq = queries.shape[0]
    y, e, d = (lax.axis_index(a) for a in AXES)
    z = e // nx
    x = e % nx
    u = jnp.where(d == 0, z, nz - 1 - z)
    owner = u < near

    def move(value, target):
        pairs = []
        for sy in range(ny):
            for sz in range(nz):
                for sx in range(nx):
                    for sd in range(2):
                        to = target(sy, sz, sx, sd)
                        if to is not None:
                            ty, tz, tx, td = to
                            pairs.append(((sy * nex + sz * nx + sx) * 2 + sd, (ty * nex + tz * nx + tx) * 2 + td))
        return lax.ppermute(value, AXES, pairs)

    def along_z(value, hops):
        def target(sy, sz, sx, sd):
            su = sz if sd == 0 else nz - 1 - sz
            if su not in hops:
                return None
            tu = hops[su]
            return sy, tu if sd == 0 else nz - 1 - tu, sx, sd

        return move(value, target)

    def swap_x(value):
        return move(value, lambda sy, sz, sx, sd: (sy, sz, 1 - sx, sd))

    def swap_y(value):
        return move(value, lambda sy, sz, sx, sd: (1 - sy, sz, sx, sd))

    def to_owner(value):
        def target(sy, sz, sx, sd):
            su = sz if sd == 0 else nz - 1 - sz
            return None if su < near else (sy, sz, sx, 1 - sd)

        return move(value, target)

    def real_plane(k):
        return jnp.where(d == 0, k, nz - 1 - k)

    def gather(own):
        first = jnp.where(owner, own, along_z(own, {0: 2, 1: 3}))
        second = jnp.where(owner, along_z(own, {0: 1, 1: 0}), along_z(own, {0: 3, 1: 2}))
        return [first, second, swap_x(first), swap_x(second)]

    planes = [real_plane(u % 2), real_plane(1 - u % 2)]
    columns = [p * nx + x_ - d * (nex // 2) for x_ in (x, 1 - x) for p in planes]

    other_grads = swap_y(stored_grads)

    pieces = gather(cut_rows(queries, nq // ny, y))
    total = None
    for piece, column in zip(pieces[:-1], columns):
        total = fisher_dot(piece, column, inverse_fisher, total)
    halves = [fisher_dot(pieces[-1], columns[-1], inverse_fisher, total, h) for h in range(2)]
    panel = panel_sum(halves[0], to_owner(halves[0]), halves[1], to_owner(halves[1]))

    pieces = gather(panel)
    other = score_dot(pieces, columns, other_grads)
    mine = score_dot(pieces, columns, stored_grads)

    def to_core_y(value):
        return move(value, lambda sy, sz, sx, sd: (sy, sz, sx, sy) if sd != sy else None)

    other = other + to_core_y(other)
    mine = mine + to_core_y(mine)
    other = move(other, lambda sy, sz, sx, sd: (1 - sy, sz, sx, sd) if sd == sy else None)
    return jnp.where(d == y, mine, other)


def solution(mesh):
    coords = [getattr(device, "coords", None) for device in mesh.devices.flat]
    nx = 2 if None in coords else len({c[0] for c in coords})
    nz = mesh.shape["ex"] // nx
    ny = mesh.shape["grp"]
    if (nz, nx, ny) == (4, 2, 2):
        body = functools.partial(per_device_quad, nz, nx, ny)
    else:
        body = per_device_any
    return jax.shard_map(
        body,
        mesh=mesh,
        in_specs=(P(None, "ex"), P("ex", "dim"), P(("grp", "ex"), "dim")),
        out_specs=P("dim", ("grp", "ex")),
        check_vma=False,
    )
```

```python
import functools

import jax
import jax.numpy as jnp
from jax import lax
from jax.experimental import pallas as pl
from jax.experimental.pallas import tpu as pltpu
from jax.sharding import PartitionSpec as P

AXES = ("grp", "ex", "dim")
NT = (((1,), (1,)), ((), ()))
VMEM = pl.BlockSpec(memory_space=pltpu.VMEM)
SMEM = pl.BlockSpec(memory_space=pltpu.SMEM)
HBM = pl.BlockSpec(memory_space=pltpu.HBM)
ANY = pl.BlockSpec(memory_space=pl.ANY)


def limit(mib):
    return pltpu.CompilerParams(vmem_limit_bytes=mib * 1024 * 1024)


def per_device_any(queries, inverse_fisher, stored_grads):
    term_block = jnp.dot(queries, inverse_fisher, preferred_element_type=jnp.float32)
    own_panel = lax.psum_scatter(term_block, "ex", scatter_dimension=1, tiled=True).astype(
        jnp.bfloat16
    )
    partial_scores = lax.dot_general(
        lax.all_gather(own_panel, "ex", axis=1, tiled=True),
        stored_grads,
        NT,
        preferred_element_type=jnp.float32,
    )
    return lax.psum_scatter(partial_scores, "dim", scatter_dimension=0, tiled=True)


def scalars(*values):
    return jnp.stack([jnp.asarray(v, jnp.int32) for v in values])


def cut_rows_kernel(at_ref, src_ref, out_ref, sem):
    rows = out_ref.shape[0]
    start = pl.multiple_of(at_ref[0] * rows, rows)
    copy = pltpu.make_async_copy(src_ref.at[pl.ds(start, rows), :], out_ref, sem)
    copy.start()
    copy.wait()


def cut_rows(src, rows, at):
    return pl.pallas_call(
        cut_rows_kernel,
        out_shape=jax.ShapeDtypeStruct((rows, src.shape[1]), src.dtype),
        in_specs=[SMEM, HBM],
        out_specs=VMEM,
        scratch_shapes=[pltpu.SemaphoreType.DMA],
        compiler_params=limit(2),
    )(scalars(at), src)


def start_blocks(fisher_ref, at, held_ref, sem):
    steps = sem.shape[0]
    rows, width = held_ref.shape
    step = rows // steps
    columns = pl.ds(pl.multiple_of(at * width, width), width)
    copies = []
    for i in range(steps):
        block = pl.ds(i * step, step)
        copies.append(pltpu.make_async_copy(fisher_ref.at[block, columns], held_ref.at[block, :], sem.at[i]))
        copies[-1].start()
    return copies


def times(chunk_ref, fisher):
    return lax.dot_general(chunk_ref[...], fisher, NT, preferred_element_type=jnp.float32)


def load_kernel(n, at_ref, fisher_ref, *refs):
    copies = []
    for k in range(n):
        copies += start_blocks(fisher_ref, at_ref[k], refs[k], refs[n].at[k])
    for copy in copies:
        copy.wait()


def load(fisher, columns, width, steps=4):
    n = len(columns)
    return pl.pallas_call(
        functools.partial(load_kernel, n),
        out_shape=[jax.ShapeDtypeStruct((fisher.shape[0], width), fisher.dtype)] * n,
        in_specs=[SMEM, HBM],
        out_specs=[VMEM] * n,
        scratch_shapes=[pltpu.SemaphoreType.DMA((n, steps))],
        compiler_params=limit(34),
        cost_estimate=pl.CostEstimate(
            flops=0, bytes_accessed=2 * n * width * fisher.shape[0], transcendentals=0
        ),
    )(scalars(*columns), fisher)


def fisher_first_kernel(at_ref, chunk0, chunk1, block0, block1, fisher_ref, out_ref, next_ref, sem):
    copies = start_blocks(fisher_ref, at_ref[0], next_ref, sem)
    step = block0.shape[0] // sem.shape[0]
    for i in range(sem.shape[0]):
        rows = slice(i * step, (i + 1) * step)
        out_ref[:, rows] = times(chunk0, block0[rows, :]) + times(chunk1, block1[rows, :])
    for copy in copies:
        copy.wait()


def fisher_first(chunks, blocks, column, fisher, steps=4):
    nq, width = chunks[0].shape
    rows = fisher.shape[0]
    return pl.pallas_call(
        fisher_first_kernel,
        out_shape=[
            jax.ShapeDtypeStruct((nq, rows), jnp.float32),
            jax.ShapeDtypeStruct((rows, width), fisher.dtype),
        ],
        in_specs=[SMEM] + [VMEM] * 4 + [HBM],
        out_specs=[VMEM] * 2,
        scratch_shapes=[pltpu.SemaphoreType.DMA((steps,))],
        compiler_params=limit(8),
        cost_estimate=pl.CostEstimate(
            flops=4 * nq * width * rows, bytes_accessed=2 * width * rows, transcendentals=0
        ),
    )(scalars(column), *chunks, *blocks, fisher)


def fisher_last_kernel(at_ref, chunk0, chunk1, block0, base_ref, fisher_ref, out_ref, held, sem):
    copies = start_blocks(fisher_ref, at_ref[0], held, sem)
    step = held.shape[0] // sem.shape[0]
    for i in range(sem.shape[0]):
        rows = slice(i * step, (i + 1) * step)
        out_ref[:, rows] = base_ref[:, rows] + times(chunk0, block0[rows, :])
    for i in range(sem.shape[0]):
        rows = slice(i * step, (i + 1) * step)
        copies[i].wait()
        out_ref[:, rows] += times(chunk1, held[rows, :])


def fisher_last(chunks, block, base, column, fisher, steps=4):
    nq, width = chunks[0].shape
    rows = fisher.shape[0]
    return pl.pallas_call(
        fisher_last_kernel,
        out_shape=jax.ShapeDtypeStruct((nq, rows), jnp.float32),
        in_specs=[SMEM] + [VMEM] * 4 + [HBM],
        out_specs=VMEM,
        scratch_shapes=[pltpu.VMEM((rows, width), fisher.dtype), pltpu.SemaphoreType.DMA((steps,))],
        compiler_params=limit(16),
        cost_estimate=pl.CostEstimate(
            flops=4 * nq * width * rows, bytes_accessed=2 * width * rows, transcendentals=0
        ),
    )(scalars(column), *chunks, block, base, fisher)


def score_kernel(n, at_ref, *refs):
    grads_ref, out_ref = refs[n], refs[-1]
    width = refs[0].shape[1]
    total = refs[n + 1][...] if len(refs) > n + 2 else None
    for k in range(n):
        grads = grads_ref[:, pl.ds(pl.multiple_of(at_ref[k] * width, width), width)]
        term = times(refs[k], grads)
        total = term if total is None else total + term
    out_ref[...] = total


def score_dot(pieces, columns, grads, *base):
    n = len(pieces)
    rows, width = pieces[0].shape
    return pl.pallas_call(
        functools.partial(score_kernel, n),
        out_shape=jax.ShapeDtypeStruct((rows, grads.shape[0]), jnp.float32),
        in_specs=[SMEM] + [VMEM] * (n + 1 + len(base)),
        out_specs=VMEM,
        compiler_params=limit(8),
        cost_estimate=pl.CostEstimate(
            flops=2 * n * rows * width * grads.shape[0],
            bytes_accessed=2 * n * width * grads.shape[0],
            transcendentals=0,
        ),
    )(scalars(*columns), *pieces, grads, *base)


def pick_kernel(at_ref, a_ref, b_ref, *refs):
    out_ref = refs[-1]

    @pl.when(at_ref[0] == 1)
    def _():
        out_ref[...] = a_ref[...]

    @pl.when(at_ref[0] != 1)
    def _():
        out_ref[...] = b_ref[...]


def pick(condition, a, b, after=()):
    return pl.pallas_call(
        pick_kernel,
        out_shape=jax.ShapeDtypeStruct(a.shape, a.dtype),
        in_specs=[SMEM] + [VMEM] * 2 + [ANY] * len(after),
        out_specs=VMEM,
        compiler_params=limit(2),
        cost_estimate=pl.CostEstimate(flops=0, bytes_accessed=2 * a.size * 2, transcendentals=0),
    )(scalars(condition), a, b, *after)


def per_device_quad(nz, nx, ny, queries, inverse_fisher, stored_grads):
    nex = nz * nx
    near = nz // 2
    nq = queries.shape[0]
    y, e, d = (lax.axis_index(a) for a in AXES)
    z = e // nx
    x = e % nx
    u = jnp.where(d == 0, z, nz - 1 - z)
    owner = u < near

    def move(value, target):
        pairs = []
        for sy in range(ny):
            for sz in range(nz):
                for sx in range(nx):
                    for sd in range(2):
                        to = target(sy, sz, sx, sd)
                        if to is not None:
                            ty, tz, tx, td = to
                            pairs.append(((sy * nex + sz * nx + sx) * 2 + sd, (ty * nex + tz * nx + tx) * 2 + td))
        return lax.ppermute(value, AXES, pairs)

    def along_z(value, hops):
        def target(sy, sz, sx, sd):
            su = sz if sd == 0 else nz - 1 - sz
            if su not in hops:
                return None
            tu = hops[su]
            return sy, tu if sd == 0 else nz - 1 - tu, sx, sd

        return move(value, target)

    def swap_x(value):
        return move(value, lambda sy, sz, sx, sd: (sy, sz, 1 - sx, sd))

    def swap_y(value):
        return move(value, lambda sy, sz, sx, sd: (1 - sy, sz, sx, sd))

    def to_owner(value):
        def target(sy, sz, sx, sd):
            su = sz if sd == 0 else nz - 1 - sz
            return None if su < near else (sy, sz, sx, 1 - sd)

        return move(value, target)

    def real_plane(k):
        return jnp.where(d == 0, k, nz - 1 - k)

    def gather(own, after=()):
        first = pick(owner, own, along_z(own, {0: 2, 1: 3}), after)
        second = pick(owner, along_z(own, {0: 1, 1: 0}), along_z(own, {0: 3, 1: 2}))
        return [first, second, swap_x(first), swap_x(second)]

    planes = [real_plane(u % 2), real_plane(1 - u % 2)]
    columns = [p * nx + x_ - d * (nex // 2) for x_ in (x, 1 - x) for p in planes]

    other_grads = swap_y(stored_grads)

    own = cut_rows(queries, nq // ny, y)
    blocks = load(inverse_fisher, columns[:2], own.shape[1])
    pieces = gather(own, blocks[:1])
    total, block = fisher_first(pieces[:2], blocks, columns[2], inverse_fisher)
    total = fisher_last(pieces[2:], block, total, columns[3], inverse_fisher)
    panel = (total + to_owner(total)).astype(jnp.bfloat16)

    pieces = gather(panel)
    other, mine = (
        score_dot(pieces[3:], columns[3:], grads, score_dot(pieces[:3], columns[:3], grads))
        for grads in (other_grads, stored_grads)
    )
    other = move(other, lambda sy, sz, sx, sd: (1 - sy, sz, sx, sy) if sd != sy else None) + move(
        other, lambda sy, sz, sx, sd: (1 - sy, sz, sx, sy) if sd == sy else None
    )
    mine = mine + move(mine, lambda sy, sz, sx, sd: (sy, sz, sx, sy) if sd != sy else None)
    return jnp.where(d == y, mine, other)


def solution(mesh):
    coords = [getattr(device, "coords", None) for device in mesh.devices.flat]
    nx = 2 if None in coords else len({c[0] for c in coords})
    nz = mesh.shape["ex"] // nx
    ny = mesh.shape["grp"]
    if (nz, nx, ny) == (4, 2, 2):
        body = functools.partial(per_device_quad, nz, nx, ny)
    else:
        body = per_device_any
    return jax.shard_map(
        body,
        mesh=mesh,
        in_specs=(P(None, "ex"), P("ex", "dim"), P(("grp", "ex"), "dim")),
        out_specs=P("dim", ("grp", "ex")),
        check_vma=False,
    )
```

```python
import functools

import jax
import jax.numpy as jnp
from jax import lax
from jax.experimental import pallas as pl
from jax.experimental.pallas import tpu as pltpu
from jax.sharding import PartitionSpec as P

AXES = ("grp", "ex", "dim")
NT = (((1,), (1,)), ((), ()))
VMEM = pl.BlockSpec(memory_space=pltpu.VMEM)
SMEM = pl.BlockSpec(memory_space=pltpu.SMEM)
HBM = pl.BlockSpec(memory_space=pltpu.HBM)
ANY = pl.BlockSpec(memory_space=pl.ANY)


def limit(mib):
    return pltpu.CompilerParams(vmem_limit_bytes=mib * 1024 * 1024)


def per_device_any(queries, inverse_fisher, stored_grads):
    term_block = jnp.dot(queries, inverse_fisher, preferred_element_type=jnp.float32)
    own_panel = lax.psum_scatter(term_block, "ex", scatter_dimension=1, tiled=True).astype(
        jnp.bfloat16
    )
    partial_scores = lax.dot_general(
        lax.all_gather(own_panel, "ex", axis=1, tiled=True),
        stored_grads,
        NT,
        preferred_element_type=jnp.float32,
    )
    return lax.psum_scatter(partial_scores, "dim", scatter_dimension=0, tiled=True)


def scalar(value):
    return jnp.asarray(value, jnp.int32).reshape(1)


ORDER = (0, 2, 1, 3)


def cut_rows_kernel(at_ref, src_ref, out_ref, sem):
    rows = out_ref.shape[0]
    start = pl.multiple_of(at_ref[0] * rows, rows)
    copy = pltpu.make_async_copy(src_ref.at[pl.ds(start, rows), :], out_ref, sem)
    copy.start()
    copy.wait()


def cut_rows(src, rows, at):
    return pl.pallas_call(
        cut_rows_kernel,
        out_shape=jax.ShapeDtypeStruct((rows, src.shape[1]), src.dtype),
        in_specs=[SMEM, HBM],
        out_specs=VMEM,
        scratch_shapes=[pltpu.SemaphoreType.DMA],
        compiler_params=limit(2),
    )(scalar(at), src)


def start_blocks(fisher_ref, at, held_ref, sem):
    steps = sem.shape[0]
    rows, width = held_ref.shape
    step = rows // steps
    columns = pl.ds(pl.multiple_of(at * width, width), width)
    copies = []
    for i in range(steps):
        block = pl.ds(i * step, step)
        copies.append(pltpu.make_async_copy(fisher_ref.at[block, columns], held_ref.at[block, :], sem.at[i]))
        copies[-1].start()
    return copies


def times(chunk_ref, fisher):
    return lax.dot_general(chunk_ref[...], fisher, NT, preferred_element_type=jnp.float32)


def load_kernel(at_ref, fisher_ref, *refs):
    copies = []
    for k, held_ref in enumerate(refs[:-1]):
        copies += start_blocks(fisher_ref, at_ref[0] ^ ORDER[k], held_ref, refs[-1].at[k])
    for copy in copies:
        copy.wait()


def load(fisher, first, n, width, steps=4):
    return pl.pallas_call(
        load_kernel,
        out_shape=[jax.ShapeDtypeStruct((fisher.shape[0], width), fisher.dtype)] * n,
        in_specs=[SMEM, HBM],
        out_specs=[VMEM] * n,
        scratch_shapes=[pltpu.SemaphoreType.DMA((n, steps))],
        compiler_params=limit(34),
        cost_estimate=pl.CostEstimate(
            flops=0, bytes_accessed=2 * n * width * fisher.shape[0], transcendentals=0
        ),
    )(scalar(first), fisher)


def fisher_first_kernel(at_ref, chunk0, chunk1, block0, block1, fisher_ref, out_ref, next_ref, sem):
    copies = start_blocks(fisher_ref, at_ref[0] ^ ORDER[2], next_ref, sem)
    step = block0.shape[0] // sem.shape[0]
    for i in range(sem.shape[0]):
        rows = slice(i * step, (i + 1) * step)
        out_ref[:, rows] = times(chunk0, block0[rows, :])
    for i in range(sem.shape[0]):
        rows = slice(i * step, (i + 1) * step)
        out_ref[:, rows] += times(chunk1, block1[rows, :])
    for copy in copies:
        copy.wait()


def fisher_first(chunks, blocks, first, fisher, steps=4):
    nq, width = chunks[0].shape
    rows = fisher.shape[0]
    return pl.pallas_call(
        fisher_first_kernel,
        out_shape=[
            jax.ShapeDtypeStruct((nq, rows), jnp.float32),
            jax.ShapeDtypeStruct((rows, width), fisher.dtype),
        ],
        in_specs=[SMEM] + [VMEM] * 4 + [HBM],
        out_specs=[VMEM] * 2,
        scratch_shapes=[pltpu.SemaphoreType.DMA((steps,))],
        compiler_params=limit(8),
        cost_estimate=pl.CostEstimate(
            flops=4 * nq * width * rows, bytes_accessed=2 * width * rows, transcendentals=0
        ),
    )(scalar(first), *chunks, *blocks, fisher)


def fisher_last_kernel(at_ref, chunk0, chunk1, block0, base_ref, fisher_ref, out_ref, held, sem):
    copies = start_blocks(fisher_ref, at_ref[0] ^ ORDER[3], held, sem)
    step = held.shape[0] // sem.shape[0]
    for i in range(sem.shape[0]):
        rows = slice(i * step, (i + 1) * step)
        out_ref[:, rows] = base_ref[:, rows] + times(chunk0, block0[rows, :])
    for i in range(sem.shape[0]):
        rows = slice(i * step, (i + 1) * step)
        copies[i].wait()
        out_ref[:, rows] += times(chunk1, held[rows, :])


def fisher_last(chunks, block, base, first, fisher, steps=4):
    nq, width = chunks[0].shape
    rows = fisher.shape[0]
    return pl.pallas_call(
        fisher_last_kernel,
        out_shape=jax.ShapeDtypeStruct((nq, rows), jnp.float32),
        in_specs=[SMEM] + [VMEM] * 4 + [HBM],
        out_specs=VMEM,
        scratch_shapes=[pltpu.VMEM((rows, width), fisher.dtype), pltpu.SemaphoreType.DMA((steps,))],
        compiler_params=limit(16),
        cost_estimate=pl.CostEstimate(
            flops=4 * nq * width * rows, bytes_accessed=2 * width * rows, transcendentals=0
        ),
    )(scalar(first), *chunks, block, base, fisher)


def score_kernel(order, has_base, at_ref, *refs):
    n = len(order)
    grads_ref, out_ref = refs[n], refs[-1]
    width = refs[0].shape[1]
    total = refs[n + 1][...] if has_base else None
    for k in range(n):
        start = pl.multiple_of((at_ref[0] ^ order[k]) * width, width)
        term = times(refs[k], grads_ref[:, pl.ds(start, width)])
        total = term if total is None else total + term
    out_ref[...] = total


def score_dot(pieces, order, first, grads, base=None, after=()):
    n = len(pieces)
    rows, width = pieces[0].shape
    operands = [*pieces, grads] + ([] if base is None else [base])
    return pl.pallas_call(
        functools.partial(score_kernel, order, base is not None),
        out_shape=jax.ShapeDtypeStruct((rows, grads.shape[0]), jnp.float32),
        in_specs=[SMEM] + [VMEM] * len(operands) + [ANY] * len(after),
        out_specs=VMEM,
        compiler_params=limit(8),
        cost_estimate=pl.CostEstimate(
            flops=2 * n * rows * width * grads.shape[0],
            bytes_accessed=2 * n * width * grads.shape[0],
            transcendentals=0,
        ),
    )(scalar(first), *operands, *after)


def pick_kernel(at_ref, a_ref, b_ref, *refs):
    out_ref = refs[-1]

    @pl.when(at_ref[0] == 1)
    def _():
        out_ref[...] = a_ref[...]

    @pl.when(at_ref[0] != 1)
    def _():
        out_ref[...] = b_ref[...]


def pick(condition, a, b, after=()):
    return pl.pallas_call(
        pick_kernel,
        out_shape=jax.ShapeDtypeStruct(a.shape, a.dtype),
        in_specs=[SMEM] + [VMEM] * 2 + [ANY] * len(after),
        out_specs=VMEM,
        compiler_params=limit(2),
        cost_estimate=pl.CostEstimate(flops=0, bytes_accessed=2 * a.size * 2, transcendentals=0),
    )(scalar(condition), a, b, *after)


def per_device_quad(nz, nx, ny, queries, inverse_fisher, stored_grads):
    nex = nz * nx
    near = nz // 2
    nq = queries.shape[0]
    y, e, d = (lax.axis_index(a) for a in AXES)
    z = e // nx
    x = e % nx
    u = jnp.where(d == 0, z, nz - 1 - z)
    owner = u < near

    def move(value, target):
        pairs = []
        for sy in range(ny):
            for sz in range(nz):
                for sx in range(nx):
                    for sd in range(2):
                        to = target(sy, sz, sx, sd)
                        if to is not None:
                            ty, tz, tx, td = to
                            pairs.append(((sy * nex + sz * nx + sx) * 2 + sd, (ty * nex + tz * nx + tx) * 2 + td))
        return lax.ppermute(value, AXES, pairs)

    def along_z(value, hops):
        def target(sy, sz, sx, sd):
            su = sz if sd == 0 else nz - 1 - sz
            if su not in hops:
                return None
            tu = hops[su]
            return sy, tu if sd == 0 else nz - 1 - tu, sx, sd

        return move(value, target)

    def swap_x(value):
        return move(value, lambda sy, sz, sx, sd: (sy, sz, 1 - sx, sd))

    def swap_y(value):
        return move(value, lambda sy, sz, sx, sd: (1 - sy, sz, sx, sd))

    def to_owner(value):
        def target(sy, sz, sx, sd):
            su = sz if sd == 0 else nz - 1 - sz
            return None if su < near else (sy, sz, sx, 1 - sd)

        return move(value, target)

    def gather(own, after=((), ())):
        first = pick(owner, own, along_z(own, {0: 2, 1: 3}), after[0])
        second = pick(owner, along_z(own, {0: 1, 1: 0}), along_z(own, {0: 3, 1: 2}), after[1])
        return [first, second, swap_x(first), swap_x(second)]

    plane = jnp.where(d == 0, u % 2, nz - 1 - u % 2)
    column = plane * nx + x - d * (nex // 2)

    other_grads = swap_y(stored_grads)

    own = cut_rows(queries, nq // ny, y)
    blocks = load(inverse_fisher, column, 2, own.shape[1])
    pieces = gather(own, (blocks[:1], ()))
    total, block = fisher_first(pieces[:2], blocks, column, inverse_fisher)
    total = fisher_last(pieces[2:], block, total, column, inverse_fisher)
    panel = (total + to_owner(total)).astype(jnp.bfloat16)

    pieces = gather(panel, ((), (other_grads,)))
    other, mine = (score_dot(pieces[:3], ORDER[:3], column, g) for g in (other_grads, stored_grads))
    other = score_dot(pieces[3:], ORDER[3:], column, other_grads, other)
    mine = score_dot(pieces[3:], ORDER[3:], column, stored_grads, mine, (other,))
    other = move(other, lambda sy, sz, sx, sd: (1 - sy, sz, sx, sy) if sd != sy else None) + move(
        other, lambda sy, sz, sx, sd: (1 - sy, sz, sx, sy) if sd == sy else None
    )
    mine = mine + move(mine, lambda sy, sz, sx, sd: (sy, sz, sx, sy) if sd != sy else None)
    return jnp.where(d == y, mine, other)


def solution(mesh):
    coords = [getattr(device, "coords", None) for device in mesh.devices.flat]
    nx = 2 if None in coords else len({c[0] for c in coords})
    nz = mesh.shape["ex"] // nx
    ny = mesh.shape["grp"]
    if (nz, nx, ny) == (4, 2, 2):
        body = functools.partial(per_device_quad, nz, nx, ny)
    else:
        body = per_device_any
    return jax.shard_map(
        body,
        mesh=mesh,
        in_specs=(P(None, "ex"), P("ex", "dim"), P(("grp", "ex"), "dim")),
        out_specs=P("dim", ("grp", "ex")),
        check_vma=False,
    )
```

```python
import functools

import jax
import jax.numpy as jnp
from jax import lax
from jax.experimental import pallas as pl
from jax.experimental.pallas import tpu as pltpu
from jax.sharding import PartitionSpec as P

AXES = ("grp", "ex", "dim")
NT = (((1,), (1,)), ((), ()))
VMEM = pl.BlockSpec(memory_space=pltpu.VMEM)
SMEM = pl.BlockSpec(memory_space=pltpu.SMEM)
HBM = pl.BlockSpec(memory_space=pltpu.HBM)
ANY = pl.BlockSpec(memory_space=pl.ANY)


def limit(mib):
    return pltpu.CompilerParams(vmem_limit_bytes=mib * 1024 * 1024)


def per_device_any(queries, inverse_fisher, stored_grads):
    term_block = jnp.dot(queries, inverse_fisher, preferred_element_type=jnp.float32)
    own_panel = lax.psum_scatter(term_block, "ex", scatter_dimension=1, tiled=True).astype(
        jnp.bfloat16
    )
    partial_scores = lax.dot_general(
        lax.all_gather(own_panel, "ex", axis=1, tiled=True),
        stored_grads,
        NT,
        preferred_element_type=jnp.float32,
    )
    return lax.psum_scatter(partial_scores, "dim", scatter_dimension=0, tiled=True)


def scalar(value):
    return jnp.asarray(value, jnp.int32).reshape(1)


ORDER = (0, 2, 1, 3)


def start_blocks(fisher_ref, at, held_ref, sem):
    steps = sem.shape[0]
    rows, width = held_ref.shape
    step = rows // steps
    columns = pl.ds(pl.multiple_of(at * width, width), width)
    copies = []
    for i in range(steps):
        block = pl.ds(i * step, step)
        copies.append(pltpu.make_async_copy(fisher_ref.at[block, columns], held_ref.at[block, :], sem.at[i]))
        copies[-1].start()
    return copies


def times(chunk_ref, fisher):
    return lax.dot_general(chunk_ref[...], fisher, NT, preferred_element_type=jnp.float32)


def load_kernel(at_ref, fisher_ref, *refs):
    copies = []
    for k, held_ref in enumerate(refs[:-1]):
        copies += start_blocks(fisher_ref, at_ref[0] ^ ORDER[k], held_ref, refs[-1].at[k])
    for copy in copies:
        copy.wait()


def load(fisher, first, n, width, steps=4):
    return pl.pallas_call(
        load_kernel,
        out_shape=[jax.ShapeDtypeStruct((fisher.shape[0], width), fisher.dtype)] * n,
        in_specs=[SMEM, HBM],
        out_specs=[VMEM] * n,
        scratch_shapes=[pltpu.SemaphoreType.DMA((n, steps))],
        compiler_params=limit(34),
        cost_estimate=pl.CostEstimate(
            flops=0, bytes_accessed=2 * n * width * fisher.shape[0], transcendentals=0
        ),
    )(scalar(first), fisher)


def fisher_first_kernel(at_ref, chunk, block, fisher_ref, out_ref, next_ref, sem):
    steps = sem.shape[0]
    step = block.shape[0] // steps
    copies = start_blocks(fisher_ref, at_ref[0] ^ ORDER[2], next_ref, sem)

    @pl.loop(0, steps)
    def _(i):
        rows = pl.ds(pl.multiple_of(i * step, step), step)
        out_ref[:, rows] = times(chunk, block[rows, :])

    for copy in copies:
        copy.wait()


def fisher_first(chunk, block, first, fisher, steps=4):
    nq, width = chunk.shape
    rows = fisher.shape[0]
    return pl.pallas_call(
        fisher_first_kernel,
        out_shape=[
            jax.ShapeDtypeStruct((nq, rows), jnp.float32),
            jax.ShapeDtypeStruct((rows, width), fisher.dtype),
        ],
        in_specs=[SMEM] + [VMEM] * 2 + [HBM],
        out_specs=[VMEM] * 2,
        scratch_shapes=[pltpu.SemaphoreType.DMA((steps,))],
        compiler_params=limit(8),
        cost_estimate=pl.CostEstimate(
            flops=2 * nq * width * rows, bytes_accessed=2 * width * rows, transcendentals=0
        ),
    )(scalar(first), chunk, block, fisher)


def fisher_last_kernel(at_ref, chunk0, chunk1, chunk2, block0, block1, base_ref, fisher_ref, out_ref, held, sem):
    steps = sem.shape[0]
    step = held.shape[0] // steps
    copies = start_blocks(fisher_ref, at_ref[0] ^ ORDER[3], held, sem)

    @pl.loop(0, steps)
    def _(i):
        rows = pl.ds(pl.multiple_of(i * step, step), step)
        out_ref[:, rows] = base_ref[:, rows] + times(chunk0, block0[rows, :])

    @pl.loop(0, steps)
    def _(i):
        rows = pl.ds(pl.multiple_of(i * step, step), step)
        out_ref[:, rows] += times(chunk1, block1[rows, :])

    for i in range(steps):
        rows = slice(i * step, (i + 1) * step)
        copies[i].wait()
        out_ref[:, rows] += times(chunk2, held[rows, :])


def fisher_last(chunks, blocks, base, first, fisher, steps=4):
    nq, width = chunks[0].shape
    rows = fisher.shape[0]
    return pl.pallas_call(
        fisher_last_kernel,
        out_shape=jax.ShapeDtypeStruct((nq, rows), jnp.float32),
        in_specs=[SMEM] + [VMEM] * 6 + [HBM],
        out_specs=VMEM,
        scratch_shapes=[pltpu.VMEM((rows, width), fisher.dtype), pltpu.SemaphoreType.DMA((steps,))],
        compiler_params=limit(16),
        cost_estimate=pl.CostEstimate(
            flops=6 * nq * width * rows, bytes_accessed=2 * width * rows, transcendentals=0
        ),
    )(scalar(first), *chunks, *blocks, base, fisher)


def score_kernel(order, has_base, at_ref, *refs):
    n = len(order)
    grads_ref, out_ref = refs[n], refs[-1]
    width = refs[0].shape[1]
    total = refs[n + 1][...] if has_base else None
    for k in range(n):
        start = pl.multiple_of((at_ref[0] ^ order[k]) * width, width)
        term = times(refs[k], grads_ref[:, pl.ds(start, width)])
        total = term if total is None else total + term
    out_ref[...] = total


def score_dot(pieces, order, first, grads, base=None, after=()):
    n = len(pieces)
    rows, width = pieces[0].shape
    operands = [*pieces, grads] + ([] if base is None else [base])
    return pl.pallas_call(
        functools.partial(score_kernel, order, base is not None),
        out_shape=jax.ShapeDtypeStruct((rows, grads.shape[0]), jnp.float32),
        in_specs=[SMEM] + [VMEM] * len(operands) + [ANY] * len(after),
        out_specs=VMEM,
        compiler_params=limit(8),
        cost_estimate=pl.CostEstimate(
            flops=2 * n * rows * width * grads.shape[0],
            bytes_accessed=2 * n * width * grads.shape[0],
            transcendentals=0,
        ),
    )(scalar(first), *operands, *after)


def pick_kernel(at_ref, a_ref, b_ref, *refs):
    out_ref = refs[-1]

    @pl.when(at_ref[0] == 1)
    def _():
        out_ref[...] = a_ref[...]

    @pl.when(at_ref[0] != 1)
    def _():
        out_ref[...] = b_ref[...]


def pick(condition, a, b, after=()):
    return pl.pallas_call(
        pick_kernel,
        out_shape=jax.ShapeDtypeStruct(a.shape, a.dtype),
        in_specs=[SMEM] + [VMEM] * 2 + [ANY] * len(after),
        out_specs=VMEM,
        compiler_params=limit(2),
        cost_estimate=pl.CostEstimate(flops=0, bytes_accessed=2 * a.size * 2, transcendentals=0),
    )(scalar(condition), a, b, *after)


def per_device_quad(nz, nx, ny, queries, inverse_fisher, stored_grads):
    nex = nz * nx
    near = nz // 2
    nq = queries.shape[0]
    y, e, d = (lax.axis_index(a) for a in AXES)
    z = e // nx
    x = e % nx
    u = jnp.where(d == 0, z, nz - 1 - z)
    owner = u < near

    def move(value, target):
        pairs = []
        for sy in range(ny):
            for sz in range(nz):
                for sx in range(nx):
                    for sd in range(2):
                        to = target(sy, sz, sx, sd)
                        if to is not None:
                            ty, tz, tx, td = to
                            pairs.append(((sy * nex + sz * nx + sx) * 2 + sd, (ty * nex + tz * nx + tx) * 2 + td))
        return lax.ppermute(value, AXES, pairs)

    def along_z(value, hops, flip=False):
        def target(sy, sz, sx, sd):
            su = sz if sd == 0 else nz - 1 - sz
            if su not in hops:
                return None
            tu = hops[su]
            return sy, tu if sd == 0 else nz - 1 - tu, 1 - sx if flip else sx, sd

        return move(value, target)

    def swap_x(value):
        return move(value, lambda sy, sz, sx, sd: (sy, sz, 1 - sx, sd))

    def swap_y(value):
        return move(value, lambda sy, sz, sx, sd: (1 - sy, sz, sx, sd))

    def to_owner(value):
        def target(sy, sz, sx, sd):
            su = sz if sd == 0 else nz - 1 - sz
            return None if su < near else (sy, sz, sx, 1 - sd)

        return move(value, target)

    def gather(own, after=()):
        first = pick(owner, own, along_z(own, {0: 2, 1: 3}), after)
        pairs = {0: 1, 1: 0, 2: 3, 3: 2}
        return [first, along_z(first, pairs), swap_x(first), along_z(first, pairs, True)]

    plane = jnp.where(d == 0, u % 2, nz - 1 - u % 2)
    column = plane * nx + x - d * (nex // 2)

    other_grads = swap_y(stored_grads)

    rows = nq // ny
    own = lax.optimization_barrier(lax.dynamic_slice_in_dim(queries, y * rows, rows, axis=0))
    blocks = load(inverse_fisher, column, 2, own.shape[1])
    pieces = gather(own, blocks[:1])
    total, block = fisher_first(pieces[0], blocks[0], column, inverse_fisher)
    total = fisher_last(pieces[1:], (blocks[1], block), total, column, inverse_fisher)
    panel = (total + to_owner(total)).astype(jnp.bfloat16)

    pieces = gather(panel)
    other, mine = (score_dot(pieces[:3], ORDER[:3], column, g) for g in (other_grads, stored_grads))
    other = score_dot(pieces[3:], ORDER[3:], column, other_grads, other)
    mine = score_dot(pieces[3:], ORDER[3:], column, stored_grads, mine, (other,))

    other = swap_y(other)
    keep = jnp.where(d == y, mine, other)
    give = jnp.where(d == y, other, mine)
    return keep + move(give, lambda sy, sz, sx, sd: (sy, sz, sx, 1 - sd))


def solution(mesh):
    coords = [getattr(device, "coords", None) for device in mesh.devices.flat]
    nx = 2 if None in coords else len({c[0] for c in coords})
    nz = mesh.shape["ex"] // nx
    ny = mesh.shape["grp"]
    if (nz, nx, ny) == (4, 2, 2):
        body = functools.partial(per_device_quad, nz, nx, ny)
    else:
        body = per_device_any
    return jax.shard_map(
        body,
        mesh=mesh,
        in_specs=(P(None, "ex"), P("ex", "dim"), P(("grp", "ex"), "dim")),
        out_specs=P("dim", ("grp", "ex")),
        check_vma=False,
    )
```

```python
import functools

import jax
import jax.numpy as jnp
from jax import lax
from jax.experimental import pallas as pl
from jax.experimental.pallas import tpu as pltpu
from jax.sharding import PartitionSpec as P

AXES = ("grp", "ex", "dim")
NT = (((1,), (1,)), ((), ()))
VMEM = pl.BlockSpec(memory_space=pltpu.VMEM)
SMEM = pl.BlockSpec(memory_space=pltpu.SMEM)
HBM = pl.BlockSpec(memory_space=pltpu.HBM)
ANY = pl.BlockSpec(memory_space=pl.ANY)


def limit(mib):
    return pltpu.CompilerParams(vmem_limit_bytes=mib * 1024 * 1024)


def per_device_any(queries, inverse_fisher, stored_grads):
    term_block = jnp.dot(queries, inverse_fisher, preferred_element_type=jnp.float32)
    own_panel = lax.psum_scatter(term_block, "ex", scatter_dimension=1, tiled=True).astype(
        jnp.bfloat16
    )
    partial_scores = lax.dot_general(
        lax.all_gather(own_panel, "ex", axis=1, tiled=True),
        stored_grads,
        NT,
        preferred_element_type=jnp.float32,
    )
    return lax.psum_scatter(partial_scores, "dim", scatter_dimension=0, tiled=True)


def scalar(value):
    return jnp.asarray(value, jnp.int32).reshape(1)


ORDER = (0, 2, 1, 3)


def start_half(fisher_ref, block, half, held_ref, sem):
    steps = sem.shape[0]
    rows, width = held_ref.shape
    step = rows // steps
    columns = pl.ds(pl.multiple_of(block * width, width), width)
    copies = []
    for i in range(steps):
        copies.append(
            pltpu.make_async_copy(
                fisher_ref.at[pl.ds(half * rows + i * step, step), columns],
                held_ref.at[pl.ds(i * step, step), :],
                sem.at[i],
            )
        )
        copies[-1].start()
    return copies


def times(chunk_ref, fisher):
    return lax.dot_general(chunk_ref[...], fisher, NT, preferred_element_type=jnp.float32)


def fisher_kernel(n_in, has_base, fetch, step, *refs):
    if fetch:
        at_ref, fisher_ref, *refs = refs
    chunk_ref, halves = (refs[0], refs[1:3]) if n_in else (None, ())
    base_ref = refs[3] if has_base else None
    outs, sem = refs[n_in + has_base : -1], refs[-1]
    held = outs[1:] if n_in else outs
    copies = []
    for k, (piece, half) in enumerate(fetch):
        copies += start_half(fisher_ref, at_ref[0] ^ ORDER[piece], half, held[k], sem.at[k])
    for h, half_ref in enumerate(halves):
        rows = half_ref.shape[0]

        @pl.loop(0, rows // step)
        def _(i):
            columns = pl.ds(pl.multiple_of(h * rows + i * step, step), step)
            term = times(chunk_ref, half_ref[pl.ds(pl.multiple_of(i * step, step), step), :])
            outs[0][:, columns] = term + base_ref[:, columns] if has_base else term

    for copy in copies:
        copy.wait()


def fisher_step(fisher, first, width, fetch, chunk=None, halves=(), base=None, step=512):
    rows = fisher.shape[0]
    ins = [] if chunk is None else [chunk, *halves]
    has_base = base is not None
    held = jax.ShapeDtypeStruct((rows // 2, width), fisher.dtype)
    out_shape = [] if chunk is None else [jax.ShapeDtypeStruct((chunk.shape[0], rows), jnp.float32)]
    out_shape += [held] * len(fetch)
    return pl.pallas_call(
        functools.partial(fisher_kernel, len(ins), has_base, fetch, step),
        out_shape=out_shape,
        in_specs=[SMEM, HBM][: 2 * bool(fetch)] + [VMEM] * (len(ins) + has_base),
        out_specs=[VMEM] * len(out_shape),
        scratch_shapes=[pltpu.SemaphoreType.DMA((max(len(fetch), 1), 2))],
        compiler_params=limit(34 if chunk is None else 20),
        cost_estimate=pl.CostEstimate(
            flops=0 if chunk is None else 2 * chunk.shape[0] * width * rows,
            bytes_accessed=width * rows * len(fetch),
            transcendentals=0,
        ),
    )(*((scalar(first), fisher) if fetch else ()), *ins, *([base] if has_base else []))


def score_kernel(order, n_grads, has_base, at_ref, *refs):
    n = len(order)
    width = refs[0].shape[1]
    for g in range(n_grads):
        grads_ref, out_ref = refs[n + g], refs[-n_grads + g]
        total = refs[n + n_grads + g][...] if has_base else None
        for k in range(n):
            start = pl.multiple_of((at_ref[0] ^ order[k]) * width, width)
            term = times(refs[k], grads_ref[:, pl.ds(start, width)])
            total = term if total is None else total + term
        out_ref[...] = total


def score_dot(pieces, order, first, grads, base=(), after=()):
    n = len(pieces)
    rows, width = pieces[0].shape
    operands = [*pieces, *grads, *base]
    return pl.pallas_call(
        functools.partial(score_kernel, order, len(grads), len(base) > 0),
        out_shape=[jax.ShapeDtypeStruct((rows, g.shape[0]), jnp.float32) for g in grads],
        in_specs=[SMEM] + [VMEM] * len(operands) + [ANY] * len(after),
        out_specs=[VMEM] * len(grads),
        compiler_params=limit(8),
        cost_estimate=pl.CostEstimate(
            flops=2 * n * rows * width * grads[0].shape[0] * len(grads),
            bytes_accessed=2 * n * width * grads[0].shape[0] * len(grads),
            transcendentals=0,
        ),
    )(scalar(first), *operands, *after)


def pick_kernel(at_ref, a_ref, b_ref, *refs):
    out_ref = refs[-1]

    @pl.when(at_ref[0] == 1)
    def _():
        out_ref[...] = a_ref[...]

    @pl.when(at_ref[0] != 1)
    def _():
        out_ref[...] = b_ref[...]


def pick(condition, a, b, after=()):
    return pl.pallas_call(
        pick_kernel,
        out_shape=jax.ShapeDtypeStruct(a.shape, a.dtype),
        in_specs=[SMEM] + [VMEM] * 2 + [ANY] * len(after),
        out_specs=VMEM,
        compiler_params=limit(2),
        cost_estimate=pl.CostEstimate(flops=0, bytes_accessed=2 * a.size * 2, transcendentals=0),
    )(scalar(condition), a, b, *after)


def per_device_quad(nz, nx, ny, queries, inverse_fisher, stored_grads):
    nex = nz * nx
    near = nz // 2
    nq = queries.shape[0]
    y, e, d = (lax.axis_index(a) for a in AXES)
    z = e // nx
    x = e % nx
    u = jnp.where(d == 0, z, nz - 1 - z)
    owner = u < near

    def move(value, target):
        pairs = []
        for sy in range(ny):
            for sz in range(nz):
                for sx in range(nx):
                    for sd in range(2):
                        to = target(sy, sz, sx, sd)
                        if to is not None:
                            ty, tz, tx, td = to
                            pairs.append(((sy * nex + sz * nx + sx) * 2 + sd, (ty * nex + tz * nx + tx) * 2 + td))
        return lax.ppermute(value, AXES, pairs)

    def along_z(value, hops, flip=False):
        def target(sy, sz, sx, sd):
            su = sz if sd == 0 else nz - 1 - sz
            if su not in hops:
                return None
            tu = hops[su]
            return sy, tu if sd == 0 else nz - 1 - tu, 1 - sx if flip else sx, sd

        return move(value, target)

    def swap_y(value):
        return move(value, lambda sy, sz, sx, sd: (1 - sy, sz, sx, sd))

    def to_owner(value):
        def target(sy, sz, sx, sd):
            su = sz if sd == 0 else nz - 1 - sz
            return None if su < near else (sy, sz, sx, 1 - sd)

        return move(value, target)

    def gather(own, after=()):
        far = along_z(own, {0: 2, 1: 3})
        steps = (((0, 1), (1, 0)), False), (((0, 0), (1, 1)), True), (((0, 1), (1, 0)), True)
        near = [along_z(own, dict(hops), flip) for hops, flip in steps]
        first = pick(owner, own, far, after)
        gate = pick(owner, first, first, near)

        def piece(k, after=()):
            if k == 0:
                return first
            hops, flip = steps[k - 1]
            hops = {2 + s: 2 + t for s, t in hops}
            return pick(owner, near[k - 1], along_z(gate, hops, flip), after)

        return piece

    plane = jnp.where(d == 0, u % 2, nz - 1 - u % 2)
    column = plane * nx + x - d * (nex // 2)

    other_grads = swap_y(stored_grads)

    rows = nq // ny
    own = lax.optimization_barrier(lax.dynamic_slice_in_dim(queries, y * rows, rows, axis=0))
    step = functools.partial(fisher_step, inverse_fisher, column, own.shape[1])
    a0, a1, b0 = step(((0, 0), (0, 1), (1, 0)))
    piece = gather(own, (a0,))
    total, b1, c0 = step(((1, 1), (2, 0)), piece(0), (a0, a1))
    total, c1, d0 = step(((2, 1), (3, 0)), piece(1), (b0, b1), total)
    total, d1 = step(((3, 1),), piece(2, (total,)), (c0, c1), total)
    (total,) = step((), piece(3, (total,)), (d0, d1), total)
    panel = (total + to_owner(total)).astype(jnp.bfloat16)

    piece = gather(panel)
    pieces = [piece(k) for k in range(3)]
    other, mine = score_dot(pieces, ORDER[:3], column, (other_grads, stored_grads))
    pieces = [piece(3, (other,))]
    (other,) = score_dot(pieces, ORDER[3:], column, (other_grads,), (other,))
    (mine,) = score_dot(pieces, ORDER[3:], column, (stored_grads,), (mine,), (other,))

    other = swap_y(other)
    keep = jnp.where(d == y, mine, other)
    give = jnp.where(d == y, other, mine)
    return keep + move(give, lambda sy, sz, sx, sd: (sy, sz, sx, 1 - sd))


def solution(mesh):
    coords = [getattr(device, "coords", None) for device in mesh.devices.flat]
    nx = 2 if None in coords else len({c[0] for c in coords})
    nz = mesh.shape["ex"] // nx
    ny = mesh.shape["grp"]
    if (nz, nx, ny) == (4, 2, 2):
        body = functools.partial(per_device_quad, nz, nx, ny)
    else:
        body = per_device_any
    return jax.shard_map(
        body,
        mesh=mesh,
        in_specs=(P(None, "ex"), P("ex", "dim"), P(("grp", "ex"), "dim")),
        out_specs=P("dim", ("grp", "ex")),
        check_vma=False,
    )
```

```python
import functools

import jax
import jax.numpy as jnp
from jax import lax
from jax.experimental import pallas as pl
from jax.experimental.pallas import tpu as pltpu
from jax.sharding import PartitionSpec as P

AXES = ("grp", "ex", "dim")
NT = (((1,), (1,)), ((), ()))
VMEM = pl.BlockSpec(memory_space=pltpu.VMEM)
SMEM = pl.BlockSpec(memory_space=pltpu.SMEM)
HBM = pl.BlockSpec(memory_space=pltpu.HBM)
ANY = pl.BlockSpec(memory_space=pl.ANY)


def limit(mib):
    return pltpu.CompilerParams(vmem_limit_bytes=mib * 1024 * 1024)


def per_device_any(queries, inverse_fisher, stored_grads):
    term_block = jnp.dot(queries, inverse_fisher, preferred_element_type=jnp.float32)
    own_panel = lax.psum_scatter(term_block, "ex", scatter_dimension=1, tiled=True).astype(
        jnp.bfloat16
    )
    partial_scores = lax.dot_general(
        lax.all_gather(own_panel, "ex", axis=1, tiled=True),
        stored_grads,
        NT,
        preferred_element_type=jnp.float32,
    )
    return lax.psum_scatter(partial_scores, "dim", scatter_dimension=0, tiled=True)


def scalar(value):
    return jnp.asarray(value, jnp.int32).reshape(1)


ORDER = (0, 2, 1, 3)


def start_half(fisher_ref, block, half, held_ref, sem):
    steps = sem.shape[0]
    rows, width = held_ref.shape
    step = rows // steps
    columns = pl.ds(pl.multiple_of(block * width, width), width)
    copies = []
    for i in range(steps):
        copies.append(
            pltpu.make_async_copy(
                fisher_ref.at[pl.ds(half * rows + i * step, step), columns],
                held_ref.at[pl.ds(i * step, step), :],
                sem.at[i],
            )
        )
        copies[-1].start()
    return copies


def times(chunk_ref, fisher):
    return lax.dot_general(chunk_ref[...], fisher, NT, preferred_element_type=jnp.float32)


def fisher_kernel(n_in, has_base, fetch, step, *refs):
    if fetch:
        at_ref, fisher_ref, *refs = refs
    chunk_ref, halves = (refs[0], refs[1:3]) if n_in else (None, ())
    base_ref = refs[3] if has_base else None
    outs, sem = refs[n_in + has_base : -1], refs[-1]
    held = outs[1:] if n_in else outs
    copies = []
    for k, (piece, half) in enumerate(fetch):
        copies += start_half(fisher_ref, at_ref[0] ^ ORDER[piece], half, held[k], sem.at[k])
    for h, half_ref in enumerate(halves):
        rows = half_ref.shape[0]

        @pl.loop(0, rows // step)
        def _(i):
            columns = pl.ds(pl.multiple_of(h * rows + i * step, step), step)
            term = times(chunk_ref, half_ref[pl.ds(pl.multiple_of(i * step, step), step), :])
            outs[0][:, columns] = term + base_ref[:, columns] if has_base else term

    for copy in copies:
        copy.wait()


def fisher_step(fisher, first, width, fetch, chunk=None, halves=(), base=None, step=512):
    rows = fisher.shape[0]
    ins = [] if chunk is None else [chunk, *halves]
    has_base = base is not None
    held = jax.ShapeDtypeStruct((rows // 2, width), fisher.dtype)
    out_shape = [] if chunk is None else [jax.ShapeDtypeStruct((chunk.shape[0], rows), jnp.float32)]
    out_shape += [held] * len(fetch)
    return pl.pallas_call(
        functools.partial(fisher_kernel, len(ins), has_base, fetch, step),
        out_shape=out_shape,
        in_specs=[SMEM, HBM][: 2 * bool(fetch)] + [VMEM] * (len(ins) + has_base),
        out_specs=[VMEM] * len(out_shape),
        scratch_shapes=[pltpu.SemaphoreType.DMA((max(len(fetch), 1), 2))],
        compiler_params=limit(34 if chunk is None else 20),
        cost_estimate=pl.CostEstimate(
            flops=0 if chunk is None else 2 * chunk.shape[0] * width * rows,
            bytes_accessed=width * rows * (len(fetch) + 2 * bool(ins)),
            transcendentals=0,
        ),
    )(*((scalar(first), fisher) if fetch else ()), *ins, *([base] if has_base else []))


def score_kernel(order, n_grads, has_base, at_ref, *refs):
    n = len(order)
    width = refs[0].shape[1]
    for g in range(n_grads):
        grads_ref, out_ref = refs[n + g], refs[-n_grads + g]
        total = refs[n + n_grads + g][...] if has_base else None
        for k in range(n):
            start = pl.multiple_of((at_ref[0] ^ order[k]) * width, width)
            term = times(refs[k], grads_ref[:, pl.ds(start, width)])
            total = term if total is None else total + term
        out_ref[...] = total


def score_dot(pieces, order, first, grads, base=(), after=()):
    n = len(pieces)
    rows, width = pieces[0].shape
    operands = [*pieces, *grads, *base]
    return pl.pallas_call(
        functools.partial(score_kernel, order, len(grads), len(base) > 0),
        out_shape=[jax.ShapeDtypeStruct((rows, g.shape[0]), jnp.float32) for g in grads],
        in_specs=[SMEM] + [VMEM] * len(operands) + [ANY] * len(after),
        out_specs=[VMEM] * len(grads),
        compiler_params=limit(8),
        cost_estimate=pl.CostEstimate(
            flops=2 * n * rows * width * grads[0].shape[0] * len(grads),
            bytes_accessed=2 * n * width * grads[0].shape[0] * len(grads),
            transcendentals=0,
        ),
    )(scalar(first), *operands, *after)


def pick_kernel(at_ref, a_ref, b_ref, *refs):
    out_ref = refs[-1]

    @pl.when(at_ref[0] == 1)
    def _():
        out_ref[...] = a_ref[...]

    @pl.when(at_ref[0] != 1)
    def _():
        out_ref[...] = b_ref[...]


def pick(condition, a, b, after=()):
    return pl.pallas_call(
        pick_kernel,
        out_shape=jax.ShapeDtypeStruct(a.shape, a.dtype),
        in_specs=[SMEM] + [VMEM] * 2 + [ANY] * len(after),
        out_specs=VMEM,
        compiler_params=limit(2),
        cost_estimate=pl.CostEstimate(flops=0, bytes_accessed=2 * a.size * 2, transcendentals=0),
    )(scalar(condition), a, b, *after)


def per_device_quad(nz, nx, ny, queries, inverse_fisher, stored_grads):
    nex = nz * nx
    near = nz // 2
    nq = queries.shape[0]
    y, e, d = (lax.axis_index(a) for a in AXES)
    z = e // nx
    x = e % nx
    u = jnp.where(d == 0, z, nz - 1 - z)
    owner = u < near

    def move(value, target):
        pairs = []
        for sy in range(ny):
            for sz in range(nz):
                for sx in range(nx):
                    for sd in range(2):
                        to = target(sy, sz, sx, sd)
                        if to is not None:
                            ty, tz, tx, td = to
                            pairs.append(((sy * nex + sz * nx + sx) * 2 + sd, (ty * nex + tz * nx + tx) * 2 + td))
        return lax.ppermute(value, AXES, pairs)

    def along_z(value, hops, flip=False):
        def target(sy, sz, sx, sd):
            su = sz if sd == 0 else nz - 1 - sz
            if su not in hops:
                return None
            tu = hops[su]
            return sy, tu if sd == 0 else nz - 1 - tu, 1 - sx if flip else sx, sd

        return move(value, target)

    def swap_y(value):
        return move(value, lambda sy, sz, sx, sd: (1 - sy, sz, sx, sd))

    def swap_core(value):
        return move(value, lambda sy, sz, sx, sd: (sy, sz, sx, 1 - sd))

    def gather(own, after=()):
        def start(sy, sz, sx, sd):
            su = sz if sd == 0 else nz - 1 - sz
            if su < near:
                return sy, sz + 2 if sd == 0 else sz - 2, sx, sd
            return sy, sz ^ 1, 1 - sx, 1 - sd

        came = move(own, start)
        first = pick(owner, own, came, after)
        pairs = {0: 1, 1: 0, 2: 3, 3: 2}
        beside = along_z(first, pairs)
        across = along_z(first, {0: 0, 1: 1, 2: 2, 3: 3}, True)
        diagonal = along_z(first, {2: 3, 3: 2}, True)
        return lambda *after: [first, beside, across, pick(owner, came, diagonal, after)]

    plane = jnp.where(d == 0, u % 2, nz - 1 - u % 2)
    column = plane * nx + x - d * (nex // 2)

    other_grads = swap_y(stored_grads)

    rows = nq // ny
    own = lax.optimization_barrier(lax.dynamic_slice_in_dim(queries, y * rows, rows, axis=0))
    step = functools.partial(fisher_step, inverse_fisher, column, own.shape[1])
    a0, a1, b0, b1 = step(((0, 0), (0, 1), (1, 0), (1, 1)))
    gathered = gather(own, (a0,))
    q0, q1, q2, _ = gathered()
    total, c0, c1 = step(((2, 0), (2, 1)), q0, (a0, a1))
    total, d0 = step(((3, 0),), q1, (b0, b1), total)
    total, d1 = step(((3, 1),), q2, (c0, c1), total)
    (total,) = step((), gathered(total)[3], (d0, d1), total)
    panel = (total + swap_core(total)).astype(jnp.bfloat16)

    grads = (other_grads, stored_grads)
    gathered = gather(panel)
    base = score_dot(gathered()[:3], ORDER[:3], column, grads)
    other, mine = score_dot(gathered(base[0])[3:], ORDER[3:], column, grads, base)

    other = swap_y(other)
    keep = jnp.where(d == y, mine, other)
    give = jnp.where(d == y, other, mine)
    return keep + swap_core(give)


def solution(mesh):
    coords = [getattr(device, "coords", None) for device in mesh.devices.flat]
    nx = 2 if None in coords else len({c[0] for c in coords})
    nz = mesh.shape["ex"] // nx
    ny = mesh.shape["grp"]
    if (nz, nx, ny) == (4, 2, 2):
        body = functools.partial(per_device_quad, nz, nx, ny)
    else:
        body = per_device_any
    return jax.shard_map(
        body,
        mesh=mesh,
        in_specs=(P(None, "ex"), P("ex", "dim"), P(("grp", "ex"), "dim")),
        out_specs=P("dim", ("grp", "ex")),
        check_vma=False,
    )
```

```python
import functools

import jax
import jax.numpy as jnp
from jax import lax
from jax.experimental import pallas as pl
from jax.experimental.pallas import tpu as pltpu
from jax.sharding import PartitionSpec as P

AXES = ("grp", "ex", "dim")
NT = (((1,), (1,)), ((), ()))
VMEM = pl.BlockSpec(memory_space=pltpu.VMEM)
SMEM = pl.BlockSpec(memory_space=pltpu.SMEM)
HBM = pl.BlockSpec(memory_space=pltpu.HBM)
ANY = pl.BlockSpec(memory_space=pl.ANY)


def limit(mib):
    return pltpu.CompilerParams(vmem_limit_bytes=mib * 1024 * 1024)


def per_device_any(queries, inverse_fisher, stored_grads):
    term_block = jnp.dot(queries, inverse_fisher, preferred_element_type=jnp.float32)
    own_panel = lax.psum_scatter(term_block, "ex", scatter_dimension=1, tiled=True).astype(
        jnp.bfloat16
    )
    partial_scores = lax.dot_general(
        lax.all_gather(own_panel, "ex", axis=1, tiled=True),
        stored_grads,
        NT,
        preferred_element_type=jnp.float32,
    )
    return lax.psum_scatter(partial_scores, "dim", scatter_dimension=0, tiled=True)


def scalar(value):
    return jnp.asarray(value, jnp.int32).reshape(1)


ORDER = (0, 2, 1, 3)


def start_half(fisher_ref, block, half, held_ref, sem):
    steps = sem.shape[0]
    rows, width = held_ref.shape
    step = rows // steps
    columns = pl.ds(pl.multiple_of(block * width, width), width)
    copies = []
    for i in range(steps):
        copies.append(
            pltpu.make_async_copy(
                fisher_ref.at[pl.ds(half * rows + i * step, step), columns],
                held_ref.at[pl.ds(i * step, step), :],
                sem.at[i],
            )
        )
        copies[-1].start()
    return copies


def times(chunk_ref, fisher):
    return lax.dot_general(chunk_ref[...], fisher, NT, preferred_element_type=jnp.float32)


def fisher_kernel(n_in, has_base, fetch, step, *refs):
    if fetch:
        at_ref, fisher_ref, *refs = refs
    chunk_ref, halves = (refs[0], refs[1:3]) if n_in else (None, ())
    base_ref = refs[3] if has_base else None
    outs, sem = refs[n_in + has_base : -1], refs[-1]
    held = outs[1:] if n_in else outs
    copies = []
    for k, (piece, half) in enumerate(fetch):
        copies += start_half(fisher_ref, at_ref[0] ^ ORDER[piece], half, held[k], sem.at[k])
    for h, half_ref in enumerate(halves):
        rows = half_ref.shape[0]

        @pl.loop(0, rows // step)
        def _(i):
            columns = pl.ds(pl.multiple_of(h * rows + i * step, step), step)
            term = times(chunk_ref, half_ref[pl.ds(pl.multiple_of(i * step, step), step), :])
            outs[0][:, columns] = term + base_ref[:, columns] if has_base else term

    for copy in copies:
        copy.wait()


def fisher_step(fisher, first, width, fetch, chunk=None, halves=(), base=None, step=1024):
    rows = fisher.shape[0]
    ins = [] if chunk is None else [chunk, *halves]
    has_base = base is not None
    held = jax.ShapeDtypeStruct((rows // 2, width), fisher.dtype)
    out_shape = [] if chunk is None else [jax.ShapeDtypeStruct((chunk.shape[0], rows), jnp.float32)]
    out_shape += [held] * len(fetch)
    return pl.pallas_call(
        functools.partial(fisher_kernel, len(ins), has_base, fetch, step),
        out_shape=out_shape,
        in_specs=[SMEM, HBM][: 2 * bool(fetch)] + [VMEM] * (len(ins) + has_base),
        out_specs=[VMEM] * len(out_shape),
        scratch_shapes=[pltpu.SemaphoreType.DMA((max(len(fetch), 1), 2))],
        compiler_params=limit(34 if chunk is None else 20),
        cost_estimate=pl.CostEstimate(
            flops=0 if chunk is None else 2 * chunk.shape[0] * width * rows,
            bytes_accessed=width * rows * (len(fetch) + 2 * bool(ins)),
            transcendentals=0,
        ),
    )(*((scalar(first), fisher) if fetch else ()), *ins, *([base] if has_base else []))


def base_kernel(at_ref, piece0, piece1, piece2, swapped, mine_grads, other_grads, mine, other, theirs):
    width = piece0.shape[1]
    starts = [pl.multiple_of((at_ref[0] ^ mask) * width, width) for mask in ORDER[:3]]
    total = None
    for piece, start in zip((piece0, piece1, piece2), starts):
        term = times(piece, mine_grads[:, pl.ds(start, width)])
        total = term if total is None else total + term
    mine[...] = total
    theirs[...] = times(swapped, mine_grads[:, pl.ds(starts[0], width)])
    other[...] = times(piece1, other_grads[:, :width]) + times(piece2, other_grads[:, width : 2 * width])


def last_kernel(at_ref, piece3, mine_grads, other_grads, mine_base, other_base, mine, other):
    width = piece3.shape[1]
    start = pl.multiple_of((at_ref[0] ^ ORDER[3]) * width, width)
    other[...] = other_base[...] + times(piece3, other_grads[:, 2 * width :])
    mine[...] = mine_base[...] + times(piece3, mine_grads[:, pl.ds(start, width)])


def score_call(kernel, n_out, examples, first, *operands):
    rows, width = operands[0].shape
    return pl.pallas_call(
        kernel,
        out_shape=[jax.ShapeDtypeStruct((rows, examples), jnp.float32)] * n_out,
        in_specs=[SMEM] + [VMEM] * len(operands),
        out_specs=[VMEM] * n_out,
        compiler_params=limit(8),
        cost_estimate=pl.CostEstimate(
            flops=2 * rows * width * examples * 2 * n_out,
            bytes_accessed=2 * width * examples * 2 * n_out,
            transcendentals=0,
        ),
    )(scalar(first), *operands)


def cut_kernel(order, at_ref, src_ref, out_ref, sem):
    width = out_ref.shape[1] // len(order)
    copies = []
    for k, mask in enumerate(order):
        start = pl.multiple_of((at_ref[0] ^ mask) * width, width)
        copies.append(
            pltpu.make_async_copy(
                src_ref.at[:, pl.ds(start, width)], out_ref.at[:, k * width : (k + 1) * width], sem.at[k]
            )
        )
        copies[-1].start()
    for copy in copies:
        copy.wait()


def cut(src, order, first, width):
    n = len(order)
    return pl.pallas_call(
        functools.partial(cut_kernel, order),
        out_shape=jax.ShapeDtypeStruct((src.shape[0], n * width), src.dtype),
        in_specs=[SMEM, HBM],
        out_specs=VMEM,
        scratch_shapes=[pltpu.SemaphoreType.DMA((n,))],
        compiler_params=limit(57),
        cost_estimate=pl.CostEstimate(
            flops=0, bytes_accessed=2 * n * width * src.shape[0], transcendentals=0
        ),
    )(scalar(first), src)


def pick_kernel(at_ref, a_ref, b_ref, *refs):
    out_ref = refs[-1]

    @pl.when(at_ref[0] == 1)
    def _():
        out_ref[...] = a_ref[...]

    @pl.when(at_ref[0] != 1)
    def _():
        out_ref[...] = b_ref[...]


def pick(condition, a, b, after=()):
    return pl.pallas_call(
        pick_kernel,
        out_shape=jax.ShapeDtypeStruct(a.shape, a.dtype),
        in_specs=[SMEM] + [VMEM] * 2 + [ANY] * len(after),
        out_specs=VMEM,
        compiler_params=limit(2),
        cost_estimate=pl.CostEstimate(flops=0, bytes_accessed=2 * a.size * 2, transcendentals=0),
    )(scalar(condition), a, b, *after)


def per_device_quad(nz, nx, ny, queries, inverse_fisher, stored_grads):
    nex = nz * nx
    near = nz // 2
    nq = queries.shape[0]
    y, e, d = (lax.axis_index(a) for a in AXES)
    z = e // nx
    x = e % nx
    u = jnp.where(d == 0, z, nz - 1 - z)
    owner = u < near

    def move(value, target):
        pairs = []
        for sy in range(ny):
            for sz in range(nz):
                for sx in range(nx):
                    for sd in range(2):
                        to = target(sy, sz, sx, sd)
                        if to is not None:
                            ty, tz, tx, td = to
                            pairs.append(((sy * nex + sz * nx + sx) * 2 + sd, (ty * nex + tz * nx + tx) * 2 + td))
        return lax.ppermute(value, AXES, pairs)

    def along_z(value, hops, flip=False):
        def target(sy, sz, sx, sd):
            su = sz if sd == 0 else nz - 1 - sz
            if su not in hops:
                return None
            tu = hops[su]
            return sy, tu if sd == 0 else nz - 1 - tu, 1 - sx if flip else sx, sd

        return move(value, target)

    def swap_y(value):
        return move(value, lambda sy, sz, sx, sd: (1 - sy, sz, sx, sd))

    def swap_core(value):
        return move(value, lambda sy, sz, sx, sd: (sy, sz, sx, 1 - sd))

    def gather(own, after=()):
        def start(sy, sz, sx, sd):
            su = sz if sd == 0 else nz - 1 - sz
            if su < near:
                return sy, sz + 2 if sd == 0 else sz - 2, sx, sd
            return sy, sz ^ 1, 1 - sx, 1 - sd

        came = move(own, start)
        first = pick(owner, own, came, after)
        beside = along_z(first, {0: 1, 1: 0, 2: 3, 3: 2})
        across = along_z(first, {0: 0, 1: 1, 2: 2, 3: 3}, True)

        def corner(after):
            ready, _ = lax.optimization_barrier((beside, after))
            return pick(owner, came, along_z(ready, {2: 2, 3: 3}, True))

        return first, beside, across, corner

    plane = jnp.where(d == 0, u % 2, nz - 1 - u % 2)
    column = plane * nx + x - d * (nex // 2)

    rows, width = nq // ny, queries.shape[1]
    own = lax.optimization_barrier(lax.dynamic_slice_in_dim(queries, y * rows, rows, axis=0))
    to_y = cut(stored_grads, ORDER[1:], column, width)
    other_grads = swap_y(to_y)
    at, _ = lax.optimization_barrier((column, to_y))
    step = functools.partial(fisher_step, inverse_fisher, at, width)
    a0, a1, b0 = step(((0, 0), (0, 1), (1, 0)))
    q0, q1, q2, corner = gather(own, (a0,))
    total, b1, c0 = step(((1, 1), (2, 0)), q0, (a0, a1))
    q3 = corner(total)
    total, c1, d0 = step(((2, 1), (3, 0)), q1, (b0, b1), total)
    total, d1 = step(((3, 1),), q2, (c0, c1), total)
    (total,) = step((), q3, (d0, d1), total)
    panel = (total + swap_core(total)).astype(jnp.bfloat16)

    p0, p1, p2, corner = gather(panel, (other_grads,))
    p3 = corner(p1)
    examples = stored_grads.shape[0]
    mine, other, theirs = score_call(
        base_kernel, 3, examples, column, p0, p1, p2, swap_y(p0), stored_grads, other_grads
    )
    p3, _ = lax.optimization_barrier((p3, mine))
    mine, other = score_call(
        last_kernel, 2, examples, column, p3, stored_grads, other_grads, mine, other
    )

    other = swap_y(other) + theirs
    keep = jnp.where(d == y, mine, other)
    give = jnp.where(d == y, other, mine)
    return keep + swap_core(give)


def solution(mesh):
    coords = [getattr(device, "coords", None) for device in mesh.devices.flat]
    nx = 2 if None in coords else len({c[0] for c in coords})
    nz = mesh.shape["ex"] // nx
    ny = mesh.shape["grp"]
    if (nz, nx, ny) == (4, 2, 2):
        body = functools.partial(per_device_quad, nz, nx, ny)
    else:
        body = per_device_any
    return jax.shard_map(
        body,
        mesh=mesh,
        in_specs=(P(None, "ex"), P("ex", "dim"), P(("grp", "ex"), "dim")),
        out_specs=P("dim", ("grp", "ex")),
        check_vma=False,
    )
```

```python
import functools

import jax
import jax.numpy as jnp
from jax import lax
from jax.experimental import pallas as pl
from jax.experimental.pallas import tpu as pltpu
from jax.sharding import PartitionSpec as P

AXES = ("grp", "ex", "dim")
NT = (((1,), (1,)), ((), ()))
VMEM = pl.BlockSpec(memory_space=pltpu.VMEM)
SMEM = pl.BlockSpec(memory_space=pltpu.SMEM)
HBM = pl.BlockSpec(memory_space=pltpu.HBM)
ANY = pl.BlockSpec(memory_space=pl.ANY)


def limit(mib):
    return pltpu.CompilerParams(vmem_limit_bytes=mib * 1024 * 1024)


def per_device_any(queries, inverse_fisher, stored_grads):
    term_block = jnp.dot(queries, inverse_fisher, preferred_element_type=jnp.float32)
    own_panel = lax.psum_scatter(term_block, "ex", scatter_dimension=1, tiled=True).astype(
        jnp.bfloat16
    )
    partial_scores = lax.dot_general(
        lax.all_gather(own_panel, "ex", axis=1, tiled=True),
        stored_grads,
        NT,
        preferred_element_type=jnp.float32,
    )
    return lax.psum_scatter(partial_scores, "dim", scatter_dimension=0, tiled=True)


def scalar(value):
    return jnp.asarray(value, jnp.int32).reshape(1)


ORDER = (0, 2, 1, 3)


def half_copies(fisher_ref, block, half, held_ref, sem):
    steps = sem.shape[0]
    rows, width = held_ref.shape
    step = rows // steps
    columns = pl.ds(pl.multiple_of(block * width, width), width)
    copies = []
    for i in range(steps):
        copies.append(
            pltpu.make_async_copy(
                fisher_ref.at[pl.ds(half * rows + i * step, step), columns],
                held_ref.at[pl.ds(i * step, step), :],
                sem.at[i],
            )
        )
    return copies


def times(chunk_ref, fisher):
    return lax.dot_general(chunk_ref[...], fisher, NT, preferred_element_type=jnp.float32)


def fisher_kernel(n_in, has_base, fetch, *refs):
    if fetch:
        at_ref, fisher_ref, *refs = refs
    chunk_ref, halves = (refs[0], refs[1:3]) if n_in else (None, ())
    base_ref = refs[3] if has_base else None
    outs, sem = refs[n_in + has_base : -1], refs[-1]
    held = outs[1:] if n_in else outs
    copies = []
    for k, (piece, half) in enumerate(fetch):
        copies += half_copies(fisher_ref, at_ref[0] ^ ORDER[piece], half, held[k], sem.at[k])
    if fetch:

        @pl.when(at_ref[0] >= 0)
        def _():
            for copy in copies:
                copy.start()

    for h, half_ref in enumerate(halves):
        rows = half_ref.shape[0]
        columns = slice(h * rows, (h + 1) * rows)
        term = times(chunk_ref, half_ref[...])
        outs[0][:, columns] = term + base_ref[:, columns] if has_base else term

    for copy in copies:
        copy.wait()


def fisher_step(fisher, first, width, fetch, chunk=None, halves=(), base=None):
    rows = fisher.shape[0]
    ins = [] if chunk is None else [chunk, *halves]
    has_base = base is not None
    held = jax.ShapeDtypeStruct((rows // 2, width), fisher.dtype)
    out_shape = [] if chunk is None else [jax.ShapeDtypeStruct((chunk.shape[0], rows), jnp.float32)]
    out_shape += [held] * len(fetch)
    return pl.pallas_call(
        functools.partial(fisher_kernel, len(ins), has_base, fetch),
        out_shape=out_shape,
        in_specs=[SMEM, HBM][: 2 * bool(fetch)] + [VMEM] * (len(ins) + has_base),
        out_specs=[VMEM] * len(out_shape),
        scratch_shapes=[pltpu.SemaphoreType.DMA((max(len(fetch), 1), 2))],
        compiler_params=limit(34 if chunk is None else 20),
        cost_estimate=pl.CostEstimate(
            flops=0 if chunk is None else 2 * chunk.shape[0] * width * rows,
            bytes_accessed=width * rows * (len(fetch) + 2 * bool(ins)),
            transcendentals=0,
        ),
    )(*((scalar(first), fisher) if fetch else ()), *ins, *([base] if has_base else []))


def base_kernel(at_ref, piece0, piece1, piece2, mine_grads, other_grads, mine, other):
    width = piece0.shape[1]
    total = None
    for piece, mask in zip((piece0, piece1, piece2), ORDER):
        start = pl.multiple_of((at_ref[0] ^ mask) * width, width)
        term = times(piece, mine_grads[:, pl.ds(start, width)])
        total = term if total is None else total + term
    mine[...] = total
    other[...] = times(piece1, other_grads[:, :width]) + times(piece2, other_grads[:, width : 2 * width])


def last_kernel(at_ref, piece3, swapped, mine_grads, other_grads, mine_base, other_base, mine, other, theirs):
    width = piece3.shape[1]
    start0, start3 = (pl.multiple_of((at_ref[0] ^ ORDER[k]) * width, width) for k in (0, 3))
    other[...] = other_base[...] + times(piece3, other_grads[:, 2 * width :])
    mine[...] = mine_base[...] + times(piece3, mine_grads[:, pl.ds(start3, width)])
    theirs[...] = times(swapped, mine_grads[:, pl.ds(start0, width)])


def score_call(kernel, n_out, examples, first, *operands):
    rows, width = operands[0].shape
    return pl.pallas_call(
        kernel,
        out_shape=[jax.ShapeDtypeStruct((rows, examples), jnp.float32)] * n_out,
        in_specs=[SMEM] + [VMEM] * len(operands),
        out_specs=[VMEM] * n_out,
        compiler_params=limit(8),
        cost_estimate=pl.CostEstimate(
            flops=2 * rows * width * examples * 2 * n_out,
            bytes_accessed=2 * width * examples * 2 * n_out,
            transcendentals=0,
        ),
    )(scalar(first), *operands)


def cut_kernel(order, at_ref, src_ref, out_ref, sem):
    width = out_ref.shape[1] // len(order)
    copies = []
    for k, mask in enumerate(order):
        start = pl.multiple_of((at_ref[0] ^ mask) * width, width)
        copies.append(
            pltpu.make_async_copy(
                src_ref.at[:, pl.ds(start, width)], out_ref.at[:, k * width : (k + 1) * width], sem.at[k]
            )
        )
        copies[-1].start()
    for copy in copies:
        copy.wait()


def cut(src, order, first, width):
    n = len(order)
    return pl.pallas_call(
        functools.partial(cut_kernel, order),
        out_shape=jax.ShapeDtypeStruct((src.shape[0], n * width), src.dtype),
        in_specs=[SMEM, HBM],
        out_specs=VMEM,
        scratch_shapes=[pltpu.SemaphoreType.DMA((n,))],
        compiler_params=limit(51),
        cost_estimate=pl.CostEstimate(
            flops=0, bytes_accessed=2 * n * width * src.shape[0], transcendentals=0
        ),
    )(scalar(first), src)


def pick_kernel(at_ref, a_ref, b_ref, *refs):
    out_ref = refs[-1]

    @pl.when(at_ref[0] == 1)
    def _():
        out_ref[...] = a_ref[...]

    @pl.when(at_ref[0] != 1)
    def _():
        out_ref[...] = b_ref[...]


def pick(condition, a, b, after=()):
    return pl.pallas_call(
        pick_kernel,
        out_shape=jax.ShapeDtypeStruct(a.shape, a.dtype),
        in_specs=[SMEM] + [VMEM] * 2 + [ANY] * len(after),
        out_specs=VMEM,
        compiler_params=limit(2),
        cost_estimate=pl.CostEstimate(flops=0, bytes_accessed=2 * a.size * 2, transcendentals=0),
    )(scalar(condition), a, b, *after)


def per_device_quad(nz, nx, ny, queries, inverse_fisher, stored_grads):
    nex = nz * nx
    near = nz // 2
    nq = queries.shape[0]
    y, e, d = (lax.axis_index(a) for a in AXES)
    z = e // nx
    x = e % nx
    u = jnp.where(d == 0, z, nz - 1 - z)
    owner = u < near

    def move(value, target):
        pairs = []
        for sy in range(ny):
            for sz in range(nz):
                for sx in range(nx):
                    for sd in range(2):
                        to = target(sy, sz, sx, sd)
                        if to is not None:
                            ty, tz, tx, td = to
                            pairs.append(((sy * nex + sz * nx + sx) * 2 + sd, (ty * nex + tz * nx + tx) * 2 + td))
        return lax.ppermute(value, AXES, pairs)

    def along_z(value, hops, flip=False):
        def target(sy, sz, sx, sd):
            su = sz if sd == 0 else nz - 1 - sz
            if su not in hops:
                return None
            tu = hops[su]
            return sy, tu if sd == 0 else nz - 1 - tu, 1 - sx if flip else sx, sd

        return move(value, target)

    def swap_y(value):
        return move(value, lambda sy, sz, sx, sd: (1 - sy, sz, sx, sd))

    def swap_core(value):
        return move(value, lambda sy, sz, sx, sd: (sy, sz, sx, 1 - sd))

    def gather(own, after=()):
        def start(sy, sz, sx, sd):
            su = sz if sd == 0 else nz - 1 - sz
            if su < near:
                return sy, sz + 2 if sd == 0 else sz - 2, sx, sd
            return sy, sz ^ 1, 1 - sx, 1 - sd

        came = move(own, start)
        first = pick(owner, own, came, after)
        beside = along_z(first, {0: 1, 1: 0, 2: 3, 3: 2})
        across = along_z(first, {0: 0, 1: 1, 2: 2, 3: 3}, True)
        diagonal = along_z(first, {2: 3, 3: 2}, True)

        def corner(after):
            ready, _ = lax.optimization_barrier((came, after))
            return pick(owner, ready, diagonal)

        return first, beside, across, corner

    plane = jnp.where(d == 0, u % 2, nz - 1 - u % 2)
    column = plane * nx + x - d * (nex // 2)

    rows, width = nq // ny, queries.shape[1]
    own, grads = lax.optimization_barrier(
        (lax.dynamic_slice_in_dim(queries, y * rows, rows, axis=0), stored_grads)
    )
    to_y = cut(grads, ORDER[1:], column, width)
    other_grads = swap_y(to_y)
    at, _ = lax.optimization_barrier((column, to_y))
    step = functools.partial(fisher_step, inverse_fisher, at, width)
    a0, a1, b0, b1 = step(((0, 0), (0, 1), (1, 0), (1, 1)))
    q0, q1, q2, corner = gather(own, (a0,))
    total, c0, c1 = step(((2, 0), (2, 1)), q0, (a0, a1))
    total, d0 = step(((3, 0),), q1, (b0, b1), total)
    total, d1 = step(((3, 1),), q2, (c0, c1), total)
    (total,) = step((), corner(total), (d0, d1), total)
    panel = (total + swap_core(total)).astype(jnp.bfloat16)

    p0, p1, p2, corner = gather(panel)
    examples = stored_grads.shape[0]
    mine, other = score_call(base_kernel, 2, examples, column, p0, p1, p2, stored_grads, other_grads)
    mine, other, theirs = score_call(
        last_kernel, 3, examples, column, corner(mine), swap_y(p0), stored_grads, other_grads, mine, other
    )

    other = swap_y(other) + theirs
    keep = jnp.where(d == y, mine, other)
    give = jnp.where(d == y, other, mine)
    return keep + swap_core(give)


def solution(mesh):
    coords = [getattr(device, "coords", None) for device in mesh.devices.flat]
    nx = 2 if None in coords else len({c[0] for c in coords})
    nz = mesh.shape["ex"] // nx
    ny = mesh.shape["grp"]
    if (nz, nx, ny) == (4, 2, 2):
        body = functools.partial(per_device_quad, nz, nx, ny)
    else:
        body = per_device_any
    return jax.shard_map(
        body,
        mesh=mesh,
        in_specs=(P(None, "ex"), P("ex", "dim"), P(("grp", "ex"), "dim")),
        out_specs=P("dim", ("grp", "ex")),
        check_vma=False,
    )
```

```python
import functools

import jax
import jax.numpy as jnp
from jax import lax
from jax.experimental import pallas as pl
from jax.experimental.pallas import tpu as pltpu
from jax.sharding import PartitionSpec as P

AXES = ("grp", "ex", "dim")
NT = (((1,), (1,)), ((), ()))
VMEM = pl.BlockSpec(memory_space=pltpu.VMEM)
SMEM = pl.BlockSpec(memory_space=pltpu.SMEM)
HBM = pl.BlockSpec(memory_space=pltpu.HBM)
ANY = pl.BlockSpec(memory_space=pl.ANY)


def limit(mib):
    return pltpu.CompilerParams(vmem_limit_bytes=mib * 1024 * 1024)


def per_device_any(queries, inverse_fisher, stored_grads):
    term_block = jnp.dot(queries, inverse_fisher, preferred_element_type=jnp.float32)
    own_panel = lax.psum_scatter(term_block, "ex", scatter_dimension=1, tiled=True).astype(
        jnp.bfloat16
    )
    partial_scores = lax.dot_general(
        lax.all_gather(own_panel, "ex", axis=1, tiled=True),
        stored_grads,
        NT,
        preferred_element_type=jnp.float32,
    )
    return lax.psum_scatter(partial_scores, "dim", scatter_dimension=0, tiled=True)


def scalar(value):
    return jnp.asarray(value, jnp.int32).reshape(1)


ORDER = (0, 2, 1, 3)


def half_copies(fisher_ref, block, half, held_ref, sem):
    steps = sem.shape[0]
    rows, width = held_ref.shape
    step = rows // steps
    columns = pl.ds(pl.multiple_of(block * width, width), width)
    copies = []
    for i in range(steps):
        copies.append(
            pltpu.make_async_copy(
                fisher_ref.at[pl.ds(half * rows + i * step, step), columns],
                held_ref.at[pl.ds(i * step, step), :],
                sem.at[i],
            )
        )
    return copies


def times(chunk_ref, fisher):
    return lax.dot_general(chunk_ref[...], fisher, NT, preferred_element_type=jnp.float32)


def fisher_kernel(n_in, has_base, fetch, *refs):
    if fetch:
        at_ref, fisher_ref, *refs = refs
    chunk_ref, halves = (refs[0], refs[1:3]) if n_in else (None, ())
    base_ref = refs[3] if has_base else None
    outs, sem = refs[n_in + has_base : -1], refs[-1]
    held = outs[1:] if n_in else outs
    copies = []
    for k, (piece, half) in enumerate(fetch):
        for copy in half_copies(fisher_ref, at_ref[0] ^ ORDER[piece], half, held[k], sem.at[k]):
            copy.start()
            copies.append(copy)

    def product(h, start, step):
        columns = pl.ds(h * halves[h].shape[0] + start, step)
        term = times(chunk_ref, halves[h][pl.ds(start, step), :])
        outs[0][:, columns] = term + base_ref[:, columns] if has_base else term

    for h, half_ref in enumerate(halves):
        rows = half_ref.shape[0]
        if fetch:

            @pl.loop(0, 2)
            def _(i):
                product(h, pl.multiple_of(i * (rows // 2), rows // 2), rows // 2)
        else:
            product(h, 0, rows)

    for copy in copies:
        copy.wait()


def fisher_step(fisher, first, width, fetch, chunk=None, halves=(), base=None):
    rows = fisher.shape[0]
    ins = [] if chunk is None else [chunk, *halves]
    has_base = base is not None
    held = jax.ShapeDtypeStruct((rows // 2, width), fisher.dtype)
    out_shape = [] if chunk is None else [jax.ShapeDtypeStruct((chunk.shape[0], rows), jnp.float32)]
    out_shape += [held] * len(fetch)
    return pl.pallas_call(
        functools.partial(fisher_kernel, len(ins), has_base, fetch),
        out_shape=out_shape,
        in_specs=[SMEM, HBM][: 2 * bool(fetch)] + [VMEM] * (len(ins) + has_base),
        out_specs=[VMEM] * len(out_shape),
        scratch_shapes=[pltpu.SemaphoreType.DMA((max(len(fetch), 1), 2))],
        compiler_params=limit(24 if chunk is None else 20),
        cost_estimate=pl.CostEstimate(
            flops=0 if chunk is None else 2 * chunk.shape[0] * width * rows,
            bytes_accessed=width * rows * (len(fetch) + 2 * bool(ins)),
            transcendentals=0,
        ),
    )(*((scalar(first), fisher) if fetch else ()), *ins, *([base] if has_base else []))


def base_kernel(at_ref, piece0, piece1, piece2, mine_grads, other_grads, mine, other):
    width = piece0.shape[1]
    total = None
    for piece, mask in zip((piece0, piece1, piece2), ORDER):
        start = pl.multiple_of((at_ref[0] ^ mask) * width, width)
        term = times(piece, mine_grads[:, pl.ds(start, width)])
        total = term if total is None else total + term
    mine[...] = total
    other[...] = times(piece1, other_grads[:, :width]) + times(piece2, other_grads[:, width : 2 * width])


def last_kernel(at_ref, piece3, mine_grads, other_grads, mine_base, other_base, mine, other):
    width = piece3.shape[1]
    start = pl.multiple_of((at_ref[0] ^ ORDER[3]) * width, width)
    other[...] = other_base[...] + times(piece3, other_grads[:, 2 * width :])
    mine[...] = mine_base[...] + times(piece3, mine_grads[:, pl.ds(start, width)])


def first_kernel(at_ref, piece0, mine_grads, theirs):
    width = piece0.shape[1]
    start = pl.multiple_of((at_ref[0] ^ ORDER[0]) * width, width)
    theirs[...] = times(piece0, mine_grads[:, pl.ds(start, width)])


def score_call(kernel, n_out, examples, first, *operands):
    rows, width = operands[0].shape
    return pl.pallas_call(
        kernel,
        out_shape=[jax.ShapeDtypeStruct((rows, examples), jnp.float32)] * n_out,
        in_specs=[SMEM] + [VMEM] * len(operands),
        out_specs=[VMEM] * n_out,
        compiler_params=limit(8),
        cost_estimate=pl.CostEstimate(
            flops=2 * rows * width * examples * 2 * n_out,
            bytes_accessed=2 * width * examples * 2 * n_out,
            transcendentals=0,
        ),
    )(scalar(first), *operands)


def cut_kernel(order, at_ref, src_ref, out_ref, sem):
    width = out_ref.shape[1] // len(order)
    copies = []
    for k, mask in enumerate(order):
        start = pl.multiple_of((at_ref[0] ^ mask) * width, width)
        copies.append(
            pltpu.make_async_copy(
                src_ref.at[:, pl.ds(start, width)], out_ref.at[:, k * width : (k + 1) * width], sem.at[k]
            )
        )
        copies[-1].start()
    for copy in copies:
        copy.wait()


def cut(src, order, first, width):
    n = len(order)
    return pl.pallas_call(
        functools.partial(cut_kernel, order),
        out_shape=jax.ShapeDtypeStruct((src.shape[0], n * width), src.dtype),
        in_specs=[SMEM, HBM],
        out_specs=VMEM,
        scratch_shapes=[pltpu.SemaphoreType.DMA((n,))],
        compiler_params=limit(50),
        cost_estimate=pl.CostEstimate(
            flops=0, bytes_accessed=2 * n * width * src.shape[0], transcendentals=0
        ),
    )(scalar(first), src)


def pick_kernel(at_ref, a_ref, b_ref, *refs):
    out_ref = refs[-1]

    @pl.when(at_ref[0] == 1)
    def _():
        out_ref[...] = a_ref[...]

    @pl.when(at_ref[0] != 1)
    def _():
        out_ref[...] = b_ref[...]


def pick(condition, a, b, after=()):
    return pl.pallas_call(
        pick_kernel,
        out_shape=jax.ShapeDtypeStruct(a.shape, a.dtype),
        in_specs=[SMEM] + [VMEM] * 2 + [ANY] * len(after),
        out_specs=VMEM,
        compiler_params=limit(2),
        cost_estimate=pl.CostEstimate(flops=0, bytes_accessed=2 * a.size * 2, transcendentals=0),
    )(scalar(condition), a, b, *after)


def per_device_quad(nz, nx, ny, queries, inverse_fisher, stored_grads):
    nex = nz * nx
    near = nz // 2
    nq = queries.shape[0]
    y, e, d = (lax.axis_index(a) for a in AXES)
    z = e // nx
    x = e % nx
    u = jnp.where(d == 0, z, nz - 1 - z)
    owner = u < near

    def move(value, target):
        pairs = []
        for sy in range(ny):
            for sz in range(nz):
                for sx in range(nx):
                    for sd in range(2):
                        to = target(sy, sz, sx, sd)
                        if to is not None:
                            ty, tz, tx, td = to
                            pairs.append(((sy * nex + sz * nx + sx) * 2 + sd, (ty * nex + tz * nx + tx) * 2 + td))
        return lax.ppermute(value, AXES, pairs)

    def along_z(value, hops, flip=False):
        def target(sy, sz, sx, sd):
            su = sz if sd == 0 else nz - 1 - sz
            if su not in hops:
                return None
            tu = hops[su]
            return sy, tu if sd == 0 else nz - 1 - tu, 1 - sx if flip else sx, sd

        return move(value, target)

    def swap_y(value):
        return move(value, lambda sy, sz, sx, sd: (1 - sy, sz, sx, sd))

    def swap_core(value):
        return move(value, lambda sy, sz, sx, sd: (sy, sz, sx, 1 - sd))

    def gather(own, after=()):
        def start(sy, sz, sx, sd):
            su = sz if sd == 0 else nz - 1 - sz
            if su < near:
                return sy, sz + 2 if sd == 0 else sz - 2, sx, sd
            return sy, sz ^ 1, 1 - sx, 1 - sd

        came = move(own, start)
        first = pick(owner, own, came, after)
        beside = along_z(first, {0: 1, 1: 0, 2: 3, 3: 2})
        across = along_z(first, {0: 0, 1: 1, 2: 2, 3: 3}, True)
        diagonal = along_z(first, {2: 3, 3: 2}, True)

        def corner(after):
            ready, _ = lax.optimization_barrier((came, after))
            return pick(owner, ready, diagonal)

        return first, beside, across, corner

    plane = jnp.where(d == 0, u % 2, nz - 1 - u % 2)
    column = plane * nx + x - d * (nex // 2)

    rows, width = nq // ny, queries.shape[1]
    own, grads = lax.optimization_barrier(
        (lax.dynamic_slice_in_dim(queries, y * rows, rows, axis=0), stored_grads)
    )
    to_y = cut(grads, ORDER[1:], column, width)
    other_grads = swap_y(to_y)
    at, _ = lax.optimization_barrier((column, to_y))
    step = functools.partial(fisher_step, inverse_fisher, at, width)
    a0, a1, b0 = step(((0, 0), (0, 1), (1, 0)))
    q0, q1, q2, corner = gather(own, (a0,))
    total, b1, c0 = step(((1, 1), (2, 0)), q0, (a0, a1))
    total, c1, d0 = step(((2, 1), (3, 0)), q1, (b0, b1), total)
    total, d1 = step(((3, 1),), q2, (c0, c1), total)
    (total,) = step((), corner(total), (d0, d1), total)
    panel = (total + swap_core(total)).astype(jnp.bfloat16)

    p0, p1, p2, corner = gather(panel)
    examples = stored_grads.shape[0]
    mine, other = score_call(base_kernel, 2, examples, column, p0, p1, p2, stored_grads, other_grads)
    mine, other = score_call(
        last_kernel, 2, examples, column, corner(mine), stored_grads, other_grads, mine, other
    )
    swapped, _ = lax.optimization_barrier((swap_y(p0), other))
    (theirs,) = score_call(first_kernel, 1, examples, column, swapped, stored_grads)

    other = swap_y(other) + theirs
    keep = jnp.where(d == y, mine, other)
    give = jnp.where(d == y, other, mine)
    return keep + swap_core(give)


def solution(mesh):
    coords = [getattr(device, "coords", None) for device in mesh.devices.flat]
    nx = 2 if None in coords else len({c[0] for c in coords})
    nz = mesh.shape["ex"] // nx
    ny = mesh.shape["grp"]
    if (nz, nx, ny) == (4, 2, 2):
        body = functools.partial(per_device_quad, nz, nx, ny)
    else:
        body = per_device_any
    return jax.shard_map(
        body,
        mesh=mesh,
        in_specs=(P(None, "ex"), P("ex", "dim"), P(("grp", "ex"), "dim")),
        out_specs=P("dim", ("grp", "ex")),
        check_vma=False,
    )
```

```python
import functools

import jax
import jax.numpy as jnp
from jax import lax
from jax.experimental import pallas as pl
from jax.experimental.pallas import tpu as pltpu
from jax.sharding import PartitionSpec as P

AXES = ("grp", "ex", "dim")
NT = (((1,), (1,)), ((), ()))
VMEM = pl.BlockSpec(memory_space=pltpu.VMEM)
SMEM = pl.BlockSpec(memory_space=pltpu.SMEM)
HBM = pl.BlockSpec(memory_space=pltpu.HBM)
ANY = pl.BlockSpec(memory_space=pl.ANY)


def limit(mib):
    return pltpu.CompilerParams(vmem_limit_bytes=mib * 1024 * 1024)


def per_device_any(queries, inverse_fisher, stored_grads):
    term_block = jnp.dot(queries, inverse_fisher, preferred_element_type=jnp.float32)
    own_panel = lax.psum_scatter(term_block, "ex", scatter_dimension=1, tiled=True).astype(
        jnp.bfloat16
    )
    partial_scores = lax.dot_general(
        lax.all_gather(own_panel, "ex", axis=1, tiled=True),
        stored_grads,
        NT,
        preferred_element_type=jnp.float32,
    )
    return lax.psum_scatter(partial_scores, "dim", scatter_dimension=0, tiled=True)


def scalar(value):
    return jnp.asarray(value, jnp.int32).reshape(1)


ORDER = (0, 2, 1, 3)


def half_copies(fisher_ref, block, half, held_ref, sem):
    steps = sem.shape[0]
    rows, width = held_ref.shape
    step = rows // steps
    columns = pl.ds(pl.multiple_of(block * width, width), width)
    copies = []
    for i in range(steps):
        copies.append(
            pltpu.make_async_copy(
                fisher_ref.at[pl.ds(half * rows + i * step, step), columns],
                held_ref.at[pl.ds(i * step, step), :],
                sem.at[i],
            )
        )
    return copies


def times(chunk_ref, fisher):
    return lax.dot_general(chunk_ref[...], fisher, NT, preferred_element_type=jnp.float32)


def fisher_kernel(n_in, has_base, fetch, *refs):
    if fetch:
        at_ref, fisher_ref, *refs = refs
    chunk_ref, halves = (refs[0], refs[1:3]) if n_in else (None, ())
    base_ref = refs[3] if has_base else None
    outs, sem = refs[n_in + has_base : -1], refs[-1]
    held = outs[1:] if n_in else outs
    copies = []
    for k, (piece, half) in enumerate(fetch):
        for copy in half_copies(fisher_ref, at_ref[0] ^ ORDER[piece], half, held[k], sem.at[k]):
            copy.start()
            copies.append(copy)

    def product(h, start, step):
        columns = pl.ds(h * halves[h].shape[0] + start, step)
        term = times(chunk_ref, halves[h][pl.ds(start, step), :])
        outs[0][:, columns] = term + base_ref[:, columns] if has_base else term

    for h, half_ref in enumerate(halves):
        rows = half_ref.shape[0]
        if fetch:

            @pl.loop(0, 2)
            def _(i):
                product(h, pl.multiple_of(i * (rows // 2), rows // 2), rows // 2)
        else:
            product(h, 0, rows)

    for copy in copies:
        copy.wait()


def fisher_step(fisher, first, width, fetch, chunk=None, halves=(), base=None):
    rows = fisher.shape[0]
    ins = [] if chunk is None else [chunk, *halves]
    has_base = base is not None
    held = jax.ShapeDtypeStruct((rows // 2, width), fisher.dtype)
    out_shape = [] if chunk is None else [jax.ShapeDtypeStruct((chunk.shape[0], rows), jnp.float32)]
    out_shape += [held] * len(fetch)
    return pl.pallas_call(
        functools.partial(fisher_kernel, len(ins), has_base, fetch),
        out_shape=out_shape,
        in_specs=[SMEM, HBM][: 2 * bool(fetch)] + [VMEM] * (len(ins) + has_base),
        out_specs=[VMEM] * len(out_shape),
        scratch_shapes=[pltpu.SemaphoreType.DMA((max(len(fetch), 1), 2))],
        compiler_params=limit(24 if chunk is None else 20),
        cost_estimate=pl.CostEstimate(
            flops=0 if chunk is None else 2 * chunk.shape[0] * width * rows,
            bytes_accessed=width * rows * (len(fetch) + 2 * bool(ins)),
            transcendentals=0,
        ),
    )(*((scalar(first), fisher) if fetch else ()), *ins, *([base] if has_base else []))


def score_kernel(order, has_base, at_ref, *refs):
    n = len(order)
    grads_ref, out_ref = refs[n], refs[-1]
    width = refs[0].shape[1]
    total = refs[n + 1][...] if has_base else None
    for k in range(n):
        start = pl.multiple_of((at_ref[0] ^ order[k]) * width, width)
        term = times(refs[k], grads_ref[:, pl.ds(start, width)])
        total = term if total is None else total + term
    out_ref[...] = total


def score_dot(pieces, order, first, grads, base=None):
    n = len(pieces)
    rows, width = pieces[0].shape
    operands = [*pieces, grads] + ([] if base is None else [base])
    return pl.pallas_call(
        functools.partial(score_kernel, order, base is not None),
        out_shape=jax.ShapeDtypeStruct((rows, grads.shape[0]), jnp.float32),
        in_specs=[SMEM] + [VMEM] * len(operands),
        out_specs=VMEM,
        compiler_params=limit(8),
        cost_estimate=pl.CostEstimate(
            flops=2 * n * rows * width * grads.shape[0],
            bytes_accessed=2 * n * width * grads.shape[0],
            transcendentals=0,
        ),
    )(scalar(first), *operands)


def pick_kernel(at_ref, a_ref, b_ref, *refs):
    out_ref = refs[-1]

    @pl.when(at_ref[0] == 1)
    def _():
        out_ref[...] = a_ref[...]

    @pl.when(at_ref[0] != 1)
    def _():
        out_ref[...] = b_ref[...]


def pick(condition, a, b, after=()):
    return pl.pallas_call(
        pick_kernel,
        out_shape=jax.ShapeDtypeStruct(a.shape, a.dtype),
        in_specs=[SMEM] + [VMEM] * 2 + [ANY] * len(after),
        out_specs=VMEM,
        compiler_params=limit(2),
        cost_estimate=pl.CostEstimate(flops=0, bytes_accessed=2 * a.size * 2, transcendentals=0),
    )(scalar(condition), a, b, *after)


def per_device_quad(nz, nx, ny, queries, inverse_fisher, stored_grads):
    nex = nz * nx
    near = nz // 2
    nq = queries.shape[0]
    y, e, d = (lax.axis_index(a) for a in AXES)
    z = e // nx
    x = e % nx
    u = jnp.where(d == 0, z, nz - 1 - z)
    owner = u < near

    def move(value, target):
        pairs = []
        for sy in range(ny):
            for sz in range(nz):
                for sx in range(nx):
                    for sd in range(2):
                        to = target(sy, sz, sx, sd)
                        if to is not None:
                            ty, tz, tx, td = to
                            pairs.append(((sy * nex + sz * nx + sx) * 2 + sd, (ty * nex + tz * nx + tx) * 2 + td))
        return lax.ppermute(value, AXES, pairs)

    def along_z(value, hops, flip=False):
        def target(sy, sz, sx, sd):
            su = sz if sd == 0 else nz - 1 - sz
            if su not in hops:
                return None
            tu = hops[su]
            return sy, tu if sd == 0 else nz - 1 - tu, 1 - sx if flip else sx, sd

        return move(value, target)

    def swap_y(value):
        return move(value, lambda sy, sz, sx, sd: (1 - sy, sz, sx, sd))

    def swap_core(value):
        return move(value, lambda sy, sz, sx, sd: (sy, sz, sx, 1 - sd))

    def gather(own, after=()):
        def start(sy, sz, sx, sd):
            su = sz if sd == 0 else nz - 1 - sz
            if su < near:
                return sy, sz + 2 if sd == 0 else sz - 2, sx, sd
            return sy, sz ^ 1, 1 - sx, 1 - sd

        came = move(own, start)
        first = pick(owner, own, came, after)
        pairs = {0: 1, 1: 0, 2: 3, 3: 2}
        beside = along_z(first, pairs)
        across = along_z(first, {0: 0, 1: 1, 2: 2, 3: 3}, True)
        diagonal = along_z(first, {2: 3, 3: 2}, True)

        def corner(after):
            ready, _ = lax.optimization_barrier((came, after))
            return pick(owner, ready, diagonal)

        return first, beside, across, corner

    plane = jnp.where(d == 0, u % 2, nz - 1 - u % 2)
    column = plane * nx + x - d * (nex // 2)

    other_grads = swap_y(stored_grads)

    rows = nq // ny
    own = lax.optimization_barrier(lax.dynamic_slice_in_dim(queries, y * rows, rows, axis=0))
    step = functools.partial(fisher_step, inverse_fisher, column, own.shape[1])
    a0, a1, b0, b1, c0 = step(((0, 0), (0, 1), (1, 0), (1, 1), (2, 0)))
    q0, q1, q2, corner = gather(own, (a0,))
    total, c1 = step(((2, 1),), q0, (a0, a1))
    total, d0 = step(((3, 0),), q1, (b0, b1), total)
    total, d1 = step(((3, 1),), q2, (c0, c1), total)
    (total,) = step((), corner(total), (d0, d1), total)
    panel = (total + swap_core(total)).astype(jnp.bfloat16)

    p0, p1, p2, corner = gather(panel)
    p3 = corner(panel)
    mine = score_dot([p0, p1], ORDER[:2], column, stored_grads)
    p2, _ = lax.optimization_barrier((p2, mine))
    other = score_dot([p0, p1, p2, p3], ORDER, column, other_grads)
    p2, p3, mine, _ = lax.optimization_barrier((p2, p3, mine, other))
    mine = score_dot([p2, p3], ORDER[2:], column, stored_grads, mine)

    other = swap_y(other)
    keep = jnp.where(d == y, mine, other)
    give = jnp.where(d == y, other, mine)
    return keep + swap_core(give)


def solution(mesh):
    coords = [getattr(device, "coords", None) for device in mesh.devices.flat]
    nx = 2 if None in coords else len({c[0] for c in coords})
    nz = mesh.shape["ex"] // nx
    ny = mesh.shape["grp"]
    if (nz, nx, ny) == (4, 2, 2):
        body = functools.partial(per_device_quad, nz, nx, ny)
    else:
        body = per_device_any
    return jax.shard_map(
        body,
        mesh=mesh,
        in_specs=(P(None, "ex"), P("ex", "dim"), P(("grp", "ex"), "dim")),
        out_specs=P("dim", ("grp", "ex")),
        check_vma=False,
    )
```

```python
import functools

import jax
import jax.numpy as jnp
from jax import lax
from jax.experimental import pallas as pl
from jax.experimental.pallas import tpu as pltpu
from jax.sharding import PartitionSpec as P

AXES = ("grp", "ex", "dim")
NT = (((1,), (1,)), ((), ()))
VMEM = pl.BlockSpec(memory_space=pltpu.VMEM)
SMEM = pl.BlockSpec(memory_space=pltpu.SMEM)
HBM = pl.BlockSpec(memory_space=pltpu.HBM)
ANY = pl.BlockSpec(memory_space=pl.ANY)


def limit(mib):
    return pltpu.CompilerParams(vmem_limit_bytes=mib * 1024 * 1024)


def per_device_any(queries, inverse_fisher, stored_grads):
    term_block = jnp.dot(queries, inverse_fisher, preferred_element_type=jnp.float32)
    own_panel = lax.psum_scatter(term_block, "ex", scatter_dimension=1, tiled=True).astype(
        jnp.bfloat16
    )
    partial_scores = lax.dot_general(
        lax.all_gather(own_panel, "ex", axis=1, tiled=True),
        stored_grads,
        NT,
        preferred_element_type=jnp.float32,
    )
    return lax.psum_scatter(partial_scores, "dim", scatter_dimension=0, tiled=True)


def scalar(value):
    return jnp.asarray(value, jnp.int32).reshape(1)


ORDER = (0, 2, 1, 3)


def half_copies(fisher_ref, block, half, held_ref, sem):
    steps = sem.shape[0]
    rows, width = held_ref.shape
    step = rows // steps
    columns = pl.ds(pl.multiple_of(block * width, width), width)
    copies = []
    for i in range(steps):
        copies.append(
            pltpu.make_async_copy(
                fisher_ref.at[pl.ds(half * rows + i * step, step), columns],
                held_ref.at[pl.ds(i * step, step), :],
                sem.at[i],
            )
        )
    return copies


def times(chunk_ref, fisher):
    return lax.dot_general(chunk_ref[...], fisher, NT, preferred_element_type=jnp.float32)


def fisher_kernel(n_in, has_base, fetch, *refs):
    if fetch:
        at_ref, fisher_ref, *refs = refs
    chunk_ref, halves = (refs[0], refs[1:3]) if n_in else (None, ())
    base_ref = refs[3] if has_base else None
    outs, sem = refs[n_in + has_base : -1], refs[-1]
    held = outs[1:] if n_in else outs
    copies = []
    for k, (piece, half) in enumerate(fetch):
        for copy in half_copies(fisher_ref, at_ref[0] ^ ORDER[piece], half, held[k], sem.at[k]):
            copy.start()
            copies.append(copy)

    def product(h, start, step):
        columns = pl.ds(h * halves[h].shape[0] + start, step)
        term = times(chunk_ref, halves[h][pl.ds(start, step), :])
        outs[0][:, columns] = term + base_ref[:, columns] if has_base else term

    for h, half_ref in enumerate(halves):
        rows = half_ref.shape[0]
        if fetch:

            @pl.loop(0, 2)
            def _(i):
                product(h, pl.multiple_of(i * (rows // 2), rows // 2), rows // 2)
        else:
            product(h, 0, rows)

    for copy in copies:
        copy.wait()


def fisher_step(fisher, first, width, fetch, chunk=None, halves=(), base=None):
    rows = fisher.shape[0]
    ins = [] if chunk is None else [chunk, *halves]
    has_base = base is not None
    held = jax.ShapeDtypeStruct((rows // 2, width), fisher.dtype)
    out_shape = [] if chunk is None else [jax.ShapeDtypeStruct((chunk.shape[0], rows), jnp.float32)]
    out_shape += [held] * len(fetch)
    return pl.pallas_call(
        functools.partial(fisher_kernel, len(ins), has_base, fetch),
        out_shape=out_shape,
        in_specs=[SMEM, HBM][: 2 * bool(fetch)] + [VMEM] * (len(ins) + has_base),
        out_specs=[VMEM] * len(out_shape),
        scratch_shapes=[pltpu.SemaphoreType.DMA((max(len(fetch), 1), 2))],
        compiler_params=limit(34 if chunk is None else 20),
        cost_estimate=pl.CostEstimate(
            flops=0 if chunk is None else 2 * chunk.shape[0] * width * rows,
            bytes_accessed=width * rows * (len(fetch) + 2 * bool(ins)),
            transcendentals=0,
        ),
    )(*((scalar(first), fisher) if fetch else ()), *ins, *([base] if has_base else []))


def score_kernel(order, has_base, at_ref, *refs):
    n = len(order)
    grads_ref, out_ref = refs[n], refs[-1]
    width = refs[0].shape[1]
    total = refs[n + 1][...] if has_base else None
    for k in range(n):
        start = pl.multiple_of((at_ref[0] ^ order[k]) * width, width)
        term = times(refs[k], grads_ref[:, pl.ds(start, width)])
        total = term if total is None else total + term
    out_ref[...] = total


def score_dot(pieces, order, first, grads, base=None):
    n = len(pieces)
    rows, width = pieces[0].shape
    operands = [*pieces, grads] + ([] if base is None else [base])
    return pl.pallas_call(
        functools.partial(score_kernel, order, base is not None),
        out_shape=jax.ShapeDtypeStruct((rows, grads.shape[0]), jnp.float32),
        in_specs=[SMEM] + [VMEM] * len(operands),
        out_specs=VMEM,
        compiler_params=limit(8),
        cost_estimate=pl.CostEstimate(
            flops=2 * n * rows * width * grads.shape[0],
            bytes_accessed=2 * n * width * grads.shape[0],
            transcendentals=0,
        ),
    )(scalar(first), *operands)


def pick_kernel(at_ref, a_ref, b_ref, *refs):
    out_ref = refs[-1]

    @pl.when(at_ref[0] == 1)
    def _():
        out_ref[...] = a_ref[...]

    @pl.when(at_ref[0] != 1)
    def _():
        out_ref[...] = b_ref[...]


def pick(condition, a, b, after=()):
    return pl.pallas_call(
        pick_kernel,
        out_shape=jax.ShapeDtypeStruct(a.shape, a.dtype),
        in_specs=[SMEM] + [VMEM] * 2 + [ANY] * len(after),
        out_specs=VMEM,
        compiler_params=limit(2),
        cost_estimate=pl.CostEstimate(flops=0, bytes_accessed=2 * a.size * 2, transcendentals=0),
    )(scalar(condition), a, b, *after)


def per_device_quad(nz, nx, ny, queries, inverse_fisher, stored_grads):
    nex = nz * nx
    near = nz // 2
    nq = queries.shape[0]
    y, e, d = (lax.axis_index(a) for a in AXES)
    z = e // nx
    x = e % nx
    u = jnp.where(d == 0, z, nz - 1 - z)
    owner = u < near

    def move(value, target):
        pairs = []
        for sy in range(ny):
            for sz in range(nz):
                for sx in range(nx):
                    for sd in range(2):
                        to = target(sy, sz, sx, sd)
                        if to is not None:
                            ty, tz, tx, td = to
                            pairs.append(((sy * nex + sz * nx + sx) * 2 + sd, (ty * nex + tz * nx + tx) * 2 + td))
        return lax.ppermute(value, AXES, pairs)

    def along_z(value, hops, flip=False):
        def target(sy, sz, sx, sd):
            su = sz if sd == 0 else nz - 1 - sz
            if su not in hops:
                return None
            tu = hops[su]
            return sy, tu if sd == 0 else nz - 1 - tu, 1 - sx if flip else sx, sd

        return move(value, target)

    def swap_y(value):
        return move(value, lambda sy, sz, sx, sd: (1 - sy, sz, sx, sd))

    def swap_core(value):
        return move(value, lambda sy, sz, sx, sd: (sy, sz, sx, 1 - sd))

    def gather(own, after=()):
        def start(sy, sz, sx, sd):
            su = sz if sd == 0 else nz - 1 - sz
            if su < near:
                return sy, sz + 2 if sd == 0 else sz - 2, sx, sd
            return sy, sz ^ 1, 1 - sx, 1 - sd

        came = move(own, start)
        first = pick(owner, own, came, after)
        pairs = {0: 1, 1: 0, 2: 3, 3: 2}
        beside = along_z(first, pairs)
        across = along_z(first, {0: 0, 1: 1, 2: 2, 3: 3}, True)
        diagonal = along_z(first, {2: 3, 3: 2}, True)

        def corner(after):
            ready, _ = lax.optimization_barrier((came, after))
            return pick(owner, ready, diagonal)

        return first, beside, across, corner

    plane = jnp.where(d == 0, u % 2, nz - 1 - u % 2)
    column = plane * nx + x - d * (nex // 2)

    other_grads = swap_y(stored_grads)

    rows = nq // ny
    own = lax.optimization_barrier(lax.dynamic_slice_in_dim(queries, y * rows, rows, axis=0))
    step = functools.partial(fisher_step, inverse_fisher, column, own.shape[1])
    a0, a1, b0, b1 = step(((0, 0), (0, 1), (1, 0), (1, 1)))
    q0, q1, q2, corner = gather(own, (a0,))
    total, c0, c1 = step(((2, 0), (2, 1)), q0, (a0, a1))
    total, d0 = step(((3, 0),), q1, (b0, b1), total)
    total, d1 = step(((3, 1),), q2, (c0, c1), total)
    (total,) = step((), corner(total), (d0, d1), total)
    panel = (total + swap_core(total)).astype(jnp.bfloat16)

    p0, p1, p2, corner = gather(panel)
    p3 = corner(panel)
    mine = score_dot([p0, p1], ORDER[:2], column, stored_grads)
    p2, _ = lax.optimization_barrier((p2, mine))
    other = score_dot([p0, p1, p2, p3], ORDER, column, other_grads)
    p2, p3, mine, _ = lax.optimization_barrier((p2, p3, mine, other))
    mine = score_dot([p2, p3], ORDER[2:], column, stored_grads, mine)

    other = swap_y(other)
    keep = jnp.where(d == y, mine, other)
    give = jnp.where(d == y, other, mine)
    return keep + swap_core(give)


def solution(mesh):
    coords = [getattr(device, "coords", None) for device in mesh.devices.flat]
    nx = 2 if None in coords else len({c[0] for c in coords})
    nz = mesh.shape["ex"] // nx
    ny = mesh.shape["grp"]
    if (nz, nx, ny) == (4, 2, 2):
        body = functools.partial(per_device_quad, nz, nx, ny)
    else:
        body = per_device_any
    return jax.shard_map(
        body,
        mesh=mesh,
        in_specs=(P(None, "ex"), P("ex", "dim"), P(("grp", "ex"), "dim")),
        out_specs=P("dim", ("grp", "ex")),
        check_vma=False,
    )
```

```python
import functools

import jax
import jax.numpy as jnp
from jax import lax
from jax.experimental import pallas as pl
from jax.experimental.pallas import tpu as pltpu
from jax.sharding import PartitionSpec as P

AXES = ("grp", "ex", "dim")
NT = (((1,), (1,)), ((), ()))
VMEM = pl.BlockSpec(memory_space=pltpu.VMEM)
SMEM = pl.BlockSpec(memory_space=pltpu.SMEM)
HBM = pl.BlockSpec(memory_space=pltpu.HBM)
ANY = pl.BlockSpec(memory_space=pl.ANY)


def limit(mib):
    return pltpu.CompilerParams(vmem_limit_bytes=mib * 1024 * 1024)


def per_device_any(queries, inverse_fisher, stored_grads):
    term_block = jnp.dot(queries, inverse_fisher, preferred_element_type=jnp.float32)
    own_panel = lax.psum_scatter(term_block, "ex", scatter_dimension=1, tiled=True).astype(
        jnp.bfloat16
    )
    partial_scores = lax.dot_general(
        lax.all_gather(own_panel, "ex", axis=1, tiled=True),
        stored_grads,
        NT,
        preferred_element_type=jnp.float32,
    )
    return lax.psum_scatter(partial_scores, "dim", scatter_dimension=0, tiled=True)


def scalar(value):
    return jnp.asarray(value, jnp.int32).reshape(1)


ORDER = (0, 2, 1, 3)


def half_copies(fisher_ref, block, half, held_ref, sem):
    steps = sem.shape[0]
    rows, width = held_ref.shape
    step = rows // steps
    columns = pl.ds(pl.multiple_of(block * width, width), width)
    copies = []
    for i in range(steps):
        copies.append(
            pltpu.make_async_copy(
                fisher_ref.at[pl.ds(half * rows + i * step, step), columns],
                held_ref.at[pl.ds(i * step, step), :],
                sem.at[i],
            )
        )
    return copies


def times(chunk_ref, fisher):
    return lax.dot_general(chunk_ref[...], fisher, NT, preferred_element_type=jnp.float32)


def fisher_kernel(n_in, has_base, fetch, *refs):
    if fetch:
        at_ref, fisher_ref, *refs = refs
    chunk_ref, halves = (refs[0], refs[1:3]) if n_in else (None, ())
    base_ref = refs[3] if has_base else None
    outs, sem = refs[n_in + has_base : -1], refs[-1]
    held = outs[1:] if n_in else outs
    copies = []
    for k, (piece, half) in enumerate(fetch):
        for copy in half_copies(fisher_ref, at_ref[0] ^ ORDER[piece], half, held[k], sem.at[k]):
            copy.start()
            copies.append(copy)

    def product(h, start, step):
        columns = pl.ds(h * halves[h].shape[0] + start, step)
        term = times(chunk_ref, halves[h][pl.ds(start, step), :])
        outs[0][:, columns] = term + base_ref[:, columns] if has_base else term

    for h, half_ref in enumerate(halves):
        rows = half_ref.shape[0]
        if fetch:

            @pl.loop(0, 2)
            def _(i):
                product(h, pl.multiple_of(i * (rows // 2), rows // 2), rows // 2)
        else:
            product(h, 0, rows)

    for copy in copies:
        copy.wait()


def fisher_step(fisher, first, width, fetch, chunk=None, halves=(), base=None):
    rows = fisher.shape[0]
    ins = [] if chunk is None else [chunk, *halves]
    has_base = base is not None
    held = jax.ShapeDtypeStruct((rows // 2, width), fisher.dtype)
    out_shape = [] if chunk is None else [jax.ShapeDtypeStruct((chunk.shape[0], rows), jnp.float32)]
    out_shape += [held] * len(fetch)
    return pl.pallas_call(
        functools.partial(fisher_kernel, len(ins), has_base, fetch),
        out_shape=out_shape,
        in_specs=[SMEM, HBM][: 2 * bool(fetch)] + [VMEM] * (len(ins) + has_base),
        out_specs=[VMEM] * len(out_shape),
        scratch_shapes=[pltpu.SemaphoreType.DMA((max(len(fetch), 1), 2))],
        compiler_params=limit(34 if chunk is None else 20),
        cost_estimate=pl.CostEstimate(
            flops=0 if chunk is None else 2 * chunk.shape[0] * width * rows,
            bytes_accessed=width * rows * (len(fetch) + 2 * bool(ins)),
            transcendentals=0,
        ),
    )(*((scalar(first), fisher) if fetch else ()), *ins, *([base] if has_base else []))


def score_kernel(order, has_base, at_ref, *refs):
    n = len(order)
    grads_ref, out_ref = refs[n], refs[-1]
    width = refs[0].shape[1]
    total = refs[n + 1][...] if has_base else None
    for k in range(n):
        start = pl.multiple_of((at_ref[0] ^ order[k]) * width, width)
        term = times(refs[k], grads_ref[:, pl.ds(start, width)])
        total = term if total is None else total + term
    out_ref[...] = total


def score_dot(pieces, order, first, grads, base=None):
    n = len(pieces)
    rows, width = pieces[0].shape
    operands = [*pieces, grads] + ([] if base is None else [base])
    return pl.pallas_call(
        functools.partial(score_kernel, order, base is not None),
        out_shape=jax.ShapeDtypeStruct((rows, grads.shape[0]), jnp.float32),
        in_specs=[SMEM] + [VMEM] * len(operands),
        out_specs=VMEM,
        compiler_params=limit(8),
        cost_estimate=pl.CostEstimate(
            flops=2 * n * rows * width * grads.shape[0],
            bytes_accessed=2 * n * width * grads.shape[0],
            transcendentals=0,
        ),
    )(scalar(first), *operands)


def pick_kernel(at_ref, a_ref, b_ref, *refs):
    out_ref = refs[-1]

    @pl.when(at_ref[0] == 1)
    def _():
        out_ref[...] = a_ref[...]

    @pl.when(at_ref[0] != 1)
    def _():
        out_ref[...] = b_ref[...]


def pick(condition, a, b, after=()):
    return pl.pallas_call(
        pick_kernel,
        out_shape=jax.ShapeDtypeStruct(a.shape, a.dtype),
        in_specs=[SMEM] + [VMEM] * 2 + [ANY] * len(after),
        out_specs=VMEM,
        compiler_params=limit(2),
        cost_estimate=pl.CostEstimate(flops=0, bytes_accessed=2 * a.size * 2, transcendentals=0),
    )(scalar(condition), a, b, *after)


def per_device_quad(nz, nx, ny, queries, inverse_fisher, stored_grads):
    nex = nz * nx
    near = nz // 2
    nq = queries.shape[0]
    y, e, d = (lax.axis_index(a) for a in AXES)
    z = e // nx
    x = e % nx
    u = jnp.where(d == 0, z, nz - 1 - z)
    owner = u < near

    def move(value, target):
        pairs = []
        for sy in range(ny):
            for sz in range(nz):
                for sx in range(nx):
                    for sd in range(2):
                        to = target(sy, sz, sx, sd)
                        if to is not None:
                            ty, tz, tx, td = to
                            pairs.append(((sy * nex + sz * nx + sx) * 2 + sd, (ty * nex + tz * nx + tx) * 2 + td))
        return lax.ppermute(value, AXES, pairs)

    def along_z(value, hops, flip=False):
        def target(sy, sz, sx, sd):
            su = sz if sd == 0 else nz - 1 - sz
            if su not in hops:
                return None
            tu = hops[su]
            return sy, tu if sd == 0 else nz - 1 - tu, 1 - sx if flip else sx, sd

        return move(value, target)

    def swap_y(value):
        return move(value, lambda sy, sz, sx, sd: (1 - sy, sz, sx, sd))

    def swap_core(value):
        return move(value, lambda sy, sz, sx, sd: (sy, sz, sx, 1 - sd))

    def gather(own, after=()):
        def start(sy, sz, sx, sd):
            su = sz if sd == 0 else nz - 1 - sz
            if su < near:
                return sy, sz + 2 if sd == 0 else sz - 2, sx, sd
            return sy, sz ^ 1, 1 - sx, 1 - sd

        came = move(own, start)
        first = pick(owner, own, came, after)
        pairs = {0: 1, 1: 0, 2: 3, 3: 2}
        beside = along_z(first, pairs)
        across = along_z(first, {0: 0, 1: 1, 2: 2, 3: 3}, True)
        diagonal = along_z(first, {2: 3, 3: 2}, True)

        def corner(after):
            ready, _ = lax.optimization_barrier((came, after))
            return pick(owner, ready, diagonal)

        return first, beside, across, corner

    plane = jnp.where(d == 0, u % 2, nz - 1 - u % 2)
    column = plane * nx + x - d * (nex // 2)

    other_grads = swap_y(stored_grads)

    rows = nq // ny
    own = lax.optimization_barrier(lax.dynamic_slice_in_dim(queries, y * rows, rows, axis=0))
    step = functools.partial(fisher_step, inverse_fisher, column, own.shape[1])
    a0, a1, b0, b1 = step(((0, 0), (0, 1), (1, 0), (1, 1)))
    q0, q1, q2, corner = gather(own, (a0,))
    total, c0, c1 = step(((2, 0), (2, 1)), q0, (a0, a1))
    total, d0 = step(((3, 0),), q1, (b0, b1), total)
    total, d1 = step(((3, 1),), q2, (c0, c1), total)
    (total,) = step((), corner(total), (d0, d1), total)
    panel = (total + swap_core(total)).astype(jnp.bfloat16)

    p0, p1, p2, corner = gather(panel)
    p3 = corner(panel)
    mine = score_dot([p0, p1], ORDER[:2], column, stored_grads)
    p2, _ = lax.optimization_barrier((p2, mine))
    other = score_dot([p0, p1, p2], ORDER[:3], column, other_grads)
    p3, _ = lax.optimization_barrier((p3, other))
    other = score_dot([p3], ORDER[3:], column, other_grads, other)
    p2, p3, mine, _ = lax.optimization_barrier((p2, p3, mine, other))
    mine = score_dot([p2, p3], ORDER[2:], column, stored_grads, mine)

    other = swap_y(other)
    keep = jnp.where(d == y, mine, other)
    give = jnp.where(d == y, other, mine)
    return keep + swap_core(give)


def solution(mesh):
    coords = [getattr(device, "coords", None) for device in mesh.devices.flat]
    nx = 2 if None in coords else len({c[0] for c in coords})
    nz = mesh.shape["ex"] // nx
    ny = mesh.shape["grp"]
    if (nz, nx, ny) == (4, 2, 2):
        body = functools.partial(per_device_quad, nz, nx, ny)
    else:
        body = per_device_any
    return jax.shard_map(
        body,
        mesh=mesh,
        in_specs=(P(None, "ex"), P("ex", "dim"), P(("grp", "ex"), "dim")),
        out_specs=P("dim", ("grp", "ex")),
        check_vma=False,
    )
```

```python
import functools

import jax
import jax.numpy as jnp
from jax import lax
from jax.experimental import pallas as pl
from jax.experimental.pallas import tpu as pltpu
from jax.sharding import PartitionSpec as P

AXES = ("grp", "ex", "dim")
NT = (((1,), (1,)), ((), ()))
VMEM = pl.BlockSpec(memory_space=pltpu.VMEM)
SMEM = pl.BlockSpec(memory_space=pltpu.SMEM)
HBM = pl.BlockSpec(memory_space=pltpu.HBM)
ANY = pl.BlockSpec(memory_space=pl.ANY)


def limit(mib):
    return pltpu.CompilerParams(vmem_limit_bytes=mib * 1024 * 1024)


def per_device_any(queries, inverse_fisher, stored_grads):
    term_block = jnp.dot(queries, inverse_fisher, preferred_element_type=jnp.float32)
    own_panel = lax.psum_scatter(term_block, "ex", scatter_dimension=1, tiled=True).astype(
        jnp.bfloat16
    )
    partial_scores = lax.dot_general(
        lax.all_gather(own_panel, "ex", axis=1, tiled=True),
        stored_grads,
        NT,
        preferred_element_type=jnp.float32,
    )
    return lax.psum_scatter(partial_scores, "dim", scatter_dimension=0, tiled=True)


def scalar(value):
    return jnp.asarray(value, jnp.int32).reshape(1)


ORDER = (0, 2, 1, 3)


def half_copies(fisher_ref, block, half, held_ref, sem):
    steps = sem.shape[0]
    rows, width = held_ref.shape
    step = rows // steps
    columns = pl.ds(pl.multiple_of(block * width, width), width)
    copies = []
    for i in range(steps):
        copies.append(
            pltpu.make_async_copy(
                fisher_ref.at[pl.ds(half * rows + i * step, step), columns],
                held_ref.at[pl.ds(i * step, step), :],
                sem.at[i],
            )
        )
    return copies


def times(chunk_ref, fisher):
    return lax.dot_general(chunk_ref[...], fisher, NT, preferred_element_type=jnp.float32)


def fisher_kernel(n_in, has_base, fetch, *refs):
    if fetch:
        at_ref, fisher_ref, *refs = refs
    chunk_ref, halves = (refs[0], refs[1:3]) if n_in else (None, ())
    base_ref = refs[3] if has_base else None
    outs, sem = refs[n_in + has_base : -1], refs[-1]
    held = outs[1:] if n_in else outs
    copies = []
    for k, (piece, half) in enumerate(fetch):
        for copy in half_copies(fisher_ref, at_ref[0] ^ ORDER[piece], half, held[k], sem.at[k]):
            copy.start()
            copies.append(copy)

    def product(h, start, step):
        columns = pl.ds(h * halves[h].shape[0] + start, step)
        term = times(chunk_ref, halves[h][pl.ds(start, step), :])
        outs[0][:, columns] = term + base_ref[:, columns] if has_base else term

    for h, half_ref in enumerate(halves):
        rows = half_ref.shape[0]
        if fetch:

            @pl.loop(0, 2)
            def _(i):
                product(h, pl.multiple_of(i * (rows // 2), rows // 2), rows // 2)
        else:
            product(h, 0, rows)

    for copy in copies:
        copy.wait()


def fisher_step(fisher, first, width, fetch, chunk=None, halves=(), base=None):
    rows = fisher.shape[0]
    ins = [] if chunk is None else [chunk, *halves]
    has_base = base is not None
    held = jax.ShapeDtypeStruct((rows // 2, width), fisher.dtype)
    out_shape = [] if chunk is None else [jax.ShapeDtypeStruct((chunk.shape[0], rows), jnp.float32)]
    out_shape += [held] * len(fetch)
    return pl.pallas_call(
        functools.partial(fisher_kernel, len(ins), has_base, fetch),
        out_shape=out_shape,
        in_specs=[SMEM, HBM][: 2 * bool(fetch)] + [VMEM] * (len(ins) + has_base),
        out_specs=[VMEM] * len(out_shape),
        scratch_shapes=[pltpu.SemaphoreType.DMA((max(len(fetch), 1), 2))],
        compiler_params=limit(34 if chunk is None else 20),
        cost_estimate=pl.CostEstimate(
            flops=0 if chunk is None else 2 * chunk.shape[0] * width * rows,
            bytes_accessed=width * rows * (len(fetch) + 2 * bool(ins)),
            transcendentals=0,
        ),
    )(*((scalar(first), fisher) if fetch else ()), *ins, *([base] if has_base else []))


def score_kernel(order, relative, has_base, at_ref, *refs):
    n = len(order)
    grads_ref, out_ref = refs[n], refs[-1]
    width = refs[0].shape[1]
    total = refs[n + 1][...] if has_base else None
    for k in range(n):
        block = at_ref[0] ^ order[k] if relative else order[k]
        start = pl.multiple_of(block * width, width)
        term = times(refs[k], grads_ref[:, pl.ds(start, width)])
        total = term if total is None else total + term
    out_ref[...] = total


def score_dot(pieces, order, first, grads, base=None):
    n = len(pieces)
    rows, width = pieces[0].shape
    operands = [*pieces, grads] + ([] if base is None else [base])
    return pl.pallas_call(
        functools.partial(score_kernel, order, first is not None, base is not None),
        out_shape=jax.ShapeDtypeStruct((rows, grads.shape[0]), jnp.float32),
        in_specs=[SMEM] + [VMEM] * len(operands),
        out_specs=VMEM,
        compiler_params=limit(8),
        cost_estimate=pl.CostEstimate(
            flops=2 * n * rows * width * grads.shape[0],
            bytes_accessed=2 * n * width * grads.shape[0],
            transcendentals=0,
        ),
    )(scalar(0 if first is None else first), *operands)


def cut_kernel(order, at_ref, src_ref, out_ref, sem):
    width = out_ref.shape[1] // len(order)
    copies = []
    for k, mask in enumerate(order):
        start = pl.multiple_of((at_ref[0] ^ mask) * width, width)
        copies.append(
            pltpu.make_async_copy(
                src_ref.at[:, pl.ds(start, width)], out_ref.at[:, k * width : (k + 1) * width], sem.at[k]
            )
        )
        copies[-1].start()
    for copy in copies:
        copy.wait()


def cut(src, order, first, width):
    n = len(order)
    return pl.pallas_call(
        functools.partial(cut_kernel, order),
        out_shape=jax.ShapeDtypeStruct((src.shape[0], n * width), src.dtype),
        in_specs=[SMEM, HBM],
        out_specs=VMEM,
        scratch_shapes=[pltpu.SemaphoreType.DMA((n,))],
        compiler_params=limit(51),
        cost_estimate=pl.CostEstimate(
            flops=0, bytes_accessed=2 * n * width * src.shape[0], transcendentals=0
        ),
    )(scalar(first), src)


def pick_kernel(at_ref, a_ref, b_ref, *refs):
    out_ref = refs[-1]

    @pl.when(at_ref[0] == 1)
    def _():
        out_ref[...] = a_ref[...]

    @pl.when(at_ref[0] != 1)
    def _():
        out_ref[...] = b_ref[...]


def pick(condition, a, b, after=()):
    return pl.pallas_call(
        pick_kernel,
        out_shape=jax.ShapeDtypeStruct(a.shape, a.dtype),
        in_specs=[SMEM] + [VMEM] * 2 + [ANY] * len(after),
        out_specs=VMEM,
        compiler_params=limit(2),
        cost_estimate=pl.CostEstimate(flops=0, bytes_accessed=2 * a.size * 2, transcendentals=0),
    )(scalar(condition), a, b, *after)


def per_device_quad(nz, nx, ny, queries, inverse_fisher, stored_grads):
    nex = nz * nx
    near = nz // 2
    nq = queries.shape[0]
    y, e, d = (lax.axis_index(a) for a in AXES)
    z = e // nx
    x = e % nx
    u = jnp.where(d == 0, z, nz - 1 - z)
    owner = u < near

    def move(value, target):
        pairs = []
        for sy in range(ny):
            for sz in range(nz):
                for sx in range(nx):
                    for sd in range(2):
                        to = target(sy, sz, sx, sd)
                        if to is not None:
                            ty, tz, tx, td = to
                            pairs.append(((sy * nex + sz * nx + sx) * 2 + sd, (ty * nex + tz * nx + tx) * 2 + td))
        return lax.ppermute(value, AXES, pairs)

    def along_z(value, hops, flip=False):
        def target(sy, sz, sx, sd):
            su = sz if sd == 0 else nz - 1 - sz
            if su not in hops:
                return None
            tu = hops[su]
            return sy, tu if sd == 0 else nz - 1 - tu, 1 - sx if flip else sx, sd

        return move(value, target)

    def swap_y(value):
        return move(value, lambda sy, sz, sx, sd: (1 - sy, sz, sx, sd))

    def swap_core(value):
        return move(value, lambda sy, sz, sx, sd: (sy, sz, sx, 1 - sd))

    def gather(own, direct, after=()):
        def start(sy, sz, sx, sd):
            su = sz if sd == 0 else nz - 1 - sz
            if su < near:
                return sy, sz + 2 if sd == 0 else sz - 2, sx, sd
            return sy, sz ^ 1, 1 - sx, 1 - sd

        came = move(own, start)
        if direct:
            corner = along_z(own, {0: 3, 1: 2}, True)
        first = pick(owner, own, came, after)
        beside = along_z(first, {0: 1, 1: 0, 2: 3, 3: 2})
        if direct:
            beside, corner = lax.optimization_barrier((beside, corner))
        across = along_z(first, {0: 0, 1: 1, 2: 2, 3: 3}, True)

        def last(after):
            if direct:
                piece, _ = lax.optimization_barrier((corner, after))
            else:
                ready, _ = lax.optimization_barrier((beside, after))
                piece = along_z(ready, {2: 2, 3: 3}, True)
            return pick(owner, came, piece)

        return first, beside, across, last

    plane = jnp.where(d == 0, u % 2, nz - 1 - u % 2)
    column = plane * nx + x - d * (nex // 2)

    rows, width = nq // ny, queries.shape[1]
    to_y = cut(stored_grads, ORDER[1:], column, width)
    queries, to_y = lax.optimization_barrier((queries, to_y))
    own = lax.dynamic_slice_in_dim(queries, y * rows, rows, axis=0)
    own, to_y = lax.optimization_barrier((own, to_y))
    other_grads = swap_y(to_y)
    step = functools.partial(fisher_step, inverse_fisher, column, width)
    a0, a1, b0, b1 = step(((0, 0), (0, 1), (1, 0), (1, 1)))
    q0, q1, q2, last = gather(own, False, (a0,))
    total, c0, c1 = step(((2, 0), (2, 1)), q0, (a0, a1))
    total, d0 = step(((3, 0),), q1, (b0, b1), total)
    q3 = last(total)
    total, d1 = step(((3, 1),), q2, (c0, c1), total)
    (total,) = step((), q3, (d0, d1), total)
    panel = (total + swap_core(total)).astype(jnp.bfloat16)

    p0, p1, p2, last = gather(panel, True, (other_grads,))
    swapped = swap_y(p0)
    mine = score_dot([p0, p1], ORDER[:2], column, stored_grads)
    p2, _ = lax.optimization_barrier((p2, mine))
    other = score_dot([p1, p2], (0, 1), None, other_grads)
    p3 = last(other)
    other = score_dot([p3], (2,), None, other_grads, other)
    p2, p3, mine, swapped, _ = lax.optimization_barrier((p2, p3, mine, swapped, other))
    mine = score_dot([p2, p3], ORDER[2:], column, stored_grads, mine)
    theirs = score_dot([swapped], ORDER[:1], column, stored_grads)

    other = swap_y(other) + theirs
    keep = jnp.where(d == y, mine, other)
    give = jnp.where(d == y, other, mine)
    return keep + swap_core(give)


def solution(mesh):
    coords = [getattr(device, "coords", None) for device in mesh.devices.flat]
    nx = 2 if None in coords else len({c[0] for c in coords})
    nz = mesh.shape["ex"] // nx
    ny = mesh.shape["grp"]
    if (nz, nx, ny) == (4, 2, 2):
        body = functools.partial(per_device_quad, nz, nx, ny)
    else:
        body = per_device_any
    return jax.shard_map(
        body,
        mesh=mesh,
        in_specs=(P(None, "ex"), P("ex", "dim"), P(("grp", "ex"), "dim")),
        out_specs=P("dim", ("grp", "ex")),
        check_vma=False,
    )
```

```python
import functools

import jax
import jax.numpy as jnp
from jax import lax
from jax.experimental import pallas as pl
from jax.experimental.pallas import tpu as pltpu
from jax.sharding import PartitionSpec as P

AXES = ("grp", "ex", "dim")
NT = (((1,), (1,)), ((), ()))
VMEM = pl.BlockSpec(memory_space=pltpu.VMEM)
SMEM = pl.BlockSpec(memory_space=pltpu.SMEM)
HBM = pl.BlockSpec(memory_space=pltpu.HBM)
ANY = pl.BlockSpec(memory_space=pl.ANY)


def limit(mib):
    return pltpu.CompilerParams(vmem_limit_bytes=mib * 1024 * 1024)


def per_device_any(queries, inverse_fisher, stored_grads):
    term_block = jnp.dot(queries, inverse_fisher, preferred_element_type=jnp.float32)
    own_panel = lax.psum_scatter(term_block, "ex", scatter_dimension=1, tiled=True).astype(
        jnp.bfloat16
    )
    partial_scores = lax.dot_general(
        lax.all_gather(own_panel, "ex", axis=1, tiled=True),
        stored_grads,
        NT,
        preferred_element_type=jnp.float32,
    )
    return lax.psum_scatter(partial_scores, "dim", scatter_dimension=0, tiled=True)


def scalar(value):
    return jnp.asarray(value, jnp.int32).reshape(1)


ORDER = (0, 2, 1, 3)


def half_copies(fisher_ref, block, half, held_ref, sem):
    steps = sem.shape[0]
    rows, width = held_ref.shape
    step = rows // steps
    columns = pl.ds(pl.multiple_of(block * width, width), width)
    copies = []
    for i in range(steps):
        copies.append(
            pltpu.make_async_copy(
                fisher_ref.at[pl.ds(half * rows + i * step, step), columns],
                held_ref.at[pl.ds(i * step, step), :],
                sem.at[i],
            )
        )
    return copies


def times(chunk_ref, fisher):
    return lax.dot_general(chunk_ref[...], fisher, NT, preferred_element_type=jnp.float32)


def fisher_kernel(n_in, has_base, fetch, *refs):
    if fetch:
        at_ref, fisher_ref, *refs = refs
    chunk_ref, halves = (refs[0], refs[1:3]) if n_in else (None, ())
    base_ref = refs[3] if has_base else None
    outs, sem = refs[n_in + has_base : -1], refs[-1]
    held = outs[1:] if n_in else outs
    copies = []
    for k, (piece, half) in enumerate(fetch):
        for copy in half_copies(fisher_ref, at_ref[0] ^ ORDER[piece], half, held[k], sem.at[k]):
            copy.start()
            copies.append(copy)

    def product(h, start, step):
        columns = pl.ds(h * halves[h].shape[0] + start, step)
        term = times(chunk_ref, halves[h][pl.ds(start, step), :])
        outs[0][:, columns] = term + base_ref[:, columns] if has_base else term

    for h, half_ref in enumerate(halves):
        rows = half_ref.shape[0]
        if fetch:

            @pl.loop(0, 2)
            def _(i):
                product(h, pl.multiple_of(i * (rows // 2), rows // 2), rows // 2)
        else:
            product(h, 0, rows)

    for copy in copies:
        copy.wait()


def fisher_step(fisher, first, width, fetch, chunk=None, halves=(), base=None):
    rows = fisher.shape[0]
    ins = [] if chunk is None else [chunk, *halves]
    has_base = base is not None
    held = jax.ShapeDtypeStruct((rows // 2, width), fisher.dtype)
    out_shape = [] if chunk is None else [jax.ShapeDtypeStruct((chunk.shape[0], rows), jnp.float32)]
    out_shape += [held] * len(fetch)
    return pl.pallas_call(
        functools.partial(fisher_kernel, len(ins), has_base, fetch),
        out_shape=out_shape,
        in_specs=[SMEM, HBM][: 2 * bool(fetch)] + [VMEM] * (len(ins) + has_base),
        out_specs=[VMEM] * len(out_shape),
        scratch_shapes=[pltpu.SemaphoreType.DMA((max(len(fetch), 1), 2))],
        compiler_params=limit(34 if chunk is None else 20),
        cost_estimate=pl.CostEstimate(
            flops=0 if chunk is None else 2 * chunk.shape[0] * width * rows,
            bytes_accessed=width * rows * (len(fetch) + 2 * bool(ins)),
            transcendentals=0,
        ),
    )(*((scalar(first), fisher) if fetch else ()), *ins, *([base] if has_base else []))


def score_kernel(order, has_base, at_ref, *refs):
    n = len(order)
    grads_ref, out_ref = refs[n], refs[-1]
    width = refs[0].shape[1]
    total = refs[n + 1][...] if has_base else None
    for k in range(n):
        start = pl.multiple_of((at_ref[0] ^ order[k]) * width, width)
        term = times(refs[k], grads_ref[:, pl.ds(start, width)])
        total = term if total is None else total + term
    out_ref[...] = total


def score_dot(pieces, order, first, grads, base=None):
    n = len(pieces)
    rows, width = pieces[0].shape
    operands = [*pieces, grads] + ([] if base is None else [base])
    return pl.pallas_call(
        functools.partial(score_kernel, order, base is not None),
        out_shape=jax.ShapeDtypeStruct((rows, grads.shape[0]), jnp.float32),
        in_specs=[SMEM] + [VMEM] * len(operands),
        out_specs=VMEM,
        compiler_params=limit(8),
        cost_estimate=pl.CostEstimate(
            flops=2 * n * rows * width * grads.shape[0],
            bytes_accessed=2 * n * width * grads.shape[0],
            transcendentals=0,
        ),
    )(scalar(first), *operands)


def pick_kernel(at_ref, a_ref, b_ref, *refs):
    out_ref = refs[-1]

    @pl.when(at_ref[0] == 1)
    def _():
        out_ref[...] = a_ref[...]

    @pl.when(at_ref[0] != 1)
    def _():
        out_ref[...] = b_ref[...]


def pick(condition, a, b, after=()):
    return pl.pallas_call(
        pick_kernel,
        out_shape=jax.ShapeDtypeStruct(a.shape, a.dtype),
        in_specs=[SMEM] + [VMEM] * 2 + [ANY] * len(after),
        out_specs=VMEM,
        compiler_params=limit(2),
        cost_estimate=pl.CostEstimate(flops=0, bytes_accessed=2 * a.size * 2, transcendentals=0),
    )(scalar(condition), a, b, *after)


def per_device_quad(nz, nx, ny, queries, inverse_fisher, stored_grads):
    nex = nz * nx
    near = nz // 2
    nq = queries.shape[0]
    y, e, d = (lax.axis_index(a) for a in AXES)
    z = e // nx
    x = e % nx
    u = jnp.where(d == 0, z, nz - 1 - z)
    owner = u < near

    def move(value, target):
        pairs = []
        for sy in range(ny):
            for sz in range(nz):
                for sx in range(nx):
                    for sd in range(2):
                        to = target(sy, sz, sx, sd)
                        if to is not None:
                            ty, tz, tx, td = to
                            pairs.append(((sy * nex + sz * nx + sx) * 2 + sd, (ty * nex + tz * nx + tx) * 2 + td))
        return lax.ppermute(value, AXES, pairs)

    def along_z(value, hops, flip=False):
        def target(sy, sz, sx, sd):
            su = sz if sd == 0 else nz - 1 - sz
            if su not in hops:
                return None
            tu = hops[su]
            return sy, tu if sd == 0 else nz - 1 - tu, 1 - sx if flip else sx, sd

        return move(value, target)

    def swap_y(value):
        return move(value, lambda sy, sz, sx, sd: (1 - sy, sz, sx, sd))

    def swap_core(value):
        return move(value, lambda sy, sz, sx, sd: (sy, sz, sx, 1 - sd))

    def gather(own, direct, after=()):
        def start(sy, sz, sx, sd):
            su = sz if sd == 0 else nz - 1 - sz
            if su < near:
                return sy, sz + 2 if sd == 0 else sz - 2, sx, sd
            return sy, sz ^ 1, 1 - sx, 1 - sd

        came = move(own, start)
        if direct:
            corner = along_z(own, {0: 3, 1: 2}, True)
        first = pick(owner, own, came, after)
        pairs = {0: 1, 1: 0, 2: 3, 3: 2}
        beside = along_z(first, pairs)
        across = along_z(first, {0: 0, 1: 1, 2: 2, 3: 3}, True)
        if direct:
            beside, corner = lax.optimization_barrier((beside, corner))
        else:
            corner = along_z(first, {2: 3, 3: 2}, True)

        def last(after):
            ready, _ = lax.optimization_barrier((came, after))
            return pick(owner, ready, corner)

        return first, beside, across, last

    plane = jnp.where(d == 0, u % 2, nz - 1 - u % 2)
    column = plane * nx + x - d * (nex // 2)

    other_grads = swap_y(stored_grads)

    rows = nq // ny
    own = lax.optimization_barrier(lax.dynamic_slice_in_dim(queries, y * rows, rows, axis=0))
    step = functools.partial(fisher_step, inverse_fisher, column, own.shape[1])
    a0, a1, b0, b1 = step(((0, 0), (0, 1), (1, 0), (1, 1)))
    q0, q1, q2, last = gather(own, False, (a0,))
    total, c0, c1 = step(((2, 0), (2, 1)), q0, (a0, a1))
    total, d0 = step(((3, 0),), q1, (b0, b1), total)
    total, d1 = step(((3, 1),), q2, (c0, c1), total)
    (total,) = step((), last(total), (d0, d1), total)
    panel = (total + swap_core(total)).astype(jnp.bfloat16)

    p0, p1, p2, last = gather(panel, True)
    p3 = last(panel)
    mine = score_dot([p0, p1], ORDER[:2], column, stored_grads)
    p2, _ = lax.optimization_barrier((p2, mine))
    other = score_dot([p0, p1, p2], ORDER[:3], column, other_grads)
    p3, _ = lax.optimization_barrier((p3, other))
    other = score_dot([p3], ORDER[3:], column, other_grads, other)
    p2, p3, mine, _ = lax.optimization_barrier((p2, p3, mine, other))
    mine = score_dot([p2, p3], ORDER[2:], column, stored_grads, mine)

    other = swap_y(other)
    keep = jnp.where(d == y, mine, other)
    give = jnp.where(d == y, other, mine)
    return keep + swap_core(give)


def solution(mesh):
    coords = [getattr(device, "coords", None) for device in mesh.devices.flat]
    nx = 2 if None in coords else len({c[0] for c in coords})
    nz = mesh.shape["ex"] // nx
    ny = mesh.shape["grp"]
    if (nz, nx, ny) == (4, 2, 2):
        body = functools.partial(per_device_quad, nz, nx, ny)
    else:
        body = per_device_any
    return jax.shard_map(
        body,
        mesh=mesh,
        in_specs=(P(None, "ex"), P("ex", "dim"), P(("grp", "ex"), "dim")),
        out_specs=P("dim", ("grp", "ex")),
        check_vma=False,
    )
```

```python
import functools

import jax
import jax.numpy as jnp
from jax import lax
from jax.experimental import pallas as pl
from jax.experimental.pallas import tpu as pltpu
from jax.sharding import PartitionSpec as P

AXES = ("grp", "ex", "dim")
NT = (((1,), (1,)), ((), ()))
VMEM = pl.BlockSpec(memory_space=pltpu.VMEM)
HBM = pl.BlockSpec(memory_space=pltpu.HBM)
ANY = pl.BlockSpec(memory_space=pl.ANY)


def limit(mib):
    return pltpu.CompilerParams(vmem_limit_bytes=mib * 1024 * 1024)


def per_device_any(queries, inverse_fisher, stored_grads):
    term_block = jnp.dot(queries, inverse_fisher, preferred_element_type=jnp.float32)
    own_panel = lax.psum_scatter(term_block, "ex", scatter_dimension=1, tiled=True).astype(
        jnp.bfloat16
    )
    partial_scores = lax.dot_general(
        lax.all_gather(own_panel, "ex", axis=1, tiled=True),
        stored_grads,
        NT,
        preferred_element_type=jnp.float32,
    )
    return lax.psum_scatter(partial_scores, "dim", scatter_dimension=0, tiled=True)


class Place:
    def __init__(self, nz, nx):
        self.y, e, self.d = (lax.axis_index(a) for a in AXES)
        z, x = lax.div(e, nx), lax.rem(e, nx)
        u = jnp.where(self.d == 0, z, nz - 1 - z)
        self.owner = u < nz // 2
        local = jnp.where(self.d == 0, lax.rem(u, 2), nz // 2 - 1 - lax.rem(u, 2))
        self.column = local * nx + x


ORDER = (0, 2, 1, 3)


def half_copies(fisher_ref, block, half, held_ref, sem):
    steps = sem.shape[0]
    rows, width = held_ref.shape
    step = rows // steps
    columns = pl.ds(pl.multiple_of(block * width, width), width)
    copies = []
    for i in range(steps):
        copies.append(
            pltpu.make_async_copy(
                fisher_ref.at[pl.ds(half * rows + i * step, step), columns],
                held_ref.at[pl.ds(i * step, step), :],
                sem.at[i],
            )
        )
    return copies


def times(chunk_ref, fisher):
    return lax.dot_general(chunk_ref[...], fisher, NT, preferred_element_type=jnp.float32)


def fisher_kernel(dims, n_in, has_base, fetch, *refs):
    if fetch:
        column = Place(*dims).column
        fisher_ref, *refs = refs
    chunk_ref, halves = (refs[0], refs[1:3]) if n_in else (None, ())
    base_ref = refs[3] if has_base else None
    outs, sem = refs[n_in + has_base : -1], refs[-1]
    held = outs[1:] if n_in else outs
    copies = []
    for k, (piece, half) in enumerate(fetch):
        for copy in half_copies(fisher_ref, column ^ ORDER[piece], half, held[k], sem.at[k]):
            copy.start()
            copies.append(copy)

    def product(h, start, step):
        columns = pl.ds(h * halves[h].shape[0] + start, step)
        term = times(chunk_ref, halves[h][pl.ds(start, step), :])
        outs[0][:, columns] = term + base_ref[:, columns] if has_base else term

    for h, half_ref in enumerate(halves):
        rows = half_ref.shape[0]
        if fetch:

            @pl.loop(0, 2)
            def _(i):
                product(h, pl.multiple_of(i * (rows // 2), rows // 2), rows // 2)
        else:
            product(h, 0, rows)

    for copy in copies:
        copy.wait()


def fisher_step(fisher, dims, width, fetch, chunk=None, halves=(), base=None):
    rows = fisher.shape[0]
    ins = [] if chunk is None else [chunk, *halves]
    has_base = base is not None
    held = jax.ShapeDtypeStruct((rows // 2, width), fisher.dtype)
    out_shape = [] if chunk is None else [jax.ShapeDtypeStruct((chunk.shape[0], rows), jnp.float32)]
    out_shape += [held] * len(fetch)
    return pl.pallas_call(
        functools.partial(fisher_kernel, dims, len(ins), has_base, fetch),
        out_shape=out_shape,
        in_specs=[HBM] * bool(fetch) + [VMEM] * (len(ins) + has_base),
        out_specs=[VMEM] * len(out_shape),
        scratch_shapes=[pltpu.SemaphoreType.DMA((max(len(fetch), 1), 2))],
        compiler_params=limit(34 if chunk is None else 20),
        cost_estimate=pl.CostEstimate(
            flops=0 if chunk is None else 2 * chunk.shape[0] * width * rows,
            bytes_accessed=width * rows * (len(fetch) + 2 * bool(ins)),
            transcendentals=0,
        ),
    )(*([fisher] if fetch else []), *ins, *([base] if has_base else []))


def score_kernel(dims, order, has_base, *refs):
    n = len(order)
    column = Place(*dims).column if dims else 0
    grads_ref, out_ref = refs[n], refs[-1]
    width = refs[0].shape[1]
    total = refs[n + 1][...] if has_base else None
    for k in range(n):
        block = column ^ order[k]
        start = pl.multiple_of(block * width, width) if dims else block * width
        term = times(refs[k], grads_ref[:, pl.ds(start, width)])
        total = term if total is None else total + term
    out_ref[...] = total


def score_dot(pieces, order, dims, grads, base=None):
    n = len(pieces)
    rows, width = pieces[0].shape
    operands = [*pieces, grads] + ([] if base is None else [base])
    return pl.pallas_call(
        functools.partial(score_kernel, dims, order, base is not None),
        out_shape=jax.ShapeDtypeStruct((rows, grads.shape[0]), jnp.float32),
        in_specs=[VMEM] * len(operands),
        out_specs=VMEM,
        compiler_params=limit(8),
        cost_estimate=pl.CostEstimate(
            flops=2 * n * rows * width * grads.shape[0],
            bytes_accessed=2 * n * width * grads.shape[0],
            transcendentals=0,
        ),
    )(*operands)


def cut_kernel(dims, order, src_ref, out_ref, sem):
    column = Place(*dims).column
    width = out_ref.shape[1] // len(order)
    copies = []
    for k, mask in enumerate(order):
        start = pl.multiple_of((column ^ mask) * width, width)
        copies.append(
            pltpu.make_async_copy(
                src_ref.at[:, pl.ds(start, width)], out_ref.at[:, k * width : (k + 1) * width], sem.at[k]
            )
        )
        copies[-1].start()
    for copy in copies:
        copy.wait()


def cut(src, order, dims, width):
    n = len(order)
    return pl.pallas_call(
        functools.partial(cut_kernel, dims, order),
        out_shape=jax.ShapeDtypeStruct((src.shape[0], n * width), src.dtype),
        in_specs=[HBM],
        out_specs=VMEM,
        scratch_shapes=[pltpu.SemaphoreType.DMA((n,))],
        compiler_params=limit(51),
        cost_estimate=pl.CostEstimate(
            flops=0, bytes_accessed=2 * n * width * src.shape[0], transcendentals=0
        ),
    )(src)


def pick_kernel(dims, mine_ref, other_ref, *refs):
    out_ref = refs[-1]
    owner = Place(*dims).owner

    @pl.when(owner)
    def _():
        out_ref[...] = mine_ref[...]

    @pl.when(jnp.logical_not(owner))
    def _():
        out_ref[...] = other_ref[...]


def pick(dims, mine, other, after=()):
    return pl.pallas_call(
        functools.partial(pick_kernel, dims),
        out_shape=jax.ShapeDtypeStruct(mine.shape, mine.dtype),
        in_specs=[VMEM] * 2 + [ANY] * len(after),
        out_specs=VMEM,
        compiler_params=limit(2),
        cost_estimate=pl.CostEstimate(flops=0, bytes_accessed=4 * mine.size, transcendentals=0),
    )(mine, other, *after)


def sort_kernel(mine_ref, other_ref, theirs_ref, keep_ref, give_ref):
    here = lax.axis_index("dim") == lax.axis_index("grp")
    mine, other = mine_ref[...], other_ref[...] + theirs_ref[...]
    keep_ref[...] = jnp.where(here, mine, other)
    give_ref[...] = jnp.where(here, other, mine)


def sort_out(mine, other, theirs):
    return pl.pallas_call(
        sort_kernel,
        out_shape=[jax.ShapeDtypeStruct(mine.shape, mine.dtype)] * 2,
        in_specs=[VMEM] * 3,
        out_specs=[VMEM] * 2,
        compiler_params=limit(2),
    )(mine, other, theirs)


def per_device_quad(nz, nx, ny, queries, inverse_fisher, stored_grads):
    nex, dims = nz * nx, (nz, nx)
    near = nz // 2
    nq = queries.shape[0]

    def move(value, target):
        pairs = []
        for sy in range(ny):
            for sz in range(nz):
                for sx in range(nx):
                    for sd in range(2):
                        to = target(sy, sz, sx, sd)
                        if to is not None:
                            ty, tz, tx, td = to
                            pairs.append(((sy * nex + sz * nx + sx) * 2 + sd, (ty * nex + tz * nx + tx) * 2 + td))
        return lax.ppermute(value, AXES, pairs)

    def along_z(value, hops, flip=False):
        def target(sy, sz, sx, sd):
            su = sz if sd == 0 else nz - 1 - sz
            if su not in hops:
                return None
            tu = hops[su]
            return sy, tu if sd == 0 else nz - 1 - tu, 1 - sx if flip else sx, sd

        return move(value, target)

    def swap_y(value):
        return move(value, lambda sy, sz, sx, sd: (1 - sy, sz, sx, sd))

    def swap_core(value):
        return move(value, lambda sy, sz, sx, sd: (sy, sz, sx, 1 - sd))

    def gather(own, direct, after=()):
        def start(sy, sz, sx, sd):
            su = sz if sd == 0 else nz - 1 - sz
            if su < near:
                return sy, sz + 2 if sd == 0 else sz - 2, sx, sd
            return sy, sz ^ 1, 1 - sx, 1 - sd

        came = move(own, start)
        if direct:
            corner = along_z(own, {0: 3, 1: 2}, True)
        first = pick(dims, own, came, after)
        pairs = {0: 1, 1: 0, 2: 3, 3: 2}
        beside = along_z(first, pairs)
        across = along_z(first, {0: 0, 1: 1, 2: 2, 3: 3}, True)
        if direct:
            beside, corner = lax.optimization_barrier((beside, corner))
        else:
            corner = along_z(first, {2: 3, 3: 2}, True)

        def last(after):
            ready, _ = lax.optimization_barrier((came, after))
            return pick(dims, ready, corner)

        return first, beside, across, last

    rows, width = nq // ny, queries.shape[1]
    to_y = cut(stored_grads, ORDER[1:], dims, width)
    queries, to_y = lax.optimization_barrier((queries, to_y))
    own = lax.dynamic_slice_in_dim(queries, lax.axis_index("grp") * rows, rows, axis=0)
    own, to_y = lax.optimization_barrier((own, to_y))
    other_grads = swap_y(to_y)
    step = functools.partial(fisher_step, inverse_fisher, dims, width)
    a0, a1, b0, b1 = step(((0, 0), (0, 1), (1, 0), (1, 1)))
    q0, q1, q2, last = gather(own, False, (a0,))
    total, c0, c1 = step(((2, 0), (2, 1)), q0, (a0, a1))
    total, d0 = step(((3, 0),), q1, (b0, b1), total)
    total, d1 = step(((3, 1),), q2, (c0, c1), total)
    (total,) = step((), last(total), (d0, d1), total)
    panel = (total + swap_core(total)).astype(jnp.bfloat16)

    p0, p1, p2, last = gather(panel, True)
    swapped = swap_y(p0)
    p1, other_grads = lax.optimization_barrier((p1, other_grads))
    mine = score_dot([p0, p1], ORDER[:2], dims, stored_grads)
    p2, _ = lax.optimization_barrier((p2, mine))
    other = score_dot([p1, p2], (0, 1), None, other_grads)
    p3 = last(other)
    other = score_dot([p3], (2,), None, other_grads, other)
    p2, p3, mine, swapped, _ = lax.optimization_barrier((p2, p3, mine, swapped, other))
    mine = score_dot([p2, p3], ORDER[2:], dims, stored_grads, mine)
    theirs = score_dot([swapped], ORDER[:1], dims, stored_grads)

    keep, give = sort_out(mine, swap_y(other), theirs)
    return keep + swap_core(give)


def solution(mesh):
    coords = [getattr(device, "coords", None) for device in mesh.devices.flat]
    nx = 2 if None in coords else len({c[0] for c in coords})
    nz = mesh.shape["ex"] // nx
    ny = mesh.shape["grp"]
    if (nz, nx, ny) == (4, 2, 2):
        body = functools.partial(per_device_quad, nz, nx, ny)
    else:
        body = per_device_any
    return jax.shard_map(
        body,
        mesh=mesh,
        in_specs=(P(None, "ex"), P("ex", "dim"), P(("grp", "ex"), "dim")),
        out_specs=P("dim", ("grp", "ex")),
        check_vma=False,
    )
```

```python
import functools

import jax
import jax.numpy as jnp
from jax import lax
from jax.experimental import pallas as pl
from jax.experimental.pallas import tpu as pltpu
from jax.sharding import PartitionSpec as P

AXES = ("grp", "ex", "dim")
NT = (((1,), (1,)), ((), ()))
VMEM = pl.BlockSpec(memory_space=pltpu.VMEM)
HBM = pl.BlockSpec(memory_space=pltpu.HBM)
ANY = pl.BlockSpec(memory_space=pl.ANY)


def limit(mib):
    return pltpu.CompilerParams(vmem_limit_bytes=mib * 1024 * 1024)


def per_device_any(queries, inverse_fisher, stored_grads):
    term_block = jnp.dot(queries, inverse_fisher, preferred_element_type=jnp.float32)
    own_panel = lax.psum_scatter(term_block, "ex", scatter_dimension=1, tiled=True).astype(
        jnp.bfloat16
    )
    partial_scores = lax.dot_general(
        lax.all_gather(own_panel, "ex", axis=1, tiled=True),
        stored_grads,
        NT,
        preferred_element_type=jnp.float32,
    )
    return lax.psum_scatter(partial_scores, "dim", scatter_dimension=0, tiled=True)


class Place:
    def __init__(self, nz, nx):
        self.y, e, self.d = (lax.axis_index(a) for a in AXES)
        z, x = lax.div(e, nx), lax.rem(e, nx)
        u = jnp.where(self.d == 0, z, nz - 1 - z)
        self.owner = u < nz // 2
        local = jnp.where(self.d == 0, lax.rem(u, 2), nz // 2 - 1 - lax.rem(u, 2))
        self.column = local * nx + x


ORDER = (0, 2, 1, 3)


def half_copies(fisher_ref, block, half, held_ref, sem):
    steps = sem.shape[0]
    rows, width = held_ref.shape
    step = rows // steps
    columns = pl.ds(pl.multiple_of(block * width, width), width)
    copies = []
    for i in range(steps):
        copies.append(
            pltpu.make_async_copy(
                fisher_ref.at[pl.ds(half * rows + i * step, step), columns],
                held_ref.at[pl.ds(i * step, step), :],
                sem.at[i],
            )
        )
    return copies


def times(chunk_ref, fisher):
    return lax.dot_general(chunk_ref[...], fisher, NT, preferred_element_type=jnp.float32)


def fisher_kernel(dims, n_in, has_base, fetch, *refs):
    if fetch:
        column = Place(*dims).column
        fisher_ref, *refs = refs
    chunk_ref, halves = (refs[0], refs[1:3]) if n_in else (None, ())
    base_ref = refs[3] if has_base else None
    outs, sem = refs[n_in + has_base : -1], refs[-1]
    held = outs[1:] if n_in else outs
    copies = []
    for k, (piece, half) in enumerate(fetch):
        for copy in half_copies(fisher_ref, column ^ ORDER[piece], half, held[k], sem.at[k]):
            copy.start()
            copies.append(copy)

    def product(h, start, step):
        columns = pl.ds(h * halves[h].shape[0] + start, step)
        term = times(chunk_ref, halves[h][pl.ds(start, step), :])
        outs[0][:, columns] = term + base_ref[:, columns] if has_base else term

    if halves:
        rows = halves[0].shape[0]
        step = rows // 2 if fetch else rows

        @pl.loop(0, rows // step)
        def _(i):
            for h in range(len(halves)):
                product(h, pl.multiple_of(i * step, step), step)

    for copy in copies:
        copy.wait()


def fisher_step(fisher, dims, width, fetch, chunk=None, halves=(), base=None):
    rows = fisher.shape[0]
    ins = [] if chunk is None else [chunk, *halves]
    has_base = base is not None
    held = jax.ShapeDtypeStruct((rows // 2, width), fisher.dtype)
    out_shape = [] if chunk is None else [jax.ShapeDtypeStruct((chunk.shape[0], rows), jnp.float32)]
    out_shape += [held] * len(fetch)
    return pl.pallas_call(
        functools.partial(fisher_kernel, dims, len(ins), has_base, fetch),
        out_shape=out_shape,
        in_specs=[HBM] * bool(fetch) + [VMEM] * (len(ins) + has_base),
        out_specs=[VMEM] * len(out_shape),
        scratch_shapes=[pltpu.SemaphoreType.DMA((max(len(fetch), 1), 2))],
        compiler_params=limit(34 if chunk is None else 20),
        cost_estimate=pl.CostEstimate(
            flops=0 if chunk is None else 2 * chunk.shape[0] * width * rows,
            bytes_accessed=width * rows * (len(fetch) + 2 * bool(ins)),
            transcendentals=0,
        ),
    )(*([fisher] if fetch else []), *ins, *([base] if has_base else []))


def score_kernel(dims, order, has_base, *refs):
    n = len(order)
    column = Place(*dims).column if dims else 0
    grads_ref, out_ref = refs[n], refs[-1]
    width = refs[0].shape[1]
    total = refs[n + 1][...] if has_base else None
    for k in range(n):
        block = column ^ order[k]
        start = pl.multiple_of(block * width, width) if dims else block * width
        term = times(refs[k], grads_ref[:, pl.ds(start, width)])
        total = term if total is None else total + term
    out_ref[...] = total


def score_dot(pieces, order, dims, grads, base=None):
    n = len(pieces)
    rows, width = pieces[0].shape
    operands = [*pieces, grads] + ([] if base is None else [base])
    return pl.pallas_call(
        functools.partial(score_kernel, dims, order, base is not None),
        out_shape=jax.ShapeDtypeStruct((rows, grads.shape[0]), jnp.float32),
        in_specs=[VMEM] * len(operands),
        out_specs=VMEM,
        compiler_params=limit(8),
        cost_estimate=pl.CostEstimate(
            flops=2 * n * rows * width * grads.shape[0],
            bytes_accessed=2 * n * width * grads.shape[0],
            transcendentals=0,
        ),
    )(*operands)


def cut_kernel(dims, order, src_ref, out_ref, sem):
    column = Place(*dims).column
    width = out_ref.shape[1] // len(order)
    copies = []
    for k, mask in enumerate(order):
        start = pl.multiple_of((column ^ mask) * width, width)
        copies.append(
            pltpu.make_async_copy(
                src_ref.at[:, pl.ds(start, width)], out_ref.at[:, k * width : (k + 1) * width], sem.at[k]
            )
        )
        copies[-1].start()
    for copy in copies:
        copy.wait()


def cut(src, order, dims, width):
    n = len(order)
    return pl.pallas_call(
        functools.partial(cut_kernel, dims, order),
        out_shape=jax.ShapeDtypeStruct((src.shape[0], n * width), src.dtype),
        in_specs=[HBM],
        out_specs=VMEM,
        scratch_shapes=[pltpu.SemaphoreType.DMA((n,))],
        compiler_params=limit(51),
        cost_estimate=pl.CostEstimate(
            flops=0, bytes_accessed=2 * n * width * src.shape[0], transcendentals=0
        ),
    )(src)


def pick_kernel(dims, mine_ref, other_ref, *refs):
    out_ref = refs[-1]
    owner = Place(*dims).owner

    @pl.when(owner)
    def _():
        out_ref[...] = mine_ref[...]

    @pl.when(jnp.logical_not(owner))
    def _():
        out_ref[...] = other_ref[...]


def pick(dims, mine, other, after=()):
    return pl.pallas_call(
        functools.partial(pick_kernel, dims),
        out_shape=jax.ShapeDtypeStruct(mine.shape, mine.dtype),
        in_specs=[VMEM] * 2 + [ANY] * len(after),
        out_specs=VMEM,
        compiler_params=limit(2),
        cost_estimate=pl.CostEstimate(flops=0, bytes_accessed=4 * mine.size, transcendentals=0),
    )(mine, other, *after)


def sort_kernel(mine_ref, other_ref, theirs_ref, keep_ref, give_ref):
    here = lax.axis_index("dim") == lax.axis_index("grp")
    mine, other = mine_ref[...], other_ref[...] + theirs_ref[...]
    keep_ref[...] = jnp.where(here, mine, other)
    give_ref[...] = jnp.where(here, other, mine)


def sort_out(mine, other, theirs):
    return pl.pallas_call(
        sort_kernel,
        out_shape=[jax.ShapeDtypeStruct(mine.shape, mine.dtype)] * 2,
        in_specs=[VMEM] * 3,
        out_specs=[VMEM] * 2,
        compiler_params=limit(2),
    )(mine, other, theirs)


def per_device_quad(nz, nx, ny, queries, inverse_fisher, stored_grads):
    nex, dims = nz * nx, (nz, nx)
    near = nz // 2
    nq = queries.shape[0]

    def move(value, target):
        pairs = []
        for sy in range(ny):
            for sz in range(nz):
                for sx in range(nx):
                    for sd in range(2):
                        to = target(sy, sz, sx, sd)
                        if to is not None:
                            ty, tz, tx, td = to
                            pairs.append(((sy * nex + sz * nx + sx) * 2 + sd, (ty * nex + tz * nx + tx) * 2 + td))
        return lax.ppermute(value, AXES, pairs)

    def along_z(value, hops, flip=False):
        def target(sy, sz, sx, sd):
            su = sz if sd == 0 else nz - 1 - sz
            if su not in hops:
                return None
            tu = hops[su]
            return sy, tu if sd == 0 else nz - 1 - tu, 1 - sx if flip else sx, sd

        return move(value, target)

    def swap_y(value):
        return move(value, lambda sy, sz, sx, sd: (1 - sy, sz, sx, sd))

    def swap_core(value):
        return move(value, lambda sy, sz, sx, sd: (sy, sz, sx, 1 - sd))

    def gather(own, direct, after=()):
        def start(sy, sz, sx, sd):
            su = sz if sd == 0 else nz - 1 - sz
            if su < near:
                return sy, sz + 2 if sd == 0 else sz - 2, sx, sd
            return sy, sz ^ 1, 1 - sx, 1 - sd

        came = move(own, start)
        if direct:
            corner = along_z(own, {0: 3, 1: 2}, True)
        first = pick(dims, own, came, after)
        pairs = {0: 1, 1: 0, 2: 3, 3: 2}
        beside = along_z(first, pairs)
        across = along_z(first, {0: 0, 1: 1, 2: 2, 3: 3}, True)
        if direct:
            beside, corner = lax.optimization_barrier((beside, corner))

        def last(before, after):
            if direct:
                piece = corner
            else:
                ready, _ = lax.optimization_barrier((first, before))
                piece = along_z(ready, {2: 3, 3: 2}, True)
            ready, _ = lax.optimization_barrier((came, after))
            return pick(dims, ready, piece)

        return first, beside, across, last

    rows, width = nq // ny, queries.shape[1]
    to_y = cut(stored_grads, ORDER[1:], dims, width)
    queries, to_y = lax.optimization_barrier((queries, to_y))
    own = lax.dynamic_slice_in_dim(queries, lax.axis_index("grp") * rows, rows, axis=0)
    own, to_y = lax.optimization_barrier((own, to_y))
    other_grads = swap_y(to_y)
    step = functools.partial(fisher_step, inverse_fisher, dims, width)
    a0, a1, b0, b1 = step(((0, 0), (0, 1), (1, 0), (1, 1)))
    q0, q1, q2, last = gather(own, False, (a0,))
    total0, c0, c1 = step(((2, 0), (2, 1)), q0, (a0, a1))
    total, d0 = step(((3, 0),), q1, (b0, b1), total0)
    total, d1 = step(((3, 1),), q2, (c0, c1), total)
    (total,) = step((), last(total0, total), (d0, d1), total)
    panel = (total + swap_core(total)).astype(jnp.bfloat16)

    p0, p1, p2, last = gather(panel, True)
    swapped = swap_y(p0)
    p1, other_grads = lax.optimization_barrier((p1, other_grads))
    mine = score_dot([p0, p1], ORDER[:2], dims, stored_grads)
    p2, _ = lax.optimization_barrier((p2, mine))
    other = score_dot([p1, p2], (0, 1), None, other_grads)
    p3 = last(other, other)
    other = score_dot([p3], (2,), None, other_grads, other)
    p2, p3, mine, swapped, _ = lax.optimization_barrier((p2, p3, mine, swapped, other))
    mine = score_dot([p2, p3], ORDER[2:], dims, stored_grads, mine)
    theirs = score_dot([swapped], ORDER[:1], dims, stored_grads)

    keep, give = sort_out(mine, swap_y(other), theirs)
    return keep + swap_core(give)


def solution(mesh):
    coords = [getattr(device, "coords", None) for device in mesh.devices.flat]
    nx = 2 if None in coords else len({c[0] for c in coords})
    nz = mesh.shape["ex"] // nx
    ny = mesh.shape["grp"]
    if (nz, nx, ny) == (4, 2, 2):
        body = functools.partial(per_device_quad, nz, nx, ny)
    else:
        body = per_device_any
    return jax.shard_map(
        body,
        mesh=mesh,
        in_specs=(P(None, "ex"), P("ex", "dim"), P(("grp", "ex"), "dim")),
        out_specs=P("dim", ("grp", "ex")),
        check_vma=False,
    )
```

```python
import functools

import jax
import jax.numpy as jnp
from jax import lax
from jax.experimental import pallas as pl
from jax.experimental.pallas import tpu as pltpu
from jax.sharding import PartitionSpec as P

AXES = ("grp", "ex", "dim")
NT = (((1,), (1,)), ((), ()))
VMEM = pl.BlockSpec(memory_space=pltpu.VMEM)
HBM = pl.BlockSpec(memory_space=pltpu.HBM)
ANY = pl.BlockSpec(memory_space=pl.ANY)


def limit(mib):
    return pltpu.CompilerParams(vmem_limit_bytes=mib * 1024 * 1024)


def per_device_any(queries, inverse_fisher, stored_grads):
    term_block = jnp.dot(queries, inverse_fisher, preferred_element_type=jnp.float32)
    own_panel = lax.psum_scatter(term_block, "ex", scatter_dimension=1, tiled=True).astype(
        jnp.bfloat16
    )
    partial_scores = lax.dot_general(
        lax.all_gather(own_panel, "ex", axis=1, tiled=True),
        stored_grads,
        NT,
        preferred_element_type=jnp.float32,
    )
    return lax.psum_scatter(partial_scores, "dim", scatter_dimension=0, tiled=True)


class Place:
    def __init__(self, nz, nx):
        self.y, e, self.d = (lax.axis_index(a) for a in AXES)
        z, x = lax.div(e, nx), lax.rem(e, nx)
        u = jnp.where(self.d == 0, z, nz - 1 - z)
        self.owner = u < nz // 2
        local = jnp.where(self.d == 0, lax.rem(u, 2), nz // 2 - 1 - lax.rem(u, 2))
        self.column = local * nx + x


ORDER = (0, 2, 1, 3)


def half_copies(fisher_ref, block, half, held_ref, sem):
    steps = sem.shape[0]
    rows, width = held_ref.shape
    step = rows // steps
    columns = pl.ds(pl.multiple_of(block * width, width), width)
    copies = []
    for i in range(steps):
        copies.append(
            pltpu.make_async_copy(
                fisher_ref.at[pl.ds(half * rows + i * step, step), columns],
                held_ref.at[pl.ds(i * step, step), :],
                sem.at[i],
            )
        )
    return copies


def times(chunk_ref, fisher):
    return lax.dot_general(chunk_ref[...], fisher, NT, preferred_element_type=jnp.float32)


def fisher_kernel(dims, n_in, has_base, fetch, *refs):
    if fetch:
        column = Place(*dims).column
        fisher_ref, *refs = refs
    chunk_ref, halves = (refs[0], refs[1:3]) if n_in else (None, ())
    base_ref = refs[3] if has_base else None
    outs, sem = refs[n_in + has_base : -1], refs[-1]
    held = outs[1:] if n_in else outs
    copies = []
    for k, (piece, half) in enumerate(fetch):
        for copy in half_copies(fisher_ref, column ^ ORDER[piece], half, held[k], sem.at[k]):
            copy.start()
            copies.append(copy)

    def product(h, start, step):
        columns = pl.ds(h * halves[h].shape[0] + start, step)
        term = times(chunk_ref, halves[h][pl.ds(start, step), :])
        outs[0][:, columns] = term + base_ref[:, columns] if has_base else term

    if halves:
        rows = halves[0].shape[0]
        step = rows // 2 if fetch else rows

        @pl.loop(0, rows // step)
        def _(i):
            for h in range(len(halves)):
                product(h, pl.multiple_of(i * step, step), step)

    for copy in copies:
        copy.wait()


def fisher_step(fisher, dims, width, fetch, chunk=None, halves=(), base=None):
    rows = fisher.shape[0]
    ins = [] if chunk is None else [chunk, *halves]
    has_base = base is not None
    held = jax.ShapeDtypeStruct((rows // 2, width), fisher.dtype)
    out_shape = [] if chunk is None else [jax.ShapeDtypeStruct((chunk.shape[0], rows), jnp.float32)]
    out_shape += [held] * len(fetch)
    return pl.pallas_call(
        functools.partial(fisher_kernel, dims, len(ins), has_base, fetch),
        out_shape=out_shape,
        in_specs=[HBM] * bool(fetch) + [VMEM] * (len(ins) + has_base),
        out_specs=[VMEM] * len(out_shape),
        scratch_shapes=[pltpu.SemaphoreType.DMA((max(len(fetch), 1), 2))],
        compiler_params=limit(34 if chunk is None else 20),
        cost_estimate=pl.CostEstimate(
            flops=0 if chunk is None else 2 * chunk.shape[0] * width * rows,
            bytes_accessed=width * rows * (len(fetch) + 2 * bool(ins)),
            transcendentals=0,
        ),
    )(*([fisher] if fetch else []), *ins, *([base] if has_base else []))


def score_kernel(dims, order, has_base, *refs):
    n = len(order)
    column = Place(*dims).column if dims else 0
    grads_ref, out_ref = refs[n], refs[-1]
    width = refs[0].shape[1]
    total = refs[n + 1][...] if has_base else None
    for k in range(n):
        block = column ^ order[k]
        start = pl.multiple_of(block * width, width) if dims else block * width
        term = times(refs[k], grads_ref[:, pl.ds(start, width)])
        total = term if total is None else total + term
    out_ref[...] = total


def score_dot(pieces, order, dims, grads, base=None):
    n = len(pieces)
    rows, width = pieces[0].shape
    operands = [*pieces, grads] + ([] if base is None else [base])
    return pl.pallas_call(
        functools.partial(score_kernel, dims, order, base is not None),
        out_shape=jax.ShapeDtypeStruct((rows, grads.shape[0]), jnp.float32),
        in_specs=[VMEM] * len(operands),
        out_specs=VMEM,
        compiler_params=limit(8),
        cost_estimate=pl.CostEstimate(
            flops=2 * n * rows * width * grads.shape[0],
            bytes_accessed=2 * n * width * grads.shape[0],
            transcendentals=0,
        ),
    )(*operands)


def cut_kernel(dims, order, src_ref, out_ref, sem):
    column = Place(*dims).column
    width = out_ref.shape[1] // len(order)
    copies = []
    for k, mask in enumerate(order):
        start = pl.multiple_of((column ^ mask) * width, width)
        copies.append(
            pltpu.make_async_copy(
                src_ref.at[:, pl.ds(start, width)], out_ref.at[:, k * width : (k + 1) * width], sem.at[k]
            )
        )
        copies[-1].start()
    for copy in copies:
        copy.wait()


def cut(src, order, dims, width):
    n = len(order)
    return pl.pallas_call(
        functools.partial(cut_kernel, dims, order),
        out_shape=jax.ShapeDtypeStruct((src.shape[0], n * width), src.dtype),
        in_specs=[HBM],
        out_specs=VMEM,
        scratch_shapes=[pltpu.SemaphoreType.DMA((n,))],
        compiler_params=limit(51),
        cost_estimate=pl.CostEstimate(
            flops=0, bytes_accessed=2 * n * width * src.shape[0], transcendentals=0
        ),
    )(src)


def pick_kernel(dims, mine_ref, other_ref, *refs):
    out_ref = refs[-1]
    owner = Place(*dims).owner

    @pl.when(owner)
    def _():
        out_ref[...] = mine_ref[...]

    @pl.when(jnp.logical_not(owner))
    def _():
        out_ref[...] = other_ref[...]


def pick(dims, mine, other, after=()):
    return pl.pallas_call(
        functools.partial(pick_kernel, dims),
        out_shape=jax.ShapeDtypeStruct(mine.shape, mine.dtype),
        in_specs=[VMEM] * 2 + [ANY] * len(after),
        out_specs=VMEM,
        compiler_params=limit(2),
        cost_estimate=pl.CostEstimate(flops=0, bytes_accessed=4 * mine.size, transcendentals=0),
    )(mine, other, *after)


def sort_kernel(mine_ref, other_ref, theirs_ref, keep_ref, give_ref):
    here = lax.axis_index("dim") == lax.axis_index("grp")
    mine, other = mine_ref[...], other_ref[...] + theirs_ref[...]
    keep_ref[...] = jnp.where(here, mine, other)
    give_ref[...] = jnp.where(here, other, mine)


def sort_out(mine, other, theirs):
    return pl.pallas_call(
        sort_kernel,
        out_shape=[jax.ShapeDtypeStruct(mine.shape, mine.dtype)] * 2,
        in_specs=[VMEM] * 3,
        out_specs=[VMEM] * 2,
        compiler_params=limit(2),
    )(mine, other, theirs)


def per_device_quad(nz, nx, ny, queries, inverse_fisher, stored_grads):
    nex, dims = nz * nx, (nz, nx)
    near = nz // 2
    nq = queries.shape[0]

    def move(value, target):
        pairs = []
        for sy in range(ny):
            for sz in range(nz):
                for sx in range(nx):
                    for sd in range(2):
                        to = target(sy, sz, sx, sd)
                        if to is not None:
                            ty, tz, tx, td = to
                            pairs.append(((sy * nex + sz * nx + sx) * 2 + sd, (ty * nex + tz * nx + tx) * 2 + td))
        return lax.ppermute(value, AXES, pairs)

    def along_z(value, hops, flip=False):
        def target(sy, sz, sx, sd):
            su = sz if sd == 0 else nz - 1 - sz
            if su not in hops:
                return None
            tu = hops[su]
            return sy, tu if sd == 0 else nz - 1 - tu, 1 - sx if flip else sx, sd

        return move(value, target)

    def swap_y(value):
        return move(value, lambda sy, sz, sx, sd: (1 - sy, sz, sx, sd))

    def swap_core(value):
        return move(value, lambda sy, sz, sx, sd: (sy, sz, sx, 1 - sd))

    def gather(own, direct, after=()):
        def start(sy, sz, sx, sd):
            su = sz if sd == 0 else nz - 1 - sz
            if su < near:
                return sy, sz + 2 if sd == 0 else sz - 2, sx, sd
            return sy, sz ^ 1, 1 - sx, 1 - sd

        came = move(own, start)
        if direct:
            corner = along_z(own, {0: 3, 1: 2}, True)
        first = pick(dims, own, came, after)
        pairs = {0: 1, 1: 0, 2: 3, 3: 2}
        beside = along_z(first, pairs)
        across = along_z(first, {0: 0, 1: 1, 2: 2, 3: 3}, True)
        if direct:
            beside, corner = lax.optimization_barrier((beside, corner))

        def last(before, after):
            if direct:
                ready, _ = lax.optimization_barrier((came, after))
                return pick(dims, ready, corner)
            ready, _ = lax.optimization_barrier((first, before))
            piece, _ = lax.optimization_barrier((along_z(ready, pairs, True), after))
            return piece

        return first, beside, across, last

    rows, width = nq // ny, queries.shape[1]
    to_y = cut(stored_grads, ORDER[1:], dims, width)
    queries, to_y = lax.optimization_barrier((queries, to_y))
    own = lax.dynamic_slice_in_dim(queries, lax.axis_index("grp") * rows, rows, axis=0)
    own, to_y = lax.optimization_barrier((own, to_y))
    other_grads = swap_y(to_y)
    step = functools.partial(fisher_step, inverse_fisher, dims, width)
    a0, a1, b0, b1 = step(((0, 0), (0, 1), (1, 0), (1, 1)))
    q0, q1, q2, last = gather(own, False, (a0,))
    total0, c0, c1 = step(((2, 0), (2, 1)), q0, (a0, a1))
    total, d0 = step(((3, 0),), q1, (b0, b1), total0)
    total, d1 = step(((3, 1),), q2, (c0, c1), total)
    (total,) = step((), last(total0, total), (d0, d1), total)
    panel = (total + swap_core(total)).astype(jnp.bfloat16)

    p0, p1, p2, last = gather(panel, True)
    swapped = swap_y(p0)
    p1, other_grads = lax.optimization_barrier((p1, other_grads))
    mine = score_dot([p0, p1], ORDER[:2], dims, stored_grads)
    p2, _ = lax.optimization_barrier((p2, mine))
    other = score_dot([p1, p2], (0, 1), None, other_grads)
    p3 = last(other, other)
    other = score_dot([p3], (2,), None, other_grads, other)
    p2, p3, mine, swapped, _ = lax.optimization_barrier((p2, p3, mine, swapped, other))
    mine = score_dot([p2, p3], ORDER[2:], dims, stored_grads, mine)
    theirs = score_dot([swapped], ORDER[:1], dims, stored_grads)

    keep, give = sort_out(mine, swap_y(other), theirs)
    return keep + swap_core(give)


def solution(mesh):
    coords = [getattr(device, "coords", None) for device in mesh.devices.flat]
    nx = 2 if None in coords else len({c[0] for c in coords})
    nz = mesh.shape["ex"] // nx
    ny = mesh.shape["grp"]
    if (nz, nx, ny) == (4, 2, 2):
        body = functools.partial(per_device_quad, nz, nx, ny)
    else:
        body = per_device_any
    return jax.shard_map(
        body,
        mesh=mesh,
        in_specs=(P(None, "ex"), P("ex", "dim"), P(("grp", "ex"), "dim")),
        out_specs=P("dim", ("grp", "ex")),
        check_vma=False,
    )
```

```python
import functools

import jax
import jax.numpy as jnp
from jax import lax
from jax.experimental import pallas as pl
from jax.experimental.pallas import tpu as pltpu
from jax.sharding import PartitionSpec as P

AXES = ("grp", "ex", "dim")
NT = (((1,), (1,)), ((), ()))
VMEM = pl.BlockSpec(memory_space=pltpu.VMEM)
HBM = pl.BlockSpec(memory_space=pltpu.HBM)
ANY = pl.BlockSpec(memory_space=pl.ANY)


def limit(mib):
    return pltpu.CompilerParams(vmem_limit_bytes=mib * 1024 * 1024)


def per_device_any(queries, inverse_fisher, stored_grads):
    term_block = jnp.dot(queries, inverse_fisher, preferred_element_type=jnp.float32)
    own_panel = lax.psum_scatter(term_block, "ex", scatter_dimension=1, tiled=True).astype(
        jnp.bfloat16
    )
    partial_scores = lax.dot_general(
        lax.all_gather(own_panel, "ex", axis=1, tiled=True),
        stored_grads,
        NT,
        preferred_element_type=jnp.float32,
    )
    return lax.psum_scatter(partial_scores, "dim", scatter_dimension=0, tiled=True)


class Place:
    def __init__(self, nz, nx):
        self.y, e, self.d = (lax.axis_index(a) for a in AXES)
        z, x = lax.div(e, nx), lax.rem(e, nx)
        u = jnp.where(self.d == 0, z, nz - 1 - z)
        self.owner = u < nz // 2
        local = jnp.where(self.d == 0, lax.rem(u, 2), nz // 2 - 1 - lax.rem(u, 2))
        self.column = local * nx + x


ORDER = (0, 2, 1, 3)


def block_copies(fisher_ref, block, start, held_ref, sem):
    rows, width = held_ref.shape
    step = 512
    columns = pl.ds(pl.multiple_of(block * width, width), width)
    return [
        pltpu.make_async_copy(
            fisher_ref.at[pl.ds(start + i * step, step), columns],
            held_ref.at[pl.ds(i * step, step), :],
            sem.at[i],
        )
        for i in range(rows // step)
    ]


def times(chunk_ref, fisher):
    return lax.dot_general(chunk_ref[...], fisher, NT, preferred_element_type=jnp.float32)


def fisher_kernel(dims, n_parts, has_base, fetch, *refs):
    if fetch:
        column = Place(*dims).column
        fisher_ref, *refs = refs
    n_in = n_parts + bool(n_parts)
    chunk_ref, parts = (refs[0], refs[1:n_in]) if n_parts else (None, ())
    base_ref = refs[n_in] if has_base else None
    outs, sem = refs[n_in + has_base : -1], refs[-1]
    held = outs[1:] if n_parts else outs
    copies = []
    for k, (piece, start, _) in enumerate(fetch):
        for copy in block_copies(fisher_ref, column ^ ORDER[piece], start, held[k], sem.at[k]):
            copy.start()
            copies.append(copy)

    if parts:
        loops = 2 if fetch else 1

        @pl.loop(0, loops)
        def _(i):
            before = 0
            for part_ref in parts:
                rows = part_ref.shape[0]
                step = rows // loops
                start = pl.multiple_of(i * step, step)
                columns = pl.ds(before + start, step)
                term = times(chunk_ref, part_ref[pl.ds(start, step), :])
                outs[0][:, columns] = term + base_ref[:, columns] if has_base else term
                before += rows

    for copy in copies:
        copy.wait()


def fisher_step(fisher, dims, width, fetch, chunk=None, parts=(), base=None):
    total = fisher.shape[0]
    ins = [] if chunk is None else [chunk, *parts]
    has_base = base is not None
    out_shape = [] if chunk is None else [jax.ShapeDtypeStruct((chunk.shape[0], total), jnp.float32)]
    out_shape += [jax.ShapeDtypeStruct((rows, width), fisher.dtype) for _, _, rows in fetch]
    fetched = sum(rows for _, _, rows in fetch)
    return pl.pallas_call(
        functools.partial(fisher_kernel, dims, len(parts), has_base, fetch),
        out_shape=out_shape,
        in_specs=[HBM] * bool(fetch) + [VMEM] * (len(ins) + has_base),
        out_specs=[VMEM] * len(out_shape),
        scratch_shapes=[pltpu.SemaphoreType.DMA((max(len(fetch), 1), 2))],
        compiler_params=limit(34 if chunk is None else 20),
        cost_estimate=pl.CostEstimate(
            flops=0 if chunk is None else 2 * chunk.shape[0] * width * total,
            bytes_accessed=2 * width * (fetched + total * bool(ins)),
            transcendentals=0,
        ),
    )(*([fisher] if fetch else []), *ins, *([base] if has_base else []))


def score_kernel(dims, order, has_base, *refs):
    n = len(order)
    column = Place(*dims).column if dims else 0
    grads_ref, out_ref = refs[n], refs[-1]
    width = refs[0].shape[1]
    total = refs[n + 1][...] if has_base else None
    for k in range(n):
        block = column ^ order[k]
        start = pl.multiple_of(block * width, width) if dims else block * width
        term = times(refs[k], grads_ref[:, pl.ds(start, width)])
        total = term if total is None else total + term
    out_ref[...] = total


def score_dot(pieces, order, dims, grads, base=None):
    n = len(pieces)
    rows, width = pieces[0].shape
    operands = [*pieces, grads] + ([] if base is None else [base])
    return pl.pallas_call(
        functools.partial(score_kernel, dims, order, base is not None),
        out_shape=jax.ShapeDtypeStruct((rows, grads.shape[0]), jnp.float32),
        in_specs=[VMEM] * len(operands),
        out_specs=VMEM,
        compiler_params=limit(8),
        cost_estimate=pl.CostEstimate(
            flops=2 * n * rows * width * grads.shape[0],
            bytes_accessed=2 * n * width * grads.shape[0],
            transcendentals=0,
        ),
    )(*operands)


def cut_kernel(dims, order, src_ref, out_ref, sem):
    column = Place(*dims).column
    width = out_ref.shape[1] // len(order)
    copies = []
    for k, mask in enumerate(order):
        start = pl.multiple_of((column ^ mask) * width, width)
        copies.append(
            pltpu.make_async_copy(
                src_ref.at[:, pl.ds(start, width)], out_ref.at[:, k * width : (k + 1) * width], sem.at[k]
            )
        )
        copies[-1].start()
    for copy in copies:
        copy.wait()


def cut(src, order, dims, width):
    n = len(order)
    return pl.pallas_call(
        functools.partial(cut_kernel, dims, order),
        out_shape=jax.ShapeDtypeStruct((src.shape[0], n * width), src.dtype),
        in_specs=[HBM],
        out_specs=VMEM,
        scratch_shapes=[pltpu.SemaphoreType.DMA((n,))],
        compiler_params=limit(51),
        cost_estimate=pl.CostEstimate(
            flops=0, bytes_accessed=2 * n * width * src.shape[0], transcendentals=0
        ),
    )(src)


def pick_kernel(dims, mine_ref, other_ref, *refs):
    out_ref = refs[-1]
    owner = Place(*dims).owner

    @pl.when(owner)
    def _():
        out_ref[...] = mine_ref[...]

    @pl.when(jnp.logical_not(owner))
    def _():
        out_ref[...] = other_ref[...]


def pick(dims, mine, other, after=()):
    return pl.pallas_call(
        functools.partial(pick_kernel, dims),
        out_shape=jax.ShapeDtypeStruct(mine.shape, mine.dtype),
        in_specs=[VMEM] * 2 + [ANY] * len(after),
        out_specs=VMEM,
        compiler_params=limit(2),
        cost_estimate=pl.CostEstimate(flops=0, bytes_accessed=4 * mine.size, transcendentals=0),
    )(mine, other, *after)


def sort_kernel(mine_ref, other_ref, theirs_ref, keep_ref, give_ref):
    here = lax.axis_index("dim") == lax.axis_index("grp")
    mine, other = mine_ref[...], other_ref[...] + theirs_ref[...]
    keep_ref[...] = jnp.where(here, mine, other)
    give_ref[...] = jnp.where(here, other, mine)


def sort_out(mine, other, theirs):
    return pl.pallas_call(
        sort_kernel,
        out_shape=[jax.ShapeDtypeStruct(mine.shape, mine.dtype)] * 2,
        in_specs=[VMEM] * 3,
        out_specs=[VMEM] * 2,
        compiler_params=limit(2),
    )(mine, other, theirs)


def per_device_quad(nz, nx, ny, queries, inverse_fisher, stored_grads):
    nex, dims = nz * nx, (nz, nx)
    near = nz // 2
    nq = queries.shape[0]

    def move(value, target):
        pairs = []
        for sy in range(ny):
            for sz in range(nz):
                for sx in range(nx):
                    for sd in range(2):
                        to = target(sy, sz, sx, sd)
                        if to is not None:
                            ty, tz, tx, td = to
                            pairs.append(((sy * nex + sz * nx + sx) * 2 + sd, (ty * nex + tz * nx + tx) * 2 + td))
        return lax.ppermute(value, AXES, pairs)

    def along_z(value, hops, flip=False):
        def target(sy, sz, sx, sd):
            su = sz if sd == 0 else nz - 1 - sz
            if su not in hops:
                return None
            tu = hops[su]
            return sy, tu if sd == 0 else nz - 1 - tu, 1 - sx if flip else sx, sd

        return move(value, target)

    def swap_y(value):
        return move(value, lambda sy, sz, sx, sd: (1 - sy, sz, sx, sd))

    def swap_core(value):
        return move(value, lambda sy, sz, sx, sd: (sy, sz, sx, 1 - sd))

    def gather(own, direct, after=()):
        def start(sy, sz, sx, sd):
            su = sz if sd == 0 else nz - 1 - sz
            if su < near:
                return sy, sz + 2 if sd == 0 else sz - 2, sx, sd
            return sy, sz ^ 1, 1 - sx, 1 - sd

        came = move(own, start)
        if direct:
            corner = along_z(own, {0: 3, 1: 2}, True)
        first = pick(dims, own, came, after)
        pairs = {0: 1, 1: 0, 2: 3, 3: 2}
        beside = along_z(first, pairs)
        across = along_z(first, {0: 0, 1: 1, 2: 2, 3: 3}, True)
        if direct:
            beside, corner = lax.optimization_barrier((beside, corner))

        def last(before, after):
            if direct:
                ready, _ = lax.optimization_barrier((came, after))
                return pick(dims, ready, corner)
            ready, _ = lax.optimization_barrier((first, before))
            piece, _ = lax.optimization_barrier((along_z(ready, pairs, True), after))
            return piece

        return first, beside, across, last

    rows, width = nq // ny, queries.shape[1]
    to_y = cut(stored_grads, ORDER[1:], dims, width)
    queries, to_y = lax.optimization_barrier((queries, to_y))
    own = lax.dynamic_slice_in_dim(queries, lax.axis_index("grp") * rows, rows, axis=0)
    own, to_y = lax.optimization_barrier((own, to_y))
    other_grads = swap_y(to_y)
    step = functools.partial(fisher_step, inverse_fisher, dims, width)
    half, quarter = inverse_fisher.shape[0] // 2, inverse_fisher.shape[0] // 4
    a0, a1, b0, b1 = step(((0, 0, half), (0, half, half), (1, 0, half), (1, half, half)))
    q0, q1, q2, last = gather(own, False, (a0,))
    total0, c0, c1 = step(((2, 0, half), (2, half, quarter)), q0, (a0, a1))
    total, c2, d0 = step(((2, half + quarter, quarter), (3, 0, half)), q1, (b0, b1), total0)
    total, d1 = step(((3, half, half),), q2, (c0, c1, c2), total)
    (total,) = step((), last(total0, total), (d0, d1), total)
    panel = (total + swap_core(total)).astype(jnp.bfloat16)

    p0, p1, p2, last = gather(panel, True)
    swapped = swap_y(p0)
    p1, other_grads = lax.optimization_barrier((p1, other_grads))
    p3 = last(p1, p1)
    other = score_dot([p1, p3], (0, 2), None, other_grads)
    p2, _ = lax.optimization_barrier((p2, other))
    other = score_dot([p2], (1,), None, other_grads, other)
    p2, swapped, _ = lax.optimization_barrier((p2, swapped, other))
    mine = score_dot([p0, p1, p2, p3], ORDER, dims, stored_grads)
    theirs = score_dot([swapped], ORDER[:1], dims, stored_grads)

    keep, give = sort_out(mine, swap_y(other), theirs)
    return keep + swap_core(give)


def solution(mesh):
    coords = [getattr(device, "coords", None) for device in mesh.devices.flat]
    nx = 2 if None in coords else len({c[0] for c in coords})
    nz = mesh.shape["ex"] // nx
    ny = mesh.shape["grp"]
    if (nz, nx, ny) == (4, 2, 2):
        body = functools.partial(per_device_quad, nz, nx, ny)
    else:
        body = per_device_any
    return jax.shard_map(
        body,
        mesh=mesh,
        in_specs=(P(None, "ex"), P("ex", "dim"), P(("grp", "ex"), "dim")),
        out_specs=P("dim", ("grp", "ex")),
        check_vma=False,
    )
```

```python
import functools

import jax
import jax.numpy as jnp
from jax import lax
from jax.experimental import pallas as pl
from jax.experimental.pallas import tpu as pltpu
from jax.sharding import PartitionSpec as P

AXES = ("grp", "ex", "dim")
NT = (((1,), (1,)), ((), ()))
VMEM = pl.BlockSpec(memory_space=pltpu.VMEM)
HBM = pl.BlockSpec(memory_space=pltpu.HBM)
ANY = pl.BlockSpec(memory_space=pl.ANY)


def limit(mib):
    return pltpu.CompilerParams(vmem_limit_bytes=mib * 1024 * 1024)


def per_device_any(queries, inverse_fisher, stored_grads):
    term_block = jnp.dot(queries, inverse_fisher, preferred_element_type=jnp.float32)
    own_panel = lax.psum_scatter(term_block, "ex", scatter_dimension=1, tiled=True).astype(
        jnp.bfloat16
    )
    partial_scores = lax.dot_general(
        lax.all_gather(own_panel, "ex", axis=1, tiled=True),
        stored_grads,
        NT,
        preferred_element_type=jnp.float32,
    )
    return lax.psum_scatter(partial_scores, "dim", scatter_dimension=0, tiled=True)


class Place:
    def __init__(self, nz, nx):
        self.y, e, self.d = (lax.axis_index(a) for a in AXES)
        z, x = lax.div(e, nx), lax.rem(e, nx)
        u = jnp.where(self.d == 0, z, nz - 1 - z)
        self.owner = u < nz // 2
        local = jnp.where(self.d == 0, lax.rem(u, 2), nz // 2 - 1 - lax.rem(u, 2))
        self.column = local * nx + x


ORDER = (0, 2, 1, 3)


def block_copies(fisher_ref, block, start, held_ref, sem):
    rows, width = held_ref.shape
    step = 512
    columns = pl.ds(pl.multiple_of(block * width, width), width)
    return [
        pltpu.make_async_copy(
            fisher_ref.at[pl.ds(start + i * step, step), columns],
            held_ref.at[pl.ds(i * step, step), :],
            sem.at[i],
        )
        for i in range(rows // step)
    ]


def times(chunk_ref, fisher):
    return lax.dot_general(chunk_ref[...], fisher, NT, preferred_element_type=jnp.float32)


def fisher_kernel(dims, n_parts, has_base, fetch, *refs):
    if fetch:
        column = Place(*dims).column
        fisher_ref, *refs = refs
    n_in = n_parts + bool(n_parts)
    chunk_ref, parts = (refs[0], refs[1:n_in]) if n_parts else (None, ())
    base_ref = refs[n_in] if has_base else None
    outs, sem = refs[n_in + has_base : -1], refs[-1]
    held = outs[1:] if n_parts else outs
    copies = []
    for k, (piece, start, _) in enumerate(fetch):
        for copy in block_copies(fisher_ref, column ^ ORDER[piece], start, held[k], sem.at[k]):
            copy.start()
            copies.append(copy)

    if parts:
        loops = 2 if fetch else 1

        @pl.loop(0, loops)
        def _(i):
            before = 0
            for part_ref in parts:
                rows = part_ref.shape[0]
                step = rows // loops
                start = pl.multiple_of(i * step, step)
                columns = pl.ds(before + start, step)
                term = times(chunk_ref, part_ref[pl.ds(start, step), :])
                outs[0][:, columns] = term + base_ref[:, columns] if has_base else term
                before += rows

    for copy in copies:
        copy.wait()


def fisher_step(fisher, dims, width, fetch, chunk=None, parts=(), base=None):
    total = fisher.shape[0]
    ins = [] if chunk is None else [chunk, *parts]
    has_base = base is not None
    out_shape = [] if chunk is None else [jax.ShapeDtypeStruct((chunk.shape[0], total), jnp.float32)]
    out_shape += [jax.ShapeDtypeStruct((rows, width), fisher.dtype) for _, _, rows in fetch]
    fetched = sum(rows for _, _, rows in fetch)
    return pl.pallas_call(
        functools.partial(fisher_kernel, dims, len(parts), has_base, fetch),
        out_shape=out_shape,
        in_specs=[HBM] * bool(fetch) + [VMEM] * (len(ins) + has_base),
        out_specs=[VMEM] * len(out_shape),
        scratch_shapes=[pltpu.SemaphoreType.DMA((max(len(fetch), 1), 2))],
        compiler_params=limit(34 if chunk is None else 20),
        cost_estimate=pl.CostEstimate(
            flops=0 if chunk is None else 2 * chunk.shape[0] * width * total,
            bytes_accessed=2 * width * (fetched + total * bool(ins)),
            transcendentals=0,
        ),
    )(*([fisher] if fetch else []), *ins, *([base] if has_base else []))


def score_kernel(dims, order, has_base, *refs):
    n = len(order)
    column = Place(*dims).column if dims else 0
    grads_ref, out_ref = refs[n], refs[-1]
    width = refs[0].shape[1]
    total = refs[n + 1][...] if has_base else None
    for k in range(n):
        block = column ^ order[k]
        start = pl.multiple_of(block * width, width) if dims else block * width
        term = times(refs[k], grads_ref[:, pl.ds(start, width)])
        total = term if total is None else total + term
    out_ref[...] = total


def score_dot(pieces, order, dims, grads, base=None):
    n = len(pieces)
    rows, width = pieces[0].shape
    operands = [*pieces, grads] + ([] if base is None else [base])
    return pl.pallas_call(
        functools.partial(score_kernel, dims, order, base is not None),
        out_shape=jax.ShapeDtypeStruct((rows, grads.shape[0]), jnp.float32),
        in_specs=[VMEM] * len(operands),
        out_specs=VMEM,
        compiler_params=limit(8),
        cost_estimate=pl.CostEstimate(
            flops=2 * n * rows * width * grads.shape[0],
            bytes_accessed=2 * n * width * grads.shape[0],
            transcendentals=0,
        ),
    )(*operands)


def cut_kernel(dims, order, src_ref, out_ref, sem):
    column = Place(*dims).column
    width = out_ref.shape[1] // len(order)
    copies = []
    for k, mask in enumerate(order):
        start = pl.multiple_of((column ^ mask) * width, width)
        copies.append(
            pltpu.make_async_copy(
                src_ref.at[:, pl.ds(start, width)], out_ref.at[:, k * width : (k + 1) * width], sem.at[k]
            )
        )
        copies[-1].start()
    for copy in copies:
        copy.wait()


def cut(src, order, dims, width):
    n = len(order)
    return pl.pallas_call(
        functools.partial(cut_kernel, dims, order),
        out_shape=jax.ShapeDtypeStruct((src.shape[0], n * width), src.dtype),
        in_specs=[HBM],
        out_specs=VMEM,
        scratch_shapes=[pltpu.SemaphoreType.DMA((n,))],
        compiler_params=limit(51),
        cost_estimate=pl.CostEstimate(
            flops=0, bytes_accessed=2 * n * width * src.shape[0], transcendentals=0
        ),
    )(src)


def pick_kernel(dims, mine_ref, other_ref, *refs):
    out_ref = refs[-1]
    owner = Place(*dims).owner

    @pl.when(owner)
    def _():
        out_ref[...] = mine_ref[...]

    @pl.when(jnp.logical_not(owner))
    def _():
        out_ref[...] = other_ref[...]


def pick(dims, mine, other, after=()):
    return pl.pallas_call(
        functools.partial(pick_kernel, dims),
        out_shape=jax.ShapeDtypeStruct(mine.shape, mine.dtype),
        in_specs=[VMEM] * 2 + [ANY] * len(after),
        out_specs=VMEM,
        compiler_params=limit(2),
        cost_estimate=pl.CostEstimate(flops=0, bytes_accessed=4 * mine.size, transcendentals=0),
    )(mine, other, *after)


def sort_kernel(mine_ref, other_ref, theirs_ref, keep_ref, give_ref):
    here = lax.axis_index("dim") == lax.axis_index("grp")
    mine, other = mine_ref[...], other_ref[...] + theirs_ref[...]
    keep_ref[...] = jnp.where(here, mine, other)
    give_ref[...] = jnp.where(here, other, mine)


def sort_out(mine, other, theirs):
    return pl.pallas_call(
        sort_kernel,
        out_shape=[jax.ShapeDtypeStruct(mine.shape, mine.dtype)] * 2,
        in_specs=[VMEM] * 3,
        out_specs=[VMEM] * 2,
        compiler_params=limit(2),
    )(mine, other, theirs)


def per_device_quad(nz, nx, ny, queries, inverse_fisher, stored_grads):
    nex, dims = nz * nx, (nz, nx)
    near = nz // 2
    nq = queries.shape[0]

    def move(value, target):
        pairs = []
        for sy in range(ny):
            for sz in range(nz):
                for sx in range(nx):
                    for sd in range(2):
                        to = target(sy, sz, sx, sd)
                        if to is not None:
                            ty, tz, tx, td = to
                            pairs.append(((sy * nex + sz * nx + sx) * 2 + sd, (ty * nex + tz * nx + tx) * 2 + td))
        return lax.ppermute(value, AXES, pairs)

    def along_z(value, hops, flip=False):
        def target(sy, sz, sx, sd):
            su = sz if sd == 0 else nz - 1 - sz
            if su not in hops:
                return None
            tu = hops[su]
            return sy, tu if sd == 0 else nz - 1 - tu, 1 - sx if flip else sx, sd

        return move(value, target)

    def swap_y(value):
        return move(value, lambda sy, sz, sx, sd: (1 - sy, sz, sx, sd))

    def swap_core(value):
        return move(value, lambda sy, sz, sx, sd: (sy, sz, sx, 1 - sd))

    def gather(own, direct, after=()):
        def start(sy, sz, sx, sd):
            su = sz if sd == 0 else nz - 1 - sz
            if su < near:
                return sy, sz + 2 if sd == 0 else sz - 2, sx, sd
            return sy, sz ^ 1, 1 - sx, 1 - sd

        def start_direct(sy, sz, sx, sd):
            su = sz if sd == 0 else nz - 1 - sz
            if su < near:
                return sy, nz - 1 - sz, 1 - sx, sd
            return sy, sz, 1 - sx, 1 - sd

        came = move(own, start)
        if direct:
            came_too = move(own, start_direct)
        first = pick(dims, own, came, after)
        pairs = {0: 1, 1: 0, 2: 3, 3: 2}
        beside = along_z(first, pairs)
        if direct:
            across = along_z(first, {2: 2, 3: 3}, True)
            beside, came_too = lax.optimization_barrier((beside, came_too))
        else:
            across = along_z(first, {0: 0, 1: 1, 2: 2, 3: 3}, True)

        def last(before, after):
            if direct:
                ready, _ = lax.optimization_barrier((came, after))
                return pick(dims, ready, came_too)
            ready, _ = lax.optimization_barrier((first, before))
            piece, _ = lax.optimization_barrier((along_z(ready, pairs, True), after))
            return piece

        def third(after):
            if direct:
                ready, _ = lax.optimization_barrier((came_too, after))
                return pick(dims, ready, across)
            return across

        return first, beside, third, last

    rows, width = nq // ny, queries.shape[1]
    to_y = cut(stored_grads, ORDER[1:], dims, width)
    queries, to_y = lax.optimization_barrier((queries, to_y))
    own = lax.dynamic_slice_in_dim(queries, lax.axis_index("grp") * rows, rows, axis=0)
    own, to_y = lax.optimization_barrier((own, to_y))
    other_grads = swap_y(to_y)
    step = functools.partial(fisher_step, inverse_fisher, dims, width)
    half, quarter = inverse_fisher.shape[0] // 2, inverse_fisher.shape[0] // 4
    a0, a1, b0, b1 = step(((0, 0, half), (0, half, half), (1, 0, half), (1, half, quarter)))
    q0, q1, third, last = gather(own, False, (a0,))
    total0, b2, c0 = step(((1, half + quarter, quarter), (2, 0, half)), q0, (a0, a1))
    total, c1, d0 = step(((2, half, half), (3, 0, quarter)), q1, (b0, b1, b2), total0)
    total, d1, d2 = step(((3, quarter, quarter), (3, half, half)), third(total), (c0, c1), total)
    (total,) = step((), last(total0, total), (d0, d1, d2), total)
    panel = (total + swap_core(total)).astype(jnp.bfloat16)

    p0, p1, third, last = gather(panel, True)
    swapped = swap_y(p0)
    p1, other_grads = lax.optimization_barrier((p1, other_grads))
    p3 = last(p1, p1)
    other = score_dot([p1, p3], (0, 2), None, other_grads)
    p2 = third(other)
    other = score_dot([p2], (1,), None, other_grads, other)
    p2, swapped, _ = lax.optimization_barrier((p2, swapped, other))
    mine = score_dot([p0, p1, p2, p3], ORDER, dims, stored_grads)
    theirs = score_dot([swapped], ORDER[:1], dims, stored_grads)

    keep, give = sort_out(mine, swap_y(other), theirs)
    return keep + swap_core(give)


def solution(mesh):
    coords = [getattr(device, "coords", None) for device in mesh.devices.flat]
    nx = 2 if None in coords else len({c[0] for c in coords})
    nz = mesh.shape["ex"] // nx
    ny = mesh.shape["grp"]
    if (nz, nx, ny) == (4, 2, 2):
        body = functools.partial(per_device_quad, nz, nx, ny)
    else:
        body = per_device_any
    return jax.shard_map(
        body,
        mesh=mesh,
        in_specs=(P(None, "ex"), P("ex", "dim"), P(("grp", "ex"), "dim")),
        out_specs=P("dim", ("grp", "ex")),
        check_vma=False,
    )
```

```python
import functools

import jax
import jax.numpy as jnp
from jax import lax
from jax.experimental import pallas as pl
from jax.experimental.pallas import tpu as pltpu
from jax.sharding import PartitionSpec as P

AXES = ("grp", "ex", "dim")
NT = (((1,), (1,)), ((), ()))
VMEM = pl.BlockSpec(memory_space=pltpu.VMEM)
HBM = pl.BlockSpec(memory_space=pltpu.HBM)
ANY = pl.BlockSpec(memory_space=pl.ANY)


def limit(mib):
    return pltpu.CompilerParams(vmem_limit_bytes=mib * 1024 * 1024)


def per_device_any(queries, inverse_fisher, stored_grads):
    term_block = jnp.dot(queries, inverse_fisher, preferred_element_type=jnp.float32)
    own_panel = lax.psum_scatter(term_block, "ex", scatter_dimension=1, tiled=True).astype(
        jnp.bfloat16
    )
    partial_scores = lax.dot_general(
        lax.all_gather(own_panel, "ex", axis=1, tiled=True),
        stored_grads,
        NT,
        preferred_element_type=jnp.float32,
    )
    return lax.psum_scatter(partial_scores, "dim", scatter_dimension=0, tiled=True)


class Place:
    def __init__(self, nz, nx):
        self.y, e, self.d = (lax.axis_index(a) for a in AXES)
        z, x = lax.div(e, nx), lax.rem(e, nx)
        u = jnp.where(self.d == 0, z, nz - 1 - z)
        self.owner = u < nz // 2
        local = jnp.where(self.d == 0, lax.rem(u, 2), nz // 2 - 1 - lax.rem(u, 2))
        self.column = local * nx + x


ORDER = (0, 2, 1, 3)


def block_copies(fisher_ref, block, start, held_ref, sem):
    rows, width = held_ref.shape
    step = 512
    columns = pl.ds(pl.multiple_of(block * width, width), width)
    return [
        pltpu.make_async_copy(
            fisher_ref.at[pl.ds(start + i * step, step), columns],
            held_ref.at[pl.ds(i * step, step), :],
            sem.at[i],
        )
        for i in range(rows // step)
    ]


def times(chunk_ref, fisher):
    return lax.dot_general(chunk_ref[...], fisher, NT, preferred_element_type=jnp.float32)


def fisher_kernel(dims, n_parts, has_base, fetch, *refs):
    if fetch:
        column = Place(*dims).column
        fisher_ref, *refs = refs
    n_in = n_parts + bool(n_parts)
    chunk_ref, parts = (refs[0], refs[1:n_in]) if n_parts else (None, ())
    base_ref = refs[n_in] if has_base else None
    outs, sem = refs[n_in + has_base : -1], refs[-1]
    held = outs[1:] if n_parts else outs
    copies = []
    for k, (piece, start, _) in enumerate(fetch):
        for copy in block_copies(fisher_ref, column ^ ORDER[piece], start, held[k], sem.at[k]):
            copy.start()
            copies.append(copy)

    if parts:
        loops = 2 if fetch else 1

        @pl.loop(0, loops)
        def _(i):
            before = 0
            for part_ref in parts:
                rows = part_ref.shape[0]
                step = rows // loops
                start = pl.multiple_of(i * step, step)
                columns = pl.ds(before + start, step)
                term = times(chunk_ref, part_ref[pl.ds(start, step), :])
                outs[0][:, columns] = term + base_ref[:, columns] if has_base else term
                before += rows

    for copy in copies:
        copy.wait()


def fisher_step(fisher, dims, width, fetch, chunk=None, parts=(), base=None):
    total = fisher.shape[0]
    ins = [] if chunk is None else [chunk, *parts]
    has_base = base is not None
    out_shape = [] if chunk is None else [jax.ShapeDtypeStruct((chunk.shape[0], total), jnp.float32)]
    out_shape += [jax.ShapeDtypeStruct((rows, width), fisher.dtype) for _, _, rows in fetch]
    fetched = sum(rows for _, _, rows in fetch)
    return pl.pallas_call(
        functools.partial(fisher_kernel, dims, len(parts), has_base, fetch),
        out_shape=out_shape,
        in_specs=[HBM] * bool(fetch) + [VMEM] * (len(ins) + has_base),
        out_specs=[VMEM] * len(out_shape),
        scratch_shapes=[pltpu.SemaphoreType.DMA((max(len(fetch), 1), 2))],
        compiler_params=limit(34 if chunk is None else 20),
        cost_estimate=pl.CostEstimate(
            flops=0 if chunk is None else 2 * chunk.shape[0] * width * total,
            bytes_accessed=2 * width * (fetched + total * bool(ins)),
            transcendentals=0,
        ),
    )(*([fisher] if fetch else []), *ins, *([base] if has_base else []))


def score_kernel(dims, order, has_base, *refs):
    n = len(order)
    column = Place(*dims).column if dims else 0
    grads_ref, out_ref = refs[n], refs[-1]
    width = refs[0].shape[1]
    total = refs[n + 1][...] if has_base else None
    for k in range(n):
        block = column ^ order[k]
        start = pl.multiple_of(block * width, width) if dims else block * width
        term = times(refs[k], grads_ref[:, pl.ds(start, width)])
        total = term if total is None else total + term
    out_ref[...] = total


def score_dot(pieces, order, dims, grads, base=None):
    n = len(pieces)
    rows, width = pieces[0].shape
    operands = [*pieces, grads] + ([] if base is None else [base])
    return pl.pallas_call(
        functools.partial(score_kernel, dims, order, base is not None),
        out_shape=jax.ShapeDtypeStruct((rows, grads.shape[0]), jnp.float32),
        in_specs=[VMEM] * len(operands),
        out_specs=VMEM,
        compiler_params=limit(8),
        cost_estimate=pl.CostEstimate(
            flops=2 * n * rows * width * grads.shape[0],
            bytes_accessed=2 * n * width * grads.shape[0],
            transcendentals=0,
        ),
    )(*operands)


def cut_kernel(dims, order, src_ref, out_ref, sem):
    column = Place(*dims).column
    width = out_ref.shape[1] // len(order)
    copies = []
    for k, mask in enumerate(order):
        start = pl.multiple_of((column ^ mask) * width, width)
        copies.append(
            pltpu.make_async_copy(
                src_ref.at[:, pl.ds(start, width)], out_ref.at[:, k * width : (k + 1) * width], sem.at[k]
            )
        )
        copies[-1].start()
    for copy in copies:
        copy.wait()


def cut(src, order, dims, width):
    n = len(order)
    return pl.pallas_call(
        functools.partial(cut_kernel, dims, order),
        out_shape=jax.ShapeDtypeStruct((src.shape[0], n * width), src.dtype),
        in_specs=[HBM],
        out_specs=VMEM,
        scratch_shapes=[pltpu.SemaphoreType.DMA((n,))],
        compiler_params=limit(51),
        cost_estimate=pl.CostEstimate(
            flops=0, bytes_accessed=2 * n * width * src.shape[0], transcendentals=0
        ),
    )(src)


def pick_kernel(dims, mine_ref, other_ref, *refs):
    out_ref = refs[-1]
    owner = Place(*dims).owner

    @pl.when(owner)
    def _():
        out_ref[...] = mine_ref[...]

    @pl.when(jnp.logical_not(owner))
    def _():
        out_ref[...] = other_ref[...]


def pick(dims, mine, other, after=()):
    return pl.pallas_call(
        functools.partial(pick_kernel, dims),
        out_shape=jax.ShapeDtypeStruct(mine.shape, mine.dtype),
        in_specs=[VMEM] * 2 + [ANY] * len(after),
        out_specs=VMEM,
        compiler_params=limit(2),
        cost_estimate=pl.CostEstimate(flops=0, bytes_accessed=4 * mine.size, transcendentals=0),
    )(mine, other, *after)


def sort_kernel(mine_ref, other_ref, theirs_ref, keep_ref, give_ref):
    here = lax.axis_index("dim") == lax.axis_index("grp")
    mine, other = mine_ref[...], other_ref[...] + theirs_ref[...]
    keep_ref[...] = jnp.where(here, mine, other)
    give_ref[...] = jnp.where(here, other, mine)


def sort_out(mine, other, theirs):
    return pl.pallas_call(
        sort_kernel,
        out_shape=[jax.ShapeDtypeStruct(mine.shape, mine.dtype)] * 2,
        in_specs=[VMEM] * 3,
        out_specs=[VMEM] * 2,
        compiler_params=limit(2),
    )(mine, other, theirs)


def per_device_quad(nz, nx, ny, queries, inverse_fisher, stored_grads):
    nex, dims = nz * nx, (nz, nx)
    near = nz // 2
    nq = queries.shape[0]

    def move(value, target):
        pairs = []
        for sy in range(ny):
            for sz in range(nz):
                for sx in range(nx):
                    for sd in range(2):
                        to = target(sy, sz, sx, sd)
                        if to is not None:
                            ty, tz, tx, td = to
                            pairs.append(((sy * nex + sz * nx + sx) * 2 + sd, (ty * nex + tz * nx + tx) * 2 + td))
        return lax.ppermute(value, AXES, pairs)

    def along_z(value, hops, flip=False):
        def target(sy, sz, sx, sd):
            su = sz if sd == 0 else nz - 1 - sz
            if su not in hops:
                return None
            tu = hops[su]
            return sy, tu if sd == 0 else nz - 1 - tu, 1 - sx if flip else sx, sd

        return move(value, target)

    def swap_y(value):
        return move(value, lambda sy, sz, sx, sd: (1 - sy, sz, sx, sd))

    def swap_core(value):
        return move(value, lambda sy, sz, sx, sd: (sy, sz, sx, 1 - sd))

    def gather(own, direct, after=()):
        def start(sy, sz, sx, sd):
            su = sz if sd == 0 else nz - 1 - sz
            if su < near:
                return sy, sz + 2 if sd == 0 else sz - 2, sx, sd
            return sy, sz ^ 1, 1 - sx, 1 - sd

        def start_direct(sy, sz, sx, sd):
            su = sz if sd == 0 else nz - 1 - sz
            if su < near:
                return sy, nz - 1 - sz, 1 - sx, sd
            return sy, sz, 1 - sx, 1 - sd

        def far_x(sy, sz, sx, sd):
            su = sz if sd == 0 else nz - 1 - sz
            return (1 - sy, sz, sx, sd) if su < near else (sy, sz, 1 - sx, sd)

        came = move(own, start)
        if direct:
            came_too = move(own, start_direct)
        first = pick(dims, own, came, after)
        pairs = {0: 1, 1: 0, 2: 3, 3: 2}
        beside = along_z(first, pairs)
        if direct:
            across = move(first, far_x)
            beside, came_too = lax.optimization_barrier((beside, came_too))
        else:
            across = along_z(first, {0: 0, 1: 1, 2: 2, 3: 3}, True)

        def last(before, after):
            if direct:
                ready, _ = lax.optimization_barrier((came, after))
                return pick(dims, ready, came_too)
            ready, _ = lax.optimization_barrier((first, before))
            piece, _ = lax.optimization_barrier((along_z(ready, pairs, True), after))
            return piece

        def third(after):
            if direct:
                ready, _ = lax.optimization_barrier((came_too, after))
                return pick(dims, ready, across)
            return across

        return first, beside, third, last

    rows, width = nq // ny, queries.shape[1]
    to_y = cut(stored_grads, ORDER[1:], dims, width)
    queries, to_y = lax.optimization_barrier((queries, to_y))
    own = lax.dynamic_slice_in_dim(queries, lax.axis_index("grp") * rows, rows, axis=0)
    own, to_y = lax.optimization_barrier((own, to_y))
    other_grads = swap_y(to_y)
    step = functools.partial(fisher_step, inverse_fisher, dims, width)
    half, quarter = inverse_fisher.shape[0] // 2, inverse_fisher.shape[0] // 4
    a0, a1, b0, b1 = step(((0, 0, half), (0, half, half), (1, 0, half), (1, half, quarter)))
    q0, q1, third, last = gather(own, False, (a0,))
    total0, b2, c0 = step(((1, half + quarter, quarter), (2, 0, half)), q0, (a0, a1))
    total, c1, d0 = step(((2, half, half), (3, 0, quarter)), q1, (b0, b1, b2), total0)
    total, d1, d2 = step(((3, quarter, quarter), (3, half, half)), third(total), (c0, c1), total)
    (total,) = step((), last(total0, total), (d0, d1, d2), total)
    panel = (total + swap_core(total)).astype(jnp.bfloat16)

    p0, p1, third, last = gather(panel, True)
    swapped = swap_y(p0)
    p1, other_grads = lax.optimization_barrier((p1, other_grads))
    p3 = last(p1, p1)
    other = score_dot([p1, p3], (0, 2), None, other_grads)
    p2 = third(other)
    other = score_dot([p2], (1,), None, other_grads, other)
    p2, swapped, _ = lax.optimization_barrier((p2, swapped, other))
    mine = score_dot([p0, p1, p2, p3], ORDER, dims, stored_grads)
    theirs = score_dot([swapped], ORDER[:1], dims, stored_grads)

    keep, give = sort_out(mine, swap_y(other), theirs)
    return keep + swap_core(give)


def solution(mesh):
    coords = [getattr(device, "coords", None) for device in mesh.devices.flat]
    nx = 2 if None in coords else len({c[0] for c in coords})
    nz = mesh.shape["ex"] // nx
    ny = mesh.shape["grp"]
    if (nz, nx, ny) == (4, 2, 2):
        body = functools.partial(per_device_quad, nz, nx, ny)
    else:
        body = per_device_any
    return jax.shard_map(
        body,
        mesh=mesh,
        in_specs=(P(None, "ex"), P("ex", "dim"), P(("grp", "ex"), "dim")),
        out_specs=P("dim", ("grp", "ex")),
        check_vma=False,
    )
```

```python
import functools

import jax
import jax.numpy as jnp
from jax import lax
from jax.experimental import pallas as pl
from jax.experimental.pallas import tpu as pltpu
from jax.sharding import PartitionSpec as P

AXES = ("grp", "ex", "dim")
NT = (((1,), (1,)), ((), ()))
VMEM = pl.BlockSpec(memory_space=pltpu.VMEM)
HBM = pl.BlockSpec(memory_space=pltpu.HBM)
ANY = pl.BlockSpec(memory_space=pl.ANY)


def limit(mib):
    return pltpu.CompilerParams(vmem_limit_bytes=mib * 1024 * 1024)


def per_device_any(queries, inverse_fisher, stored_grads):
    term_block = jnp.dot(queries, inverse_fisher, preferred_element_type=jnp.float32)
    own_panel = lax.psum_scatter(term_block, "ex", scatter_dimension=1, tiled=True).astype(
        jnp.bfloat16
    )
    partial_scores = lax.dot_general(
        lax.all_gather(own_panel, "ex", axis=1, tiled=True),
        stored_grads,
        NT,
        preferred_element_type=jnp.float32,
    )
    return lax.psum_scatter(partial_scores, "dim", scatter_dimension=0, tiled=True)


class Place:
    def __init__(self, nz, nx):
        self.y, e, self.d = (lax.axis_index(a) for a in AXES)
        z, x = lax.div(e, nx), lax.rem(e, nx)
        u = jnp.where(self.d == 0, z, nz - 1 - z)
        self.owner = u < nz // 2
        local = jnp.where(self.d == 0, lax.rem(u, 2), nz // 2 - 1 - lax.rem(u, 2))
        self.column = local * nx + x


ORDER = (0, 2, 1, 3)


def block_copies(fisher_ref, block, start, held_ref, sem):
    rows, width = held_ref.shape
    step = 512
    columns = pl.ds(pl.multiple_of(block * width, width), width)
    return [
        pltpu.make_async_copy(
            fisher_ref.at[pl.ds(start + i * step, step), columns],
            held_ref.at[pl.ds(i * step, step), :],
            sem.at[i],
        )
        for i in range(rows // step)
    ]


def times(chunk_ref, fisher):
    return lax.dot_general(chunk_ref[...], fisher, NT, preferred_element_type=jnp.float32)


def fisher_kernel(dims, n_parts, has_base, fetch, *refs):
    if fetch:
        column = Place(*dims).column
        fisher_ref, *refs = refs
    n_in = n_parts + bool(n_parts)
    chunk_ref, parts = (refs[0], refs[1:n_in]) if n_parts else (None, ())
    base_ref = refs[n_in] if has_base else None
    outs, sem = refs[n_in + has_base : -1], refs[-1]
    held = outs[1:] if n_parts else outs
    copies = []
    for k, (piece, start, _) in enumerate(fetch):
        for copy in block_copies(fisher_ref, column ^ ORDER[piece], start, held[k], sem.at[k]):
            copy.start()
            copies.append(copy)

    if parts:
        loops = 2 if fetch else 1

        @pl.loop(0, loops)
        def _(i):
            before = 0
            for part_ref in parts:
                rows = part_ref.shape[0]
                step = rows // loops
                start = pl.multiple_of(i * step, step)
                columns = pl.ds(before + start, step)
                term = times(chunk_ref, part_ref[pl.ds(start, step), :])
                outs[0][:, columns] = term + base_ref[:, columns] if has_base else term
                before += rows

    for copy in copies:
        copy.wait()


def fisher_step(fisher, dims, width, fetch, chunk=None, parts=(), base=None):
    total = fisher.shape[0]
    ins = [] if chunk is None else [chunk, *parts]
    has_base = base is not None
    out_shape = [] if chunk is None else [jax.ShapeDtypeStruct((chunk.shape[0], total), jnp.float32)]
    out_shape += [jax.ShapeDtypeStruct((rows, width), fisher.dtype) for _, _, rows in fetch]
    fetched = sum(rows for _, _, rows in fetch)
    return pl.pallas_call(
        functools.partial(fisher_kernel, dims, len(parts), has_base, fetch),
        out_shape=out_shape,
        in_specs=[HBM] * bool(fetch) + [VMEM] * (len(ins) + has_base),
        out_specs=[VMEM] * len(out_shape),
        scratch_shapes=[pltpu.SemaphoreType.DMA((max(len(fetch), 1), 2))],
        compiler_params=limit(34 if chunk is None else 20),
        cost_estimate=pl.CostEstimate(
            flops=0 if chunk is None else 2 * chunk.shape[0] * width * total,
            bytes_accessed=2 * width * (fetched + total * bool(ins)),
            transcendentals=0,
        ),
    )(*([fisher] if fetch else []), *ins, *([base] if has_base else []))


def score_kernel(dims, order, has_base, *refs):
    n = len(order)
    column = Place(*dims).column if dims else 0
    grads_ref, out_ref = refs[n], refs[-1]
    width = refs[0].shape[1]
    total = refs[n + 1][...] if has_base else None
    for k in range(n):
        block = column ^ order[k]
        start = pl.multiple_of(block * width, width) if dims else block * width
        term = times(refs[k], grads_ref[:, pl.ds(start, width)])
        total = term if total is None else total + term
    out_ref[...] = total


def score_dot(pieces, order, dims, grads, base=None):
    n = len(pieces)
    rows, width = pieces[0].shape
    operands = [*pieces, grads] + ([] if base is None else [base])
    return pl.pallas_call(
        functools.partial(score_kernel, dims, order, base is not None),
        out_shape=jax.ShapeDtypeStruct((rows, grads.shape[0]), jnp.float32),
        in_specs=[VMEM] * len(operands),
        out_specs=VMEM,
        compiler_params=limit(8),
        cost_estimate=pl.CostEstimate(
            flops=2 * n * rows * width * grads.shape[0],
            bytes_accessed=2 * n * width * grads.shape[0],
            transcendentals=0,
        ),
    )(*operands)


def cut_kernel(dims, order, src_ref, out_ref, sem):
    column = Place(*dims).column
    width = out_ref.shape[1] // len(order)
    copies = []
    for k, mask in enumerate(order):
        start = pl.multiple_of((column ^ mask) * width, width)
        copies.append(
            pltpu.make_async_copy(
                src_ref.at[:, pl.ds(start, width)], out_ref.at[:, k * width : (k + 1) * width], sem.at[k]
            )
        )
        copies[-1].start()
    for copy in copies:
        copy.wait()


def cut(src, order, dims, width):
    n = len(order)
    return pl.pallas_call(
        functools.partial(cut_kernel, dims, order),
        out_shape=jax.ShapeDtypeStruct((src.shape[0], n * width), src.dtype),
        in_specs=[HBM],
        out_specs=VMEM,
        scratch_shapes=[pltpu.SemaphoreType.DMA((n,))],
        compiler_params=limit(51),
        cost_estimate=pl.CostEstimate(
            flops=0, bytes_accessed=2 * n * width * src.shape[0], transcendentals=0
        ),
    )(src)


def pick_kernel(dims, mine_ref, other_ref, *refs):
    out_ref = refs[-1]
    owner = Place(*dims).owner

    @pl.when(owner)
    def _():
        out_ref[...] = mine_ref[...]

    @pl.when(jnp.logical_not(owner))
    def _():
        out_ref[...] = other_ref[...]


def pick(dims, mine, other, after=()):
    return pl.pallas_call(
        functools.partial(pick_kernel, dims),
        out_shape=jax.ShapeDtypeStruct(mine.shape, mine.dtype),
        in_specs=[VMEM] * 2 + [ANY] * len(after),
        out_specs=VMEM,
        compiler_params=limit(2),
        cost_estimate=pl.CostEstimate(flops=0, bytes_accessed=4 * mine.size, transcendentals=0),
    )(mine, other, *after)


def sort_kernel(mine_ref, other_ref, theirs_ref, keep_ref, give_ref):
    here = lax.axis_index("dim") == lax.axis_index("grp")
    mine, other = mine_ref[...], other_ref[...] + theirs_ref[...]
    keep_ref[...] = jnp.where(here, mine, other)
    give_ref[...] = jnp.where(here, other, mine)


def sort_out(mine, other, theirs):
    return pl.pallas_call(
        sort_kernel,
        out_shape=[jax.ShapeDtypeStruct(mine.shape, mine.dtype)] * 2,
        in_specs=[VMEM] * 3,
        out_specs=[VMEM] * 2,
        compiler_params=limit(2),
    )(mine, other, theirs)


def per_device_quad(nz, nx, ny, queries, inverse_fisher, stored_grads):
    nex, dims = nz * nx, (nz, nx)
    near = nz // 2
    nq = queries.shape[0]

    def move(value, target):
        pairs = []
        for sy in range(ny):
            for sz in range(nz):
                for sx in range(nx):
                    for sd in range(2):
                        to = target(sy, sz, sx, sd)
                        if to is not None:
                            ty, tz, tx, td = to
                            pairs.append(((sy * nex + sz * nx + sx) * 2 + sd, (ty * nex + tz * nx + tx) * 2 + td))
        return lax.ppermute(value, AXES, pairs)

    def along_z(value, hops, flip=False):
        def target(sy, sz, sx, sd):
            su = sz if sd == 0 else nz - 1 - sz
            if su not in hops:
                return None
            tu = hops[su]
            return sy, tu if sd == 0 else nz - 1 - tu, 1 - sx if flip else sx, sd

        return move(value, target)

    def swap_y(value):
        return move(value, lambda sy, sz, sx, sd: (1 - sy, sz, sx, sd))

    def swap_core(value):
        return move(value, lambda sy, sz, sx, sd: (sy, sz, sx, 1 - sd))

    def gather(own, direct, after=()):
        def start(sy, sz, sx, sd):
            su = sz if sd == 0 else nz - 1 - sz
            if su < near:
                return sy, sz + 2 if sd == 0 else sz - 2, sx, sd
            return sy, sz ^ 1, 1 - sx, 1 - sd

        def help_beside(sy, sz, sx, sd):
            su = sz if sd == 0 else nz - 1 - sz
            return sy, sz if su < near else sz ^ 1, sx, 1 - sd

        def help_across(sy, sz, sx, sd):
            su = sz if sd == 0 else nz - 1 - sz
            return sy, sz, sx if su < near else 1 - sx, 1 - sd

        def among_far(flip_z, flip_x):
            def target(sy, sz, sx, sd):
                su = sz if sd == 0 else nz - 1 - sz
                if su < near:
                    return 1 - sy, sz, sx, sd
                return sy, sz ^ flip_z, sx ^ flip_x, sd

            return target

        came = move(own, start)
        if direct:
            helped = [move(own, help_beside), move(own, help_across)]
        first = pick(dims, own, came, after)
        if direct:
            beside, across, corner = (move(first, among_far(*f)) for f in ((1, 0), (0, 1), (1, 1)))
            beside, *helped = lax.optimization_barrier((beside, *helped))

            def later(mine, other):
                def take(after):
                    ready, _ = lax.optimization_barrier((mine, after))
                    return pick(dims, ready, other)

                return take

            return first, later(helped[0], beside), later(helped[1], across), later(came, corner)

        pairs = {0: 1, 1: 0, 2: 3, 3: 2}

        def corner(before, after):
            ready, _ = lax.optimization_barrier((first, before))
            return lax.optimization_barrier((along_z(ready, pairs, True), after))[0]

        across = along_z(first, {0: 0, 1: 1, 2: 2, 3: 3}, True)
        return first, along_z(first, pairs), across, corner

    rows, width = nq // ny, queries.shape[1]
    to_y = cut(stored_grads, ORDER[1:], dims, width)
    queries, to_y = lax.optimization_barrier((queries, to_y))
    own = lax.dynamic_slice_in_dim(queries, lax.axis_index("grp") * rows, rows, axis=0)
    own, to_y = lax.optimization_barrier((own, to_y))
    other_grads = swap_y(to_y)
    step = functools.partial(fisher_step, inverse_fisher, dims, width)
    half, quarter = inverse_fisher.shape[0] // 2, inverse_fisher.shape[0] // 4
    a0, a1, b0, b1 = step(((0, 0, half), (0, half, half), (1, 0, half), (1, half, quarter)))
    q0, q1, q2, last = gather(own, False, (a0,))
    total0, b2, c0 = step(((1, half + quarter, quarter), (2, 0, half)), q0, (a0, a1))
    total, c1, d0 = step(((2, half, half), (3, 0, quarter)), q1, (b0, b1, b2), total0)
    total, d1, d2 = step(((3, quarter, quarter), (3, half, half)), q2, (c0, c1), total)
    (total,) = step((), last(total0, total), (d0, d1, d2), total)
    panel = (total + swap_core(total)).astype(jnp.bfloat16)

    p0, second, third, fourth = gather(panel, True)
    swapped = swap_y(p0)
    p1 = second(p0)
    p1, other_grads = lax.optimization_barrier((p1, other_grads))
    p2 = third(p1)
    other = score_dot([p1, p2], (0, 1), None, other_grads)
    p3 = fourth(other)
    other = score_dot([p3], (2,), None, other_grads, other)
    p3, swapped, _ = lax.optimization_barrier((p3, swapped, other))
    mine = score_dot([p0, p1, p2, p3], ORDER, dims, stored_grads)
    theirs = score_dot([swapped], ORDER[:1], dims, stored_grads)

    keep, give = sort_out(mine, swap_y(other), theirs)
    return keep + swap_core(give)


def solution(mesh):
    coords = [getattr(device, "coords", None) for device in mesh.devices.flat]
    nx = 2 if None in coords else len({c[0] for c in coords})
    nz = mesh.shape["ex"] // nx
    ny = mesh.shape["grp"]
    if (nz, nx, ny) == (4, 2, 2):
        body = functools.partial(per_device_quad, nz, nx, ny)
    else:
        body = per_device_any
    return jax.shard_map(
        body,
        mesh=mesh,
        in_specs=(P(None, "ex"), P("ex", "dim"), P(("grp", "ex"), "dim")),
        out_specs=P("dim", ("grp", "ex")),
        check_vma=False,
    )
```

```python
import functools

import jax
import jax.numpy as jnp
from jax import lax
from jax.experimental import pallas as pl
from jax.experimental.pallas import tpu as pltpu
from jax.sharding import PartitionSpec as P

AXES = ("grp", "ex", "dim")
NT = (((1,), (1,)), ((), ()))
VMEM = pl.BlockSpec(memory_space=pltpu.VMEM)
HBM = pl.BlockSpec(memory_space=pltpu.HBM)
ANY = pl.BlockSpec(memory_space=pl.ANY)


def limit(mib):
    return pltpu.CompilerParams(vmem_limit_bytes=mib * 1024 * 1024)


def per_device_any(queries, inverse_fisher, stored_grads):
    term_block = jnp.dot(queries, inverse_fisher, preferred_element_type=jnp.float32)
    own_panel = lax.psum_scatter(term_block, "ex", scatter_dimension=1, tiled=True).astype(
        jnp.bfloat16
    )
    partial_scores = lax.dot_general(
        lax.all_gather(own_panel, "ex", axis=1, tiled=True),
        stored_grads,
        NT,
        preferred_element_type=jnp.float32,
    )
    return lax.psum_scatter(partial_scores, "dim", scatter_dimension=0, tiled=True)


class Place:
    def __init__(self, nz, nx):
        self.y, e, self.d = (lax.axis_index(a) for a in AXES)
        z, x = lax.div(e, nx), lax.rem(e, nx)
        u = jnp.where(self.d == 0, z, nz - 1 - z)
        self.owner = u < nz // 2
        local = jnp.where(self.d == 0, lax.rem(u, 2), nz // 2 - 1 - lax.rem(u, 2))
        self.column = local * nx + x


ORDER = (0, 2, 1, 3)


def block_copies(fisher_ref, block, start, held_ref, sem):
    rows, width = held_ref.shape
    step = 512
    columns = pl.ds(pl.multiple_of(block * width, width), width)
    return [
        pltpu.make_async_copy(
            fisher_ref.at[pl.ds(start + i * step, step), columns],
            held_ref.at[pl.ds(i * step, step), :],
            sem.at[i],
        )
        for i in range(rows // step)
    ]


def times(chunk_ref, fisher):
    return lax.dot_general(chunk_ref[...], fisher, NT, preferred_element_type=jnp.float32)


def fisher_kernel(dims, n_parts, has_base, fetch, *refs):
    if fetch:
        column = Place(*dims).column
        fisher_ref, *refs = refs
    n_in = n_parts + bool(n_parts)
    chunk_ref, parts = (refs[0], refs[1:n_in]) if n_parts else (None, ())
    base_ref = refs[n_in] if has_base else None
    outs, sem = refs[n_in + has_base : -1], refs[-1]
    held = outs[1:] if n_parts else outs
    copies = []
    for k, (piece, start, _) in enumerate(fetch):
        for copy in block_copies(fisher_ref, column ^ ORDER[piece], start, held[k], sem.at[k]):
            copy.start()
            copies.append(copy)

    if parts:
        loops = 2 if fetch else 1

        @pl.loop(0, loops)
        def _(i):
            before = 0
            for part_ref in parts:
                rows = part_ref.shape[0]
                step = rows // loops
                start = pl.multiple_of(i * step, step)
                columns = pl.ds(before + start, step)
                term = times(chunk_ref, part_ref[pl.ds(start, step), :])
                outs[0][:, columns] = term + base_ref[:, columns] if has_base else term
                before += rows

    for copy in copies:
        copy.wait()


def fisher_step(fisher, dims, width, fetch, chunk=None, parts=(), base=None):
    total = fisher.shape[0]
    ins = [] if chunk is None else [chunk, *parts]
    has_base = base is not None
    out_shape = [] if chunk is None else [jax.ShapeDtypeStruct((chunk.shape[0], total), jnp.float32)]
    out_shape += [jax.ShapeDtypeStruct((rows, width), fisher.dtype) for _, _, rows in fetch]
    fetched = sum(rows for _, _, rows in fetch)
    return pl.pallas_call(
        functools.partial(fisher_kernel, dims, len(parts), has_base, fetch),
        out_shape=out_shape,
        in_specs=[HBM] * bool(fetch) + [VMEM] * (len(ins) + has_base),
        out_specs=[VMEM] * len(out_shape),
        scratch_shapes=[pltpu.SemaphoreType.DMA((max(len(fetch), 1), 2))],
        compiler_params=limit(34 if chunk is None else 20),
        cost_estimate=pl.CostEstimate(
            flops=0 if chunk is None else 2 * chunk.shape[0] * width * total,
            bytes_accessed=2 * width * (fetched + total * bool(ins)),
            transcendentals=0,
        ),
    )(*([fisher] if fetch else []), *ins, *([base] if has_base else []))


def score_kernel(dims, order, has_base, *refs):
    n = len(order)
    column = Place(*dims).column if dims else 0
    grads_ref, out_ref = refs[n], refs[-1]
    width = refs[0].shape[1]
    total = refs[n + 1][...] if has_base else None
    for k in range(n):
        block = column ^ order[k]
        start = pl.multiple_of(block * width, width) if dims else block * width
        term = times(refs[k], grads_ref[:, pl.ds(start, width)])
        total = term if total is None else total + term
    out_ref[...] = total


def score_dot(pieces, order, dims, grads, base=None):
    n = len(pieces)
    rows, width = pieces[0].shape
    operands = [*pieces, grads] + ([] if base is None else [base])
    return pl.pallas_call(
        functools.partial(score_kernel, dims, order, base is not None),
        out_shape=jax.ShapeDtypeStruct((rows, grads.shape[0]), jnp.float32),
        in_specs=[VMEM] * len(operands),
        out_specs=VMEM,
        compiler_params=limit(8),
        cost_estimate=pl.CostEstimate(
            flops=2 * n * rows * width * grads.shape[0],
            bytes_accessed=2 * n * width * grads.shape[0],
            transcendentals=0,
        ),
    )(*operands)


def cut_kernel(dims, order, src_ref, out_ref, sem):
    column = Place(*dims).column
    width = out_ref.shape[1] // len(order)
    copies = []
    for k, mask in enumerate(order):
        start = pl.multiple_of((column ^ mask) * width, width)
        copies.append(
            pltpu.make_async_copy(
                src_ref.at[:, pl.ds(start, width)], out_ref.at[:, k * width : (k + 1) * width], sem.at[k]
            )
        )
        copies[-1].start()
    for copy in copies:
        copy.wait()


def cut(src, order, dims, width):
    n = len(order)
    return pl.pallas_call(
        functools.partial(cut_kernel, dims, order),
        out_shape=jax.ShapeDtypeStruct((src.shape[0], n * width), src.dtype),
        in_specs=[HBM],
        out_specs=VMEM,
        scratch_shapes=[pltpu.SemaphoreType.DMA((n,))],
        compiler_params=limit(51),
        cost_estimate=pl.CostEstimate(
            flops=0, bytes_accessed=2 * n * width * src.shape[0], transcendentals=0
        ),
    )(src)


def pick_kernel(dims, mine_ref, other_ref, *refs):
    out_ref = refs[-1]
    owner = Place(*dims).owner

    @pl.when(owner)
    def _():
        out_ref[...] = mine_ref[...]

    @pl.when(jnp.logical_not(owner))
    def _():
        out_ref[...] = other_ref[...]


def pick(dims, mine, other, after=()):
    return pl.pallas_call(
        functools.partial(pick_kernel, dims),
        out_shape=jax.ShapeDtypeStruct(mine.shape, mine.dtype),
        in_specs=[VMEM] * 2 + [ANY] * len(after),
        out_specs=VMEM,
        compiler_params=limit(2),
        cost_estimate=pl.CostEstimate(flops=0, bytes_accessed=4 * mine.size, transcendentals=0),
    )(mine, other, *after)


def sort_kernel(mine_ref, other_ref, theirs_ref, keep_ref, give_ref):
    here = lax.axis_index("dim") == lax.axis_index("grp")
    mine, other = mine_ref[...], other_ref[...] + theirs_ref[...]
    keep_ref[...] = jnp.where(here, mine, other)
    give_ref[...] = jnp.where(here, other, mine)


def sort_out(mine, other, theirs):
    return pl.pallas_call(
        sort_kernel,
        out_shape=[jax.ShapeDtypeStruct(mine.shape, mine.dtype)] * 2,
        in_specs=[VMEM] * 3,
        out_specs=[VMEM] * 2,
        compiler_params=limit(2),
    )(mine, other, theirs)


def per_device_quad(nz, nx, ny, queries, inverse_fisher, stored_grads):
    nex, dims = nz * nx, (nz, nx)
    near = nz // 2
    nq = queries.shape[0]

    def move(value, target):
        pairs = []
        for sy in range(ny):
            for sz in range(nz):
                for sx in range(nx):
                    for sd in range(2):
                        to = target(sy, sz, sx, sd)
                        if to is not None:
                            ty, tz, tx, td = to
                            pairs.append(((sy * nex + sz * nx + sx) * 2 + sd, (ty * nex + tz * nx + tx) * 2 + td))
        return lax.ppermute(value, AXES, pairs)

    def along_z(value, hops, flip=False):
        def target(sy, sz, sx, sd):
            su = sz if sd == 0 else nz - 1 - sz
            if su not in hops:
                return None
            tu = hops[su]
            return sy, tu if sd == 0 else nz - 1 - tu, 1 - sx if flip else sx, sd

        return move(value, target)

    def swap_y(value):
        return move(value, lambda sy, sz, sx, sd: (1 - sy, sz, sx, sd))

    def swap_core(value):
        return move(value, lambda sy, sz, sx, sd: (sy, sz, sx, 1 - sd))

    def gather(own, direct, after=()):
        def start(sy, sz, sx, sd):
            su = sz if sd == 0 else nz - 1 - sz
            if su < near:
                return sy, sz + 2 if sd == 0 else sz - 2, sx, sd
            return sy, sz ^ 1, 1 - sx, 1 - sd

        def help_beside(sy, sz, sx, sd):
            su = sz if sd == 0 else nz - 1 - sz
            return sy, sz if su < near else sz ^ 1, sx, 1 - sd

        def help_across(sy, sz, sx, sd):
            su = sz if sd == 0 else nz - 1 - sz
            return sy, sz, sx if su < near else 1 - sx, 1 - sd

        def among_far(flip_z, flip_x):
            def target(sy, sz, sx, sd):
                su = sz if sd == 0 else nz - 1 - sz
                if su < near:
                    return sy, sz, sx, sd
                return sy, sz ^ flip_z, sx ^ flip_x, sd

            return target

        came = move(own, start)
        if direct:
            helped = [move(own, help_beside), move(own, help_across)]
        first = pick(dims, own, came, after)
        if direct:
            beside, across, corner = (move(first, among_far(*f)) for f in ((1, 0), (0, 1), (1, 1)))
            beside, *helped = lax.optimization_barrier((beside, *helped))

            def later(mine, other):
                def take(after):
                    ready, _ = lax.optimization_barrier((mine, after))
                    return pick(dims, ready, other)

                return take

            return first, later(helped[0], beside), later(helped[1], across), later(came, corner)

        pairs = {0: 1, 1: 0, 2: 3, 3: 2}

        def corner(before, after):
            ready, _ = lax.optimization_barrier((first, before))
            return lax.optimization_barrier((along_z(ready, pairs, True), after))[0]

        across = along_z(first, {0: 0, 1: 1, 2: 2, 3: 3}, True)
        return first, along_z(first, pairs), across, corner

    rows, width = nq // ny, queries.shape[1]
    to_y = cut(stored_grads, ORDER[1:], dims, width)
    queries, to_y = lax.optimization_barrier((queries, to_y))
    own = lax.dynamic_slice_in_dim(queries, lax.axis_index("grp") * rows, rows, axis=0)
    own, to_y = lax.optimization_barrier((own, to_y))
    other_grads = swap_y(to_y)
    step = functools.partial(fisher_step, inverse_fisher, dims, width)
    half, quarter = inverse_fisher.shape[0] // 2, inverse_fisher.shape[0] // 4
    a0, a1, b0, b1 = step(((0, 0, half), (0, half, half), (1, 0, half), (1, half, quarter)))
    q0, q1, q2, last = gather(own, False, (a0,))
    total0, b2, c0 = step(((1, half + quarter, quarter), (2, 0, half)), q0, (a0, a1))
    total, c1, d0 = step(((2, half, half), (3, 0, quarter)), q1, (b0, b1, b2), total0)
    total, d1, d2 = step(((3, quarter, quarter), (3, half, half)), q2, (c0, c1), total)
    (total,) = step((), last(total0, total), (d0, d1, d2), total)
    panel = (total + swap_core(total)).astype(jnp.bfloat16)

    p0, second, third, fourth = gather(panel, True)
    swapped = swap_y(p0)
    p1 = second(p0)
    p1, other_grads = lax.optimization_barrier((p1, other_grads))
    p2 = third(p1)
    other = score_dot([p1, p2], (0, 1), None, other_grads)
    p3 = fourth(other)
    other = score_dot([p3], (2,), None, other_grads, other)
    p3, swapped, _ = lax.optimization_barrier((p3, swapped, other))
    mine = score_dot([p0, p1, p2, p3], ORDER, dims, stored_grads)
    theirs = score_dot([swapped], ORDER[:1], dims, stored_grads)

    keep, give = sort_out(mine, swap_y(other), theirs)
    return keep + swap_core(give)


def solution(mesh):
    coords = [getattr(device, "coords", None) for device in mesh.devices.flat]
    nx = 2 if None in coords else len({c[0] for c in coords})
    nz = mesh.shape["ex"] // nx
    ny = mesh.shape["grp"]
    if (nz, nx, ny) == (4, 2, 2):
        body = functools.partial(per_device_quad, nz, nx, ny)
    else:
        body = per_device_any
    return jax.shard_map(
        body,
        mesh=mesh,
        in_specs=(P(None, "ex"), P("ex", "dim"), P(("grp", "ex"), "dim")),
        out_specs=P("dim", ("grp", "ex")),
        check_vma=False,
    )
```

```python
import functools

import jax
import jax.numpy as jnp
from jax import lax
from jax.experimental import pallas as pl
from jax.experimental.pallas import tpu as pltpu
from jax.sharding import PartitionSpec as P

AXES = ("grp", "ex", "dim")
NT = (((1,), (1,)), ((), ()))
VMEM = pl.BlockSpec(memory_space=pltpu.VMEM)
HBM = pl.BlockSpec(memory_space=pltpu.HBM)
ANY = pl.BlockSpec(memory_space=pl.ANY)


def limit(mib):
    return pltpu.CompilerParams(vmem_limit_bytes=mib * 1024 * 1024)


def per_device_any(queries, inverse_fisher, stored_grads):
    term_block = jnp.dot(queries, inverse_fisher, preferred_element_type=jnp.float32)
    own_panel = lax.psum_scatter(term_block, "ex", scatter_dimension=1, tiled=True).astype(
        jnp.bfloat16
    )
    partial_scores = lax.dot_general(
        lax.all_gather(own_panel, "ex", axis=1, tiled=True),
        stored_grads,
        NT,
        preferred_element_type=jnp.float32,
    )
    return lax.psum_scatter(partial_scores, "dim", scatter_dimension=0, tiled=True)


class Place:
    def __init__(self, nz, nx):
        self.y, e, self.d = (lax.axis_index(a) for a in AXES)
        z, x = lax.div(e, nx), lax.rem(e, nx)
        u = jnp.where(self.d == 0, z, nz - 1 - z)
        self.owner = u < nz // 2
        local = jnp.where(self.d == 0, lax.rem(u, 2), nz // 2 - 1 - lax.rem(u, 2))
        self.column = local * nx + x


ORDER = (0, 2, 1, 3)


def block_copies(fisher_ref, block, start, held_ref, sem):
    rows, width = held_ref.shape
    step = 512
    columns = pl.ds(pl.multiple_of(block * width, width), width)
    return [
        pltpu.make_async_copy(
            fisher_ref.at[pl.ds(start + i * step, step), columns],
            held_ref.at[pl.ds(i * step, step), :],
            sem.at[i],
        )
        for i in range(rows // step)
    ]


def times(chunk_ref, fisher):
    return lax.dot_general(chunk_ref[...], fisher, NT, preferred_element_type=jnp.float32)


def fisher_kernel(dims, n_parts, has_base, fetch, *refs):
    if fetch:
        column = Place(*dims).column
        fisher_ref, *refs = refs
    n_in = n_parts + bool(n_parts)
    chunk_ref, parts = (refs[0], refs[1:n_in]) if n_parts else (None, ())
    base_ref = refs[n_in] if has_base else None
    outs, sem = refs[n_in + has_base : -1], refs[-1]
    held = outs[1:] if n_parts else outs
    copies = []
    for k, (piece, start, _) in enumerate(fetch):
        for copy in block_copies(fisher_ref, column ^ ORDER[piece], start, held[k], sem.at[k]):
            copy.start()
            copies.append(copy)

    if parts:
        loops = 2 if fetch else 1

        @pl.loop(0, loops)
        def _(i):
            before = 0
            for part_ref in parts:
                rows = part_ref.shape[0]
                step = rows // loops
                start = pl.multiple_of(i * step, step)
                columns = pl.ds(before + start, step)
                term = times(chunk_ref, part_ref[pl.ds(start, step), :])
                outs[0][:, columns] = term + base_ref[:, columns] if has_base else term
                before += rows

    for copy in copies:
        copy.wait()


def fisher_step(fisher, dims, width, fetch, chunk=None, parts=(), base=None):
    total = fisher.shape[0]
    ins = [] if chunk is None else [chunk, *parts]
    has_base = base is not None
    out_shape = [] if chunk is None else [jax.ShapeDtypeStruct((chunk.shape[0], total), jnp.float32)]
    out_shape += [jax.ShapeDtypeStruct((rows, width), fisher.dtype) for _, _, rows in fetch]
    fetched = sum(rows for _, _, rows in fetch)
    return pl.pallas_call(
        functools.partial(fisher_kernel, dims, len(parts), has_base, fetch),
        out_shape=out_shape,
        in_specs=[HBM] * bool(fetch) + [VMEM] * (len(ins) + has_base),
        out_specs=[VMEM] * len(out_shape),
        scratch_shapes=[pltpu.SemaphoreType.DMA((max(len(fetch), 1), 2))],
        compiler_params=limit(34 if chunk is None else 20),
        cost_estimate=pl.CostEstimate(
            flops=0 if chunk is None else 2 * chunk.shape[0] * width * total,
            bytes_accessed=2 * width * (fetched + total * bool(ins)),
            transcendentals=0,
        ),
    )(*([fisher] if fetch else []), *ins, *([base] if has_base else []))


def score_kernel(dims, order, has_base, *refs):
    n = len(order)
    column = Place(*dims).column if dims else 0
    grads_ref, out_ref = refs[n], refs[-1]
    width = refs[0].shape[1]
    total = refs[n + 1][...] if has_base else None
    for k in range(n):
        block = column ^ order[k]
        start = pl.multiple_of(block * width, width) if dims else block * width
        term = times(refs[k], grads_ref[:, pl.ds(start, width)])
        total = term if total is None else total + term
    out_ref[...] = total


def score_dot(pieces, order, dims, grads, base=None):
    n = len(pieces)
    rows, width = pieces[0].shape
    operands = [*pieces, grads] + ([] if base is None else [base])
    return pl.pallas_call(
        functools.partial(score_kernel, dims, order, base is not None),
        out_shape=jax.ShapeDtypeStruct((rows, grads.shape[0]), jnp.float32),
        in_specs=[VMEM] * len(operands),
        out_specs=VMEM,
        compiler_params=limit(8),
        cost_estimate=pl.CostEstimate(
            flops=2 * n * rows * width * grads.shape[0],
            bytes_accessed=2 * n * width * grads.shape[0],
            transcendentals=0,
        ),
    )(*operands)


def cut_kernel(dims, order, src_ref, out_ref, sem):
    column = Place(*dims).column
    width = out_ref.shape[1] // len(order)
    copies = []
    for k, mask in enumerate(order):
        start = pl.multiple_of((column ^ mask) * width, width)
        copies.append(
            pltpu.make_async_copy(
                src_ref.at[:, pl.ds(start, width)], out_ref.at[:, k * width : (k + 1) * width], sem.at[k]
            )
        )
        copies[-1].start()
    for copy in copies:
        copy.wait()


def cut(src, order, dims, width):
    n = len(order)
    return pl.pallas_call(
        functools.partial(cut_kernel, dims, order),
        out_shape=jax.ShapeDtypeStruct((src.shape[0], n * width), src.dtype),
        in_specs=[HBM],
        out_specs=VMEM,
        scratch_shapes=[pltpu.SemaphoreType.DMA((n,))],
        compiler_params=limit(51),
        cost_estimate=pl.CostEstimate(
            flops=0, bytes_accessed=2 * n * width * src.shape[0], transcendentals=0
        ),
    )(src)


def pick_kernel(dims, mine_ref, other_ref, *refs):
    out_ref = refs[-1]
    owner = Place(*dims).owner

    @pl.when(owner)
    def _():
        out_ref[...] = mine_ref[...]

    @pl.when(jnp.logical_not(owner))
    def _():
        out_ref[...] = other_ref[...]


def pick(dims, mine, other, after=()):
    return pl.pallas_call(
        functools.partial(pick_kernel, dims),
        out_shape=jax.ShapeDtypeStruct(mine.shape, mine.dtype),
        in_specs=[VMEM] * 2 + [ANY] * len(after),
        out_specs=VMEM,
        compiler_params=limit(2),
        cost_estimate=pl.CostEstimate(flops=0, bytes_accessed=4 * mine.size, transcendentals=0),
    )(mine, other, *after)


def sort_kernel(mine_ref, other_ref, theirs_ref, keep_ref, give_ref):
    here = lax.axis_index("dim") == lax.axis_index("grp")
    mine, other = mine_ref[...], other_ref[...] + theirs_ref[...]
    keep_ref[...] = jnp.where(here, mine, other)
    give_ref[...] = jnp.where(here, other, mine)


def sort_out(mine, other, theirs):
    return pl.pallas_call(
        sort_kernel,
        out_shape=[jax.ShapeDtypeStruct(mine.shape, mine.dtype)] * 2,
        in_specs=[VMEM] * 3,
        out_specs=[VMEM] * 2,
        compiler_params=limit(2),
    )(mine, other, theirs)


def per_device_quad(nz, nx, ny, queries, inverse_fisher, stored_grads):
    nex, dims = nz * nx, (nz, nx)
    near = nz // 2
    nq = queries.shape[0]

    def move(value, target):
        pairs = []
        for sy in range(ny):
            for sz in range(nz):
                for sx in range(nx):
                    for sd in range(2):
                        to = target(sy, sz, sx, sd)
                        if to is not None:
                            ty, tz, tx, td = to
                            pairs.append(((sy * nex + sz * nx + sx) * 2 + sd, (ty * nex + tz * nx + tx) * 2 + td))
        return lax.ppermute(value, AXES, pairs)

    def along_z(value, hops, flip=False):
        def target(sy, sz, sx, sd):
            su = sz if sd == 0 else nz - 1 - sz
            if su not in hops:
                return None
            tu = hops[su]
            return sy, tu if sd == 0 else nz - 1 - tu, 1 - sx if flip else sx, sd

        return move(value, target)

    def swap_y(value):
        return move(value, lambda sy, sz, sx, sd: (1 - sy, sz, sx, sd))

    def swap_core(value):
        return move(value, lambda sy, sz, sx, sd: (sy, sz, sx, 1 - sd))

    def gather(own, direct, after=()):
        def start(sy, sz, sx, sd):
            su = sz if sd == 0 else nz - 1 - sz
            if su < near:
                return sy, sz + 2 if sd == 0 else sz - 2, sx, sd
            return sy, sz ^ 1, 1 - sx, 1 - sd

        came = move(own, start)
        if direct:
            corner = along_z(own, {0: 3, 1: 2}, True)
        first = pick(dims, own, came, after)
        pairs = {0: 1, 1: 0, 2: 3, 3: 2}
        beside = along_z(first, pairs)
        across = along_z(first, {0: 0, 1: 1, 2: 2, 3: 3}, True)
        if direct:
            beside, corner = lax.optimization_barrier((beside, corner))

        def last(before, after):
            if direct:
                ready, _ = lax.optimization_barrier((came, after))
                return pick(dims, ready, corner)
            ready, _ = lax.optimization_barrier((first, before))
            piece, _ = lax.optimization_barrier((along_z(ready, pairs, True), after))
            return piece

        return first, beside, across, last

    rows, width = nq // ny, queries.shape[1]
    to_y = cut(stored_grads, ORDER[1:], dims, width)
    queries, to_y = lax.optimization_barrier((queries, to_y))
    own = lax.dynamic_slice_in_dim(queries, lax.axis_index("grp") * rows, rows, axis=0)
    own, to_y = lax.optimization_barrier((own, to_y))
    other_grads = swap_y(to_y)
    step = functools.partial(fisher_step, inverse_fisher, dims, width)
    half, quarter = inverse_fisher.shape[0] // 2, inverse_fisher.shape[0] // 4
    a0, a1, b0, b1 = step(((0, 0, half), (0, half, half), (1, 0, half), (1, half, quarter)))
    q0, q1, q2, last = gather(own, False, (a0,))
    total0, b2, c0 = step(((1, half + quarter, quarter), (2, 0, half)), q0, (a0, a1))
    total, c1, d0 = step(((2, half, half), (3, 0, quarter)), q1, (b0, b1, b2), total0)
    total, d1, d2 = step(((3, quarter, quarter), (3, half, half)), q2, (c0, c1), total)
    (total,) = step((), last(total0, total), (d0, d1, d2), total)
    panel = (total + swap_core(total)).astype(jnp.bfloat16)

    p0, p1, p2, last = gather(panel, True)
    swapped = swap_y(p0)
    p1, other_grads = lax.optimization_barrier((p1, other_grads))
    p3 = last(p1, p1)
    other = score_dot([p1, p3], (0, 2), None, other_grads)
    p2, _ = lax.optimization_barrier((p2, other))
    other = score_dot([p2], (1,), None, other_grads, other)
    p2, swapped, _ = lax.optimization_barrier((p2, swapped, other))
    mine = score_dot([p0, p1, p2, p3], ORDER, dims, stored_grads)
    theirs = score_dot([swapped], ORDER[:1], dims, stored_grads)

    keep, give = sort_out(mine, swap_y(other), theirs)
    return keep + swap_core(give)


def solution(mesh):
    coords = [getattr(device, "coords", None) for device in mesh.devices.flat]
    nx = 2 if None in coords else len({c[0] for c in coords})
    nz = mesh.shape["ex"] // nx
    ny = mesh.shape["grp"]
    if (nz, nx, ny) == (4, 2, 2):
        body = functools.partial(per_device_quad, nz, nx, ny)
    else:
        body = per_device_any
    return jax.shard_map(
        body,
        mesh=mesh,
        in_specs=(P(None, "ex"), P("ex", "dim"), P(("grp", "ex"), "dim")),
        out_specs=P("dim", ("grp", "ex")),
        check_vma=False,
    )
```

```python
import functools

import jax
import jax.numpy as jnp
from jax import lax
from jax.experimental import pallas as pl
from jax.experimental.pallas import tpu as pltpu
from jax.sharding import PartitionSpec as P

AXES = ("grp", "ex", "dim")
NT = (((1,), (1,)), ((), ()))
VMEM = pl.BlockSpec(memory_space=pltpu.VMEM)
HBM = pl.BlockSpec(memory_space=pltpu.HBM)
ANY = pl.BlockSpec(memory_space=pl.ANY)


def limit(mib):
    return pltpu.CompilerParams(vmem_limit_bytes=mib * 1024 * 1024)


def per_device_any(queries, inverse_fisher, stored_grads):
    term_block = jnp.dot(queries, inverse_fisher, preferred_element_type=jnp.float32)
    own_panel = lax.psum_scatter(term_block, "ex", scatter_dimension=1, tiled=True).astype(
        jnp.bfloat16
    )
    partial_scores = lax.dot_general(
        lax.all_gather(own_panel, "ex", axis=1, tiled=True),
        stored_grads,
        NT,
        preferred_element_type=jnp.float32,
    )
    return lax.psum_scatter(partial_scores, "dim", scatter_dimension=0, tiled=True)


class Place:
    def __init__(self, nz, nx):
        self.y, e, self.d = (lax.axis_index(a) for a in AXES)
        z, x = lax.div(e, nx), lax.rem(e, nx)
        u = jnp.where(self.d == 0, z, nz - 1 - z)
        self.owner = u < nz // 2
        local = jnp.where(self.d == 0, lax.rem(u, 2), nz // 2 - 1 - lax.rem(u, 2))
        self.column = local * nx + x


ORDER = (0, 2, 1, 3)


def block_copies(fisher_ref, block, start, held_ref, sem):
    rows, width = held_ref.shape
    step = 512
    columns = pl.ds(pl.multiple_of(block * width, width), width)
    return [
        pltpu.make_async_copy(
            fisher_ref.at[pl.ds(start + i * step, step), columns],
            held_ref.at[pl.ds(i * step, step), :],
            sem.at[i],
        )
        for i in range(rows // step)
    ]


def times(chunk_ref, fisher):
    return lax.dot_general(chunk_ref[...], fisher, NT, preferred_element_type=jnp.float32)


def fisher_kernel(dims, n_parts, has_base, fetch, *refs):
    if fetch:
        column = Place(*dims).column
        fisher_ref, *refs = refs
    n_in = n_parts + bool(n_parts)
    chunk_ref, parts = (refs[0], refs[1:n_in]) if n_parts else (None, ())
    base_ref = refs[n_in] if has_base else None
    outs, sem = refs[n_in + has_base : -1], refs[-1]
    held = outs[1:] if n_parts else outs
    copies = []
    for k, (piece, start, _) in enumerate(fetch):
        for copy in block_copies(fisher_ref, column ^ ORDER[piece], start, held[k], sem.at[k]):
            copy.start()
            copies.append(copy)

    if parts:
        loops = 2 if fetch else 1

        @pl.loop(0, loops)
        def _(i):
            before = 0
            for part_ref in parts:
                rows = part_ref.shape[0]
                step = rows // loops
                start = pl.multiple_of(i * step, step)
                columns = pl.ds(before + start, step)
                term = times(chunk_ref, part_ref[pl.ds(start, step), :])
                outs[0][:, columns] = term + base_ref[:, columns] if has_base else term
                before += rows

    for copy in copies:
        copy.wait()


def fisher_step(fisher, dims, width, fetch, chunk=None, parts=(), base=None):
    total = fisher.shape[0]
    ins = [] if chunk is None else [chunk, *parts]
    has_base = base is not None
    out_shape = [] if chunk is None else [jax.ShapeDtypeStruct((chunk.shape[0], total), jnp.float32)]
    out_shape += [jax.ShapeDtypeStruct((rows, width), fisher.dtype) for _, _, rows in fetch]
    fetched = sum(rows for _, _, rows in fetch)
    return pl.pallas_call(
        functools.partial(fisher_kernel, dims, len(parts), has_base, fetch),
        out_shape=out_shape,
        in_specs=[HBM] * bool(fetch) + [VMEM] * (len(ins) + has_base),
        out_specs=[VMEM] * len(out_shape),
        scratch_shapes=[pltpu.SemaphoreType.DMA((max(len(fetch), 1), 2))],
        compiler_params=limit(34 if chunk is None else 20),
        cost_estimate=pl.CostEstimate(
            flops=0 if chunk is None else 2 * chunk.shape[0] * width * total,
            bytes_accessed=2 * width * (fetched + total * bool(ins)),
            transcendentals=0,
        ),
    )(*([fisher] if fetch else []), *ins, *([base] if has_base else []))


def score_kernel(dims, order, has_base, *refs):
    n = len(order)
    column = Place(*dims).column if dims else 0
    grads_ref, out_ref = refs[n], refs[-1]
    width = refs[0].shape[1]
    total = refs[n + 1][...] if has_base else None
    for k in range(n):
        block = column ^ order[k]
        start = pl.multiple_of(block * width, width) if dims else block * width
        term = times(refs[k], grads_ref[:, pl.ds(start, width)])
        total = term if total is None else total + term
    out_ref[...] = total


def score_dot(pieces, order, dims, grads, base=None):
    n = len(pieces)
    rows, width = pieces[0].shape
    operands = [*pieces, grads] + ([] if base is None else [base])
    return pl.pallas_call(
        functools.partial(score_kernel, dims, order, base is not None),
        out_shape=jax.ShapeDtypeStruct((rows, grads.shape[0]), jnp.float32),
        in_specs=[VMEM] * len(operands),
        out_specs=VMEM,
        compiler_params=limit(8),
        cost_estimate=pl.CostEstimate(
            flops=2 * n * rows * width * grads.shape[0],
            bytes_accessed=2 * n * width * grads.shape[0],
            transcendentals=0,
        ),
    )(*operands)


def cut_kernel(dims, order, src_ref, out_ref, sem):
    column = Place(*dims).column
    width = out_ref.shape[1] // len(order)
    copies = []
    for k, mask in enumerate(order):
        start = pl.multiple_of((column ^ mask) * width, width)
        copies.append(
            pltpu.make_async_copy(
                src_ref.at[:, pl.ds(start, width)], out_ref.at[:, k * width : (k + 1) * width], sem.at[k]
            )
        )
        copies[-1].start()
    for copy in copies:
        copy.wait()


def cut(src, order, dims, width):
    n = len(order)
    return pl.pallas_call(
        functools.partial(cut_kernel, dims, order),
        out_shape=jax.ShapeDtypeStruct((src.shape[0], n * width), src.dtype),
        in_specs=[HBM],
        out_specs=VMEM,
        scratch_shapes=[pltpu.SemaphoreType.DMA((n,))],
        compiler_params=limit(51),
        cost_estimate=pl.CostEstimate(
            flops=0, bytes_accessed=2 * n * width * src.shape[0], transcendentals=0
        ),
    )(src)


def pick_kernel(dims, mine_ref, other_ref, *refs):
    out_ref = refs[-1]
    owner = Place(*dims).owner

    @pl.when(owner)
    def _():
        out_ref[...] = mine_ref[...]

    @pl.when(jnp.logical_not(owner))
    def _():
        out_ref[...] = other_ref[...]


def pick(dims, mine, other, after=()):
    return pl.pallas_call(
        functools.partial(pick_kernel, dims),
        out_shape=jax.ShapeDtypeStruct(mine.shape, mine.dtype),
        in_specs=[VMEM] * 2 + [ANY] * len(after),
        out_specs=VMEM,
        compiler_params=limit(2),
        cost_estimate=pl.CostEstimate(flops=0, bytes_accessed=4 * mine.size, transcendentals=0),
    )(mine, other, *after)


def sort_kernel(mine_ref, other_ref, theirs_ref, keep_ref, give_ref):
    here = lax.axis_index("dim") == lax.axis_index("grp")
    mine, other = mine_ref[...], other_ref[...] + theirs_ref[...]
    keep_ref[...] = jnp.where(here, mine, other)
    give_ref[...] = jnp.where(here, other, mine)


def sort_out(mine, other, theirs):
    return pl.pallas_call(
        sort_kernel,
        out_shape=[jax.ShapeDtypeStruct(mine.shape, mine.dtype)] * 2,
        in_specs=[VMEM] * 3,
        out_specs=[VMEM] * 2,
        compiler_params=limit(2),
    )(mine, other, theirs)


def per_device_quad(nz, nx, ny, queries, inverse_fisher, stored_grads):
    nex, dims = nz * nx, (nz, nx)
    near = nz // 2
    nq = queries.shape[0]

    def move(value, target):
        pairs = []
        for sy in range(ny):
            for sz in range(nz):
                for sx in range(nx):
                    for sd in range(2):
                        to = target(sy, sz, sx, sd)
                        if to is not None:
                            ty, tz, tx, td = to
                            pairs.append(((sy * nex + sz * nx + sx) * 2 + sd, (ty * nex + tz * nx + tx) * 2 + td))
        return lax.ppermute(value, AXES, pairs)

    def along_z(value, hops, flip=False):
        def target(sy, sz, sx, sd):
            su = sz if sd == 0 else nz - 1 - sz
            if su not in hops:
                return None
            tu = hops[su]
            return sy, tu if sd == 0 else nz - 1 - tu, 1 - sx if flip else sx, sd

        return move(value, target)

    def swap_y(value):
        return move(value, lambda sy, sz, sx, sd: (1 - sy, sz, sx, sd))

    def swap_core(value):
        return move(value, lambda sy, sz, sx, sd: (sy, sz, sx, 1 - sd))

    def gather(own, direct, after=()):
        def start(sy, sz, sx, sd):
            su = sz if sd == 0 else nz - 1 - sz
            if su < near:
                return sy, sz + 2 if sd == 0 else sz - 2, sx, sd
            return sy, sz ^ 1, 1 - sx, 1 - sd

        came = move(own, start)
        if direct:
            corner = along_z(own, {0: 3, 1: 2}, True)
        first = pick(dims, own, came, after)
        pairs = {0: 1, 1: 0, 2: 3, 3: 2}
        beside = along_z(first, pairs)
        across = along_z(first, {0: 0, 1: 1, 2: 2, 3: 3}, True)
        if direct:
            across, corner = lax.optimization_barrier((across, corner))

        def last(before, after):
            if direct:
                ready, _ = lax.optimization_barrier((came, after))
                return pick(dims, ready, corner)
            ready, _ = lax.optimization_barrier((first, before))
            piece, _ = lax.optimization_barrier((along_z(ready, pairs, True), after))
            return piece

        return first, beside, across, last

    rows, width = nq // ny, queries.shape[1]
    to_y = cut(stored_grads, ORDER[1:], dims, width)
    queries, to_y = lax.optimization_barrier((queries, to_y))
    own = lax.dynamic_slice_in_dim(queries, lax.axis_index("grp") * rows, rows, axis=0)
    own, to_y = lax.optimization_barrier((own, to_y))
    other_grads = swap_y(to_y)
    step = functools.partial(fisher_step, inverse_fisher, dims, width)
    half, quarter = inverse_fisher.shape[0] // 2, inverse_fisher.shape[0] // 4
    a0, a1, b0, b1 = step(((0, 0, half), (0, half, half), (1, 0, half), (1, half, quarter)))
    q0, q1, q2, last = gather(own, False, (a0,))
    total0, b2, c0 = step(((1, half + quarter, quarter), (2, 0, half)), q0, (a0, a1))
    total, c1, d0 = step(((2, half, half), (3, 0, quarter)), q1, (b0, b1, b2), total0)
    total, d1, d2 = step(((3, quarter, quarter), (3, half, half)), q2, (c0, c1), total)
    (total,) = step((), last(total0, total), (d0, d1, d2), total)
    panel = (total + swap_core(total)).astype(jnp.bfloat16)

    p0, p1, p2, last = gather(panel, True)
    swapped = swap_y(p0)
    p2, other_grads = lax.optimization_barrier((p2, other_grads))
    p3 = last(p2, p2)
    other = score_dot([p2, p3], (1, 2), None, other_grads)
    p1, _ = lax.optimization_barrier((p1, other))
    other = score_dot([p1], (0,), None, other_grads, other)
    p1, swapped, _ = lax.optimization_barrier((p1, swapped, other))
    mine = score_dot([p0, p1, p2, p3], ORDER, dims, stored_grads)
    theirs = score_dot([swapped], ORDER[:1], dims, stored_grads)

    keep, give = sort_out(mine, swap_y(other), theirs)
    return keep + swap_core(give)


def solution(mesh):
    coords = [getattr(device, "coords", None) for device in mesh.devices.flat]
    nx = 2 if None in coords else len({c[0] for c in coords})
    nz = mesh.shape["ex"] // nx
    ny = mesh.shape["grp"]
    if (nz, nx, ny) == (4, 2, 2):
        body = functools.partial(per_device_quad, nz, nx, ny)
    else:
        body = per_device_any
    return jax.shard_map(
        body,
        mesh=mesh,
        in_specs=(P(None, "ex"), P("ex", "dim"), P(("grp", "ex"), "dim")),
        out_specs=P("dim", ("grp", "ex")),
        check_vma=False,
    )
```

```python
import functools

import jax
import jax.numpy as jnp
from jax import lax
from jax.experimental import pallas as pl
from jax.experimental.pallas import tpu as pltpu
from jax.sharding import PartitionSpec as P

AXES = ("grp", "ex", "dim")
NT = (((1,), (1,)), ((), ()))
VMEM = pl.BlockSpec(memory_space=pltpu.VMEM)
HBM = pl.BlockSpec(memory_space=pltpu.HBM)
ANY = pl.BlockSpec(memory_space=pl.ANY)


def limit(mib):
    return pltpu.CompilerParams(vmem_limit_bytes=mib * 1024 * 1024)


def per_device_any(queries, inverse_fisher, stored_grads):
    term_block = jnp.dot(queries, inverse_fisher, preferred_element_type=jnp.float32)
    own_panel = lax.psum_scatter(term_block, "ex", scatter_dimension=1, tiled=True).astype(
        jnp.bfloat16
    )
    partial_scores = lax.dot_general(
        lax.all_gather(own_panel, "ex", axis=1, tiled=True),
        stored_grads,
        NT,
        preferred_element_type=jnp.float32,
    )
    return lax.psum_scatter(partial_scores, "dim", scatter_dimension=0, tiled=True)


class Place:
    def __init__(self, nz, nx):
        self.y, e, self.d = (lax.axis_index(a) for a in AXES)
        z, x = lax.div(e, nx), lax.rem(e, nx)
        u = jnp.where(self.d == 0, z, nz - 1 - z)
        self.owner = u < nz // 2
        local = jnp.where(self.d == 0, lax.rem(u, 2), nz // 2 - 1 - lax.rem(u, 2))
        self.column = local * nx + x


ORDER = (0, 2, 1, 3)


def block_copies(fisher_ref, block, start, held_ref, sem):
    rows, width = held_ref.shape
    step = 512
    columns = pl.ds(pl.multiple_of(block * width, width), width)
    return [
        pltpu.make_async_copy(
            fisher_ref.at[pl.ds(start + i * step, step), columns],
            held_ref.at[pl.ds(i * step, step), :],
            sem.at[i],
        )
        for i in range(rows // step)
    ]


def times(chunk_ref, fisher):
    return lax.dot_general(chunk_ref[...], fisher, NT, preferred_element_type=jnp.float32)


def fisher_kernel(dims, n_parts, has_base, fetch, first, *refs):
    if fetch:
        column = Place(*dims).column
        fisher_ref, *refs = refs
    n_in = n_parts + bool(n_parts)
    chunk_ref, parts = (refs[0], refs[1:n_in]) if n_parts else (None, ())
    base_ref = refs[n_in] if has_base else None
    outs, sem = refs[n_in + has_base : -1], refs[-1]
    held = outs[1:] if n_parts else outs
    copies = []
    for k, (piece, start, _) in enumerate(fetch):
        for copy in block_copies(fisher_ref, column ^ ORDER[piece], start, held[k], sem.at[k]):
            copy.start()
            copies.append(copy)

    if parts:
        loops = 2 if fetch else 1

        @pl.loop(0, loops)
        def _(i):
            before = 0
            for part_ref in parts:
                rows = part_ref.shape[0]
                step = rows // loops
                start = pl.multiple_of(i * step, step)
                term = times(chunk_ref, part_ref[pl.ds(start, step), :])
                if has_base:
                    term = term + base_ref[:, pl.ds(first + before + start, step)]
                outs[0][:, pl.ds(before + start, step)] = term
                before += rows

    for copy in copies:
        copy.wait()


def fisher_step(fisher, dims, width, fetch, chunk=None, parts=(), base=None, first=0):
    total = sum(part.shape[0] for part in parts)
    ins = [] if chunk is None else [chunk, *parts]
    has_base = base is not None
    out_shape = [] if chunk is None else [jax.ShapeDtypeStruct((chunk.shape[0], total), jnp.float32)]
    out_shape += [jax.ShapeDtypeStruct((rows, width), fisher.dtype) for _, _, rows in fetch]
    fetched = sum(rows for _, _, rows in fetch)
    return pl.pallas_call(
        functools.partial(fisher_kernel, dims, len(parts), has_base, fetch, first),
        out_shape=out_shape,
        in_specs=[HBM] * bool(fetch) + [VMEM] * (len(ins) + has_base),
        out_specs=[VMEM] * len(out_shape),
        scratch_shapes=[pltpu.SemaphoreType.DMA((max(len(fetch), 1), 2))],
        compiler_params=limit(34 if chunk is None else 20),
        cost_estimate=pl.CostEstimate(
            flops=0 if chunk is None else 2 * chunk.shape[0] * width * total,
            bytes_accessed=2 * width * (fetched + total * bool(ins)),
            transcendentals=0,
        ),
    )(*([fisher] if fetch else []), *ins, *([base] if has_base else []))


def score_kernel(dims, order, has_base, *refs):
    n = len(order)
    column = Place(*dims).column if dims else 0
    grads_ref, out_ref = refs[n], refs[-1]
    width = refs[0].shape[1]
    total = refs[n + 1][...] if has_base else None
    for k in range(n):
        block = column ^ order[k]
        start = pl.multiple_of(block * width, width) if dims else block * width
        term = times(refs[k], grads_ref[:, pl.ds(start, width)])
        total = term if total is None else total + term
    out_ref[...] = total


def score_dot(pieces, order, dims, grads, base=None):
    n = len(pieces)
    rows, width = pieces[0].shape
    operands = [*pieces, grads] + ([] if base is None else [base])
    return pl.pallas_call(
        functools.partial(score_kernel, dims, order, base is not None),
        out_shape=jax.ShapeDtypeStruct((rows, grads.shape[0]), jnp.float32),
        in_specs=[VMEM] * len(operands),
        out_specs=VMEM,
        compiler_params=limit(8),
        cost_estimate=pl.CostEstimate(
            flops=2 * n * rows * width * grads.shape[0],
            bytes_accessed=2 * n * width * grads.shape[0],
            transcendentals=0,
        ),
    )(*operands)


def cut_kernel(dims, order, src_ref, out_ref, sem):
    column = Place(*dims).column
    width = out_ref.shape[1] // len(order)
    copies = []
    for k, mask in enumerate(order):
        start = pl.multiple_of((column ^ mask) * width, width)
        copies.append(
            pltpu.make_async_copy(
                src_ref.at[:, pl.ds(start, width)], out_ref.at[:, k * width : (k + 1) * width], sem.at[k]
            )
        )
        copies[-1].start()
    for copy in copies:
        copy.wait()


def cut(src, order, dims, width):
    n = len(order)
    return pl.pallas_call(
        functools.partial(cut_kernel, dims, order),
        out_shape=jax.ShapeDtypeStruct((src.shape[0], n * width), src.dtype),
        in_specs=[HBM],
        out_specs=VMEM,
        scratch_shapes=[pltpu.SemaphoreType.DMA((n,))],
        compiler_params=limit(51),
        cost_estimate=pl.CostEstimate(
            flops=0, bytes_accessed=2 * n * width * src.shape[0], transcendentals=0
        ),
    )(src)


def pick_kernel(dims, mine_ref, other_ref, *refs):
    out_ref = refs[-1]
    owner = Place(*dims).owner

    @pl.when(owner)
    def _():
        out_ref[...] = mine_ref[...]

    @pl.when(jnp.logical_not(owner))
    def _():
        out_ref[...] = other_ref[...]


def pick(dims, mine, other, after=()):
    return pl.pallas_call(
        functools.partial(pick_kernel, dims),
        out_shape=jax.ShapeDtypeStruct(mine.shape, mine.dtype),
        in_specs=[VMEM] * 2 + [ANY] * len(after),
        out_specs=VMEM,
        compiler_params=limit(2),
        cost_estimate=pl.CostEstimate(flops=0, bytes_accessed=4 * mine.size, transcendentals=0),
    )(mine, other, *after)


def sort_kernel(mine_ref, other_ref, theirs_ref, keep_ref, give_ref):
    here = lax.axis_index("dim") == lax.axis_index("grp")
    mine, other = mine_ref[...], other_ref[...] + theirs_ref[...]
    keep_ref[...] = jnp.where(here, mine, other)
    give_ref[...] = jnp.where(here, other, mine)


def sort_out(mine, other, theirs):
    return pl.pallas_call(
        sort_kernel,
        out_shape=[jax.ShapeDtypeStruct(mine.shape, mine.dtype)] * 2,
        in_specs=[VMEM] * 3,
        out_specs=[VMEM] * 2,
        compiler_params=limit(2),
    )(mine, other, theirs)


def join_kernel(low_ref, high_ref, other_high_ref, out_ref):
    width = low_ref.shape[1]
    out_ref[:, :width] = low_ref[...].astype(out_ref.dtype)
    out_ref[:, width:] = (high_ref[...] + other_high_ref[...]).astype(out_ref.dtype)


def join(low, high, other_high):
    return pl.pallas_call(
        join_kernel,
        out_shape=jax.ShapeDtypeStruct((low.shape[0], 2 * low.shape[1]), jnp.bfloat16),
        in_specs=[VMEM] * 3,
        out_specs=VMEM,
        compiler_params=limit(2),
    )(low, high, other_high)


def per_device_quad(nz, nx, ny, queries, inverse_fisher, stored_grads):
    nex, dims = nz * nx, (nz, nx)
    near = nz // 2
    nq = queries.shape[0]

    def move(value, target):
        pairs = []
        for sy in range(ny):
            for sz in range(nz):
                for sx in range(nx):
                    for sd in range(2):
                        to = target(sy, sz, sx, sd)
                        if to is not None:
                            ty, tz, tx, td = to
                            pairs.append(((sy * nex + sz * nx + sx) * 2 + sd, (ty * nex + tz * nx + tx) * 2 + td))
        return lax.ppermute(value, AXES, pairs)

    def along_z(value, hops, flip=False):
        def target(sy, sz, sx, sd):
            su = sz if sd == 0 else nz - 1 - sz
            if su not in hops:
                return None
            tu = hops[su]
            return sy, tu if sd == 0 else nz - 1 - tu, 1 - sx if flip else sx, sd

        return move(value, target)

    def swap_y(value):
        return move(value, lambda sy, sz, sx, sd: (1 - sy, sz, sx, sd))

    def swap_core(value):
        return move(value, lambda sy, sz, sx, sd: (sy, sz, sx, 1 - sd))

    def gather(own, direct, after=()):
        def start(sy, sz, sx, sd):
            su = sz if sd == 0 else nz - 1 - sz
            if su < near:
                return sy, sz + 2 if sd == 0 else sz - 2, sx, sd
            return sy, sz ^ 1, 1 - sx, 1 - sd

        came = move(own, start)
        if direct:
            corner = along_z(own, {0: 3, 1: 2}, True)
        first = pick(dims, own, came, after)
        pairs = {0: 1, 1: 0, 2: 3, 3: 2}
        beside = along_z(first, pairs)
        across = along_z(first, {0: 0, 1: 1, 2: 2, 3: 3}, True)
        if direct:
            beside, corner = lax.optimization_barrier((beside, corner))

        def last(before, after):
            if direct:
                ready, _ = lax.optimization_barrier((came, after))
                return pick(dims, ready, corner)
            ready, _ = lax.optimization_barrier((first, before))
            piece, _ = lax.optimization_barrier((along_z(ready, pairs, True), after))
            return piece

        return first, beside, across, last

    rows, width = nq // ny, queries.shape[1]
    to_y = cut(stored_grads, ORDER[1:], dims, width)
    queries, to_y = lax.optimization_barrier((queries, to_y))
    own = lax.dynamic_slice_in_dim(queries, lax.axis_index("grp") * rows, rows, axis=0)
    own, to_y = lax.optimization_barrier((own, to_y))
    other_grads = swap_y(to_y)
    step = functools.partial(fisher_step, inverse_fisher, dims, width)
    half, quarter = inverse_fisher.shape[0] // 2, inverse_fisher.shape[0] // 4
    a0, a1, b0, b1 = step(((0, 0, half), (0, half, half), (1, 0, half), (1, half, quarter)))
    q0, q1, q2, last = gather(own, False, (a0,))
    total0, b2, c0 = step(((1, half + quarter, quarter), (2, 0, half)), q0, (a0, a1))
    total, c1, d0 = step(((2, half, half), (3, 0, quarter)), q1, (b0, b1, b2), total0)
    total, d1, d2 = step(((3, quarter, quarter), (3, half, half)), q2, (c0, c1), total)
    q3 = last(total0, total)
    (low,) = step((), q3, (d0, d1), total)
    other_low = swap_core(low)
    after_low, _ = lax.optimization_barrier((total, low))
    (high,) = step((), q3, (d2,), after_low, half)
    low, high = lax.optimization_barrier((low + other_low, high))
    panel = join(low, high, swap_core(high))

    p0, p1, p2, last = gather(panel, True)
    swapped = swap_y(p0)
    p1, other_grads = lax.optimization_barrier((p1, other_grads))
    p3 = last(p1, p1)
    other = score_dot([p1, p3], (0, 2), None, other_grads)
    p2, _ = lax.optimization_barrier((p2, other))
    other = score_dot([p2], (1,), None, other_grads, other)
    p2, swapped, _ = lax.optimization_barrier((p2, swapped, other))
    mine = score_dot([p0, p1, p2, p3], ORDER, dims, stored_grads)
    theirs = score_dot([swapped], ORDER[:1], dims, stored_grads)

    keep, give = sort_out(mine, swap_y(other), theirs)
    return keep + swap_core(give)


def solution(mesh):
    coords = [getattr(device, "coords", None) for device in mesh.devices.flat]
    nx = 2 if None in coords else len({c[0] for c in coords})
    nz = mesh.shape["ex"] // nx
    ny = mesh.shape["grp"]
    if (nz, nx, ny) == (4, 2, 2):
        body = functools.partial(per_device_quad, nz, nx, ny)
    else:
        body = per_device_any
    return jax.shard_map(
        body,
        mesh=mesh,
        in_specs=(P(None, "ex"), P("ex", "dim"), P(("grp", "ex"), "dim")),
        out_specs=P("dim", ("grp", "ex")),
        check_vma=False,
    )
```

```python
import functools

import jax
import jax.numpy as jnp
from jax import lax
from jax.experimental import pallas as pl
from jax.experimental.pallas import tpu as pltpu
from jax.sharding import PartitionSpec as P

AXES = ("grp", "ex", "dim")
NT = (((1,), (1,)), ((), ()))
VMEM = pl.BlockSpec(memory_space=pltpu.VMEM)
HBM = pl.BlockSpec(memory_space=pltpu.HBM)
ANY = pl.BlockSpec(memory_space=pl.ANY)


def limit(mib):
    return pltpu.CompilerParams(vmem_limit_bytes=mib * 1024 * 1024)


def per_device_any(queries, inverse_fisher, stored_grads):
    term_block = jnp.dot(queries, inverse_fisher, preferred_element_type=jnp.float32)
    own_panel = lax.psum_scatter(term_block, "ex", scatter_dimension=1, tiled=True).astype(
        jnp.bfloat16
    )
    partial_scores = lax.dot_general(
        lax.all_gather(own_panel, "ex", axis=1, tiled=True),
        stored_grads,
        NT,
        preferred_element_type=jnp.float32,
    )
    return lax.psum_scatter(partial_scores, "dim", scatter_dimension=0, tiled=True)


class Place:
    def __init__(self, nz, nx):
        self.y, e, self.d = (lax.axis_index(a) for a in AXES)
        z, x = lax.div(e, nx), lax.rem(e, nx)
        u = jnp.where(self.d == 0, z, nz - 1 - z)
        self.owner = u < nz // 2
        local = jnp.where(self.d == 0, lax.rem(u, 2), nz // 2 - 1 - lax.rem(u, 2))
        self.column = local * nx + x


ORDER = (0, 2, 1, 3)


def block_copies(fisher_ref, block, start, held_ref, sem):
    rows, width = held_ref.shape
    step = 256
    columns = pl.ds(pl.multiple_of(block * width, width), width)
    return [
        pltpu.make_async_copy(
            fisher_ref.at[pl.ds(start + i * step, step), columns],
            held_ref.at[pl.ds(i * step, step), :],
            sem.at[i],
        )
        for i in range(rows // step)
    ]


def times(chunk_ref, fisher):
    return lax.dot_general(chunk_ref[...], fisher, NT, preferred_element_type=jnp.float32)


def fisher_kernel(dims, n_parts, has_base, fetch, *refs):
    if fetch:
        column = Place(*dims).column
        fisher_ref, *refs = refs
    n_in = n_parts + bool(n_parts)
    chunk_ref, parts = (refs[0], refs[1:n_in]) if n_parts else (None, ())
    base_ref = refs[n_in] if has_base else None
    outs, sem = refs[n_in + has_base : -1], refs[-1]
    held = outs[1:] if n_parts else outs
    copies = []
    for k, (piece, start, _) in enumerate(fetch):
        for copy in block_copies(fisher_ref, column ^ ORDER[piece], start, held[k], sem.at[k]):
            copy.start()
            copies.append(copy)

    if parts:
        loops = 2 if fetch else 1

        @pl.loop(0, loops)
        def _(i):
            before = 0
            for part_ref in parts:
                rows = part_ref.shape[0]
                step = rows // loops
                start = pl.multiple_of(i * step, step)
                columns = pl.ds(before + start, step)
                term = times(chunk_ref, part_ref[pl.ds(start, step), :])
                outs[0][:, columns] = term + base_ref[:, columns] if has_base else term
                before += rows

    for copy in copies:
        copy.wait()


def fisher_step(fisher, dims, width, fetch, chunk=None, parts=(), base=None):
    total = fisher.shape[0]
    ins = [] if chunk is None else [chunk, *parts]
    has_base = base is not None
    out_shape = [] if chunk is None else [jax.ShapeDtypeStruct((chunk.shape[0], total), jnp.float32)]
    out_shape += [jax.ShapeDtypeStruct((rows, width), fisher.dtype) for _, _, rows in fetch]
    fetched = sum(rows for _, _, rows in fetch)
    return pl.pallas_call(
        functools.partial(fisher_kernel, dims, len(parts), has_base, fetch),
        out_shape=out_shape,
        in_specs=[HBM] * bool(fetch) + [VMEM] * (len(ins) + has_base),
        out_specs=[VMEM] * len(out_shape),
        scratch_shapes=[pltpu.SemaphoreType.DMA((max(len(fetch), 1), 4))],
        compiler_params=limit(34 if chunk is None else 20),
        cost_estimate=pl.CostEstimate(
            flops=0 if chunk is None else 2 * chunk.shape[0] * width * total,
            bytes_accessed=2 * width * (fetched + total * bool(ins)),
            transcendentals=0,
        ),
    )(*([fisher] if fetch else []), *ins, *([base] if has_base else []))


def score_kernel(dims, order, has_base, *refs):
    n = len(order)
    column = Place(*dims).column if dims else 0
    grads_ref, out_ref = refs[n], refs[-1]
    width = refs[0].shape[1]
    total = refs[n + 1][...] if has_base else None
    for k in range(n):
        block = column ^ order[k]
        start = pl.multiple_of(block * width, width) if dims else block * width
        term = times(refs[k], grads_ref[:, pl.ds(start, width)])
        total = term if total is None else total + term
    out_ref[...] = total


def score_dot(pieces, order, dims, grads, base=None):
    n = len(pieces)
    rows, width = pieces[0].shape
    operands = [*pieces, grads] + ([] if base is None else [base])
    return pl.pallas_call(
        functools.partial(score_kernel, dims, order, base is not None),
        out_shape=jax.ShapeDtypeStruct((rows, grads.shape[0]), jnp.float32),
        in_specs=[VMEM] * len(operands),
        out_specs=VMEM,
        compiler_params=limit(8),
        cost_estimate=pl.CostEstimate(
            flops=2 * n * rows * width * grads.shape[0],
            bytes_accessed=2 * n * width * grads.shape[0],
            transcendentals=0,
        ),
    )(*operands)


def cut_kernel(dims, order, src_ref, out_ref, sem):
    column = Place(*dims).column
    width = out_ref.shape[1] // len(order)
    copies = []
    for k, mask in enumerate(order):
        start = pl.multiple_of((column ^ mask) * width, width)
        copies.append(
            pltpu.make_async_copy(
                src_ref.at[:, pl.ds(start, width)], out_ref.at[:, k * width : (k + 1) * width], sem.at[k]
            )
        )
        copies[-1].start()
    for copy in copies:
        copy.wait()


def cut(src, order, dims, width):
    n = len(order)
    return pl.pallas_call(
        functools.partial(cut_kernel, dims, order),
        out_shape=jax.ShapeDtypeStruct((src.shape[0], n * width), src.dtype),
        in_specs=[HBM],
        out_specs=VMEM,
        scratch_shapes=[pltpu.SemaphoreType.DMA((n,))],
        compiler_params=limit(51),
        cost_estimate=pl.CostEstimate(
            flops=0, bytes_accessed=2 * n * width * src.shape[0], transcendentals=0
        ),
    )(src)


def pick_kernel(dims, mine_ref, other_ref, *refs):
    out_ref = refs[-1]
    owner = Place(*dims).owner

    @pl.when(owner)
    def _():
        out_ref[...] = mine_ref[...]

    @pl.when(jnp.logical_not(owner))
    def _():
        out_ref[...] = other_ref[...]


def pick(dims, mine, other, after=()):
    return pl.pallas_call(
        functools.partial(pick_kernel, dims),
        out_shape=jax.ShapeDtypeStruct(mine.shape, mine.dtype),
        in_specs=[VMEM] * 2 + [ANY] * len(after),
        out_specs=VMEM,
        compiler_params=limit(2),
        cost_estimate=pl.CostEstimate(flops=0, bytes_accessed=4 * mine.size, transcendentals=0),
    )(mine, other, *after)


def sort_kernel(mine_ref, other_ref, theirs_ref, keep_ref, give_ref):
    here = lax.axis_index("dim") == lax.axis_index("grp")
    mine, other = mine_ref[...], other_ref[...] + theirs_ref[...]
    keep_ref[...] = jnp.where(here, mine, other)
    give_ref[...] = jnp.where(here, other, mine)


def sort_out(mine, other, theirs):
    return pl.pallas_call(
        sort_kernel,
        out_shape=[jax.ShapeDtypeStruct(mine.shape, mine.dtype)] * 2,
        in_specs=[VMEM] * 3,
        out_specs=[VMEM] * 2,
        compiler_params=limit(2),
    )(mine, other, theirs)


def per_device_quad(nz, nx, ny, queries, inverse_fisher, stored_grads):
    nex, dims = nz * nx, (nz, nx)
    near = nz // 2
    nq = queries.shape[0]

    def move(value, target):
        pairs = []
        for sy in range(ny):
            for sz in range(nz):
                for sx in range(nx):
                    for sd in range(2):
                        to = target(sy, sz, sx, sd)
                        if to is not None:
                            ty, tz, tx, td = to
                            pairs.append(((sy * nex + sz * nx + sx) * 2 + sd, (ty * nex + tz * nx + tx) * 2 + td))
        return lax.ppermute(value, AXES, pairs)

    def along_z(value, hops, flip=False):
        def target(sy, sz, sx, sd):
            su = sz if sd == 0 else nz - 1 - sz
            if su not in hops:
                return None
            tu = hops[su]
            return sy, tu if sd == 0 else nz - 1 - tu, 1 - sx if flip else sx, sd

        return move(value, target)

    def swap_y(value):
        return move(value, lambda sy, sz, sx, sd: (1 - sy, sz, sx, sd))

    def swap_core(value):
        return move(value, lambda sy, sz, sx, sd: (sy, sz, sx, 1 - sd))

    def gather(own, direct, after=()):
        def start(sy, sz, sx, sd):
            su = sz if sd == 0 else nz - 1 - sz
            if su < near:
                return sy, sz + 2 if sd == 0 else sz - 2, sx, sd
            return sy, sz ^ 1, 1 - sx, 1 - sd

        came = move(own, start)
        if direct:
            corner = along_z(own, {0: 3, 1: 2}, True)
        first = pick(dims, own, came, after)
        pairs = {0: 1, 1: 0, 2: 3, 3: 2}
        beside = along_z(first, pairs)
        across = along_z(first, {0: 0, 1: 1, 2: 2, 3: 3}, True)
        if direct:
            beside, corner = lax.optimization_barrier((beside, corner))

        def last(before, after):
            if direct:
                ready, _ = lax.optimization_barrier((came, after))
                return pick(dims, ready, corner)
            ready, _ = lax.optimization_barrier((first, before))
            piece, _ = lax.optimization_barrier((along_z(ready, pairs, True), after))
            return piece

        return first, beside, across, last

    rows, width = nq // ny, queries.shape[1]
    to_y = cut(stored_grads, ORDER[1:], dims, width)
    queries, to_y = lax.optimization_barrier((queries, to_y))
    own = lax.dynamic_slice_in_dim(queries, lax.axis_index("grp") * rows, rows, axis=0)
    own, to_y = lax.optimization_barrier((own, to_y))
    other_grads = swap_y(to_y)
    step = functools.partial(fisher_step, inverse_fisher, dims, width)
    half, quarter = inverse_fisher.shape[0] // 2, inverse_fisher.shape[0] // 4
    a0, a1, b0, b1 = step(((0, 0, half), (0, half, half), (1, 0, half), (1, half, quarter)))
    q0, q1, q2, last = gather(own, False, (a0,))
    total0, b2, c0 = step(((1, half + quarter, quarter), (2, 0, half)), q0, (a0, a1))
    total, c1, d0 = step(((2, half, half), (3, 0, quarter)), q1, (b0, b1, b2), total0)
    total, d1, d2 = step(((3, quarter, quarter), (3, half, half)), q2, (c0, c1), total)
    (total,) = step((), last(total0, total), (d0, d1, d2), total)
    panel = (total + swap_core(total)).astype(jnp.bfloat16)

    p0, p1, p2, last = gather(panel, True)
    swapped = swap_y(p0)
    p1, other_grads = lax.optimization_barrier((p1, other_grads))
    p3 = last(p1, p1)
    other = score_dot([p1, p3], (0, 2), None, other_grads)
    p2, _ = lax.optimization_barrier((p2, other))
    other = score_dot([p2], (1,), None, other_grads, other)
    p2, swapped, _ = lax.optimization_barrier((p2, swapped, other))
    mine = score_dot([p0, p1, p2, p3], ORDER, dims, stored_grads)
    theirs = score_dot([swapped], ORDER[:1], dims, stored_grads)

    keep, give = sort_out(mine, swap_y(other), theirs)
    return keep + swap_core(give)


def solution(mesh):
    coords = [getattr(device, "coords", None) for device in mesh.devices.flat]
    nx = 2 if None in coords else len({c[0] for c in coords})
    nz = mesh.shape["ex"] // nx
    ny = mesh.shape["grp"]
    if (nz, nx, ny) == (4, 2, 2):
        body = functools.partial(per_device_quad, nz, nx, ny)
    else:
        body = per_device_any
    return jax.shard_map(
        body,
        mesh=mesh,
        in_specs=(P(None, "ex"), P("ex", "dim"), P(("grp", "ex"), "dim")),
        out_specs=P("dim", ("grp", "ex")),
        check_vma=False,
    )
```
